32 devices in a mesh: seq: 8 (over z, core), mp: 4 (over y, x).
Axes of the slice: x: 2, y: 2, z: 4, core: 2. Of those that a mesh axis runs over, the one named last changes fastest.
Arguments:
- inputs: bfloat16 [4, 4096, 1536], P(None, 'seq', 'mp'), may hold values from -6 to 6
- cotangent: bfloat16 [4, 4096, 1536], P(None, 'seq', 'mp'), may hold values from -6 to 6
- mixer_gain: bfloat16 [1536], replicated, may hold values from 0.099609375 to 1.8984375
- in_weight: bfloat16 [1536, 3, 1536], P(None, None, 'mp'), may hold values from -0.15625 to 0.15625
- in_entry: bfloat16 [1536, 128], P('mp'), may hold values from -0.15625 to 0.15625
- in_exit: bfloat16 [128, 3, 1536], P(None, None, 'mp'), may hold values from -0.75 to 0.75
- conv_weight: bfloat16 [3, 1536], P(None, 'mp'), may hold values from -3.5 to 3.5
- out_weight: bfloat16 [1536, 1536], P('mp'), may hold values from -0.15625 to 0.15625
- out_entry: bfloat16 [1536, 128], P('mp'), may hold values from -0.15625 to 0.15625
- out_exit: bfloat16 [128, 1536], P(None, 'mp'), may hold values from -0.75 to 0.75
- ffn_gain: bfloat16 [1536], replicated, may hold values from 0.099609375 to 1.8984375
- gate_weight: bfloat16 [1536, 6912], P(None, 'mp'), may hold values from -0.15625 to 0.15625
- gate_entry: bfloat16 [1536, 128], P('mp'), may hold values from -0.15625 to 0.15625
- gate_exit: bfloat16 [128, 6912], P(None, 'mp'), may hold values from -0.75 to 0.75
- up_weight: bfloat16 [1536, 6912], P(None, 'mp'), may hold values from -0.15625 to 0.15625
- up_entry: bfloat16 [1536, 128], P('mp'), may hold values from -0.15625 to 0.15625
- up_exit: bfloat16 [128, 6912], P(None, 'mp'), may hold values from -0.75 to 0.75
- down_weight: bfloat16 [6912, 1536], P('mp'), may hold values from -0.078125 to 0.078125
- down_entry: bfloat16 [6912, 128], P('mp'), may hold values from -0.078125 to 0.078125
- down_exit: bfloat16 [128, 1536], P(None, 'mp'), may hold values from -0.75 to 0.75
- doc_starts: int32 [4, 8], replicated, may hold values from 0 to 4095, as said below
- adapter_ids: int32 [4, 8], replicated, may hold values from 0 to 7
Outputs:
- output: bfloat16 [4, 4096, 1536], P(None, 'seq', 'mp')
- input_grad: float32 [4, 4096, 1536], P(None, 'seq', 'mp')
- in_entry_grad: float32 [1536, 128], P('mp')
- in_exit_grad: float32 [128, 3, 1536], P(None, None, 'mp')
- out_entry_grad: float32 [1536, 128], P('mp')
- out_exit_grad: float32 [128, 1536], P(None, 'mp')
- gate_entry_grad: float32 [1536, 128], P('mp')
- gate_exit_grad: float32 [128, 6912], P(None, 'mp')
- up_entry_gradient: float32 [1536, 128], P('mp')
- up_exit_grad: float32 [128, 6912], P(None, 'mp')
- down_entry_grad: float32 [6912, 128], P('mp')
- down_exit_grad: float32 [128, 1536], P(None, 'mp')
The draws below stay inside these ranges and needn't reach their ends.
Inputs may be any that keep to these rules, and one draw needn't show every extreme that they name: `doc_starts`: each row begins with 0 and rises strictly; a document runs from its start to the next start or to its sequence's end.
All inputs are finite; a program needn't handle non-finite values.
Results may differ from the reference program's by a relative error of at most 0.017.
Values may be sent and summed in bfloat16 or wider, within the bound.
No kernel may reach another device: no remote copies, remote signals or barrier semaphores. Data moves between devices by JAX's collectives and lax.ppermute only.
A program may use at most 256 MiB of HBM per device.

```python
import jax
import jax.numpy as jnp
from jax import lax

D = 1536
FF = 6912
RANK = 16
ADAPT = 8
NDOC = 8
SEQS = 4
L_DEV = 512
LEN = 4096


def draw_doc_starts(key, part):
    key = jax.random.fold_in(key, 7)
    half_count = NDOC // 2
    anchor = jnp.zeros((1,), jnp.int32)
    head = jnp.sort(jax.random.permutation(jax.random.fold_in(key, 1), L_DEV - 1)[:half_count - 1] + 1)
    tail = jnp.sort(jax.random.permutation(jax.random.fold_in(key, 2), L_DEV - 1)[:half_count] + LEN - L_DEV + 1)
    spanning = jnp.concatenate([anchor, head.astype(jnp.int32), tail.astype(jnp.int32)])
    rows = []
    for row_number in range(SEQS):
        picks = jax.random.permutation(jax.random.fold_in(key, 10 + row_number), LEN - 1)[:NDOC - 1] + 1
        rows.append(jnp.concatenate([anchor, jnp.sort(picks).astype(jnp.int32)]))
    free_rows = jnp.stack(rows)
    chosen = jax.random.randint(jax.random.fold_in(key, 3), (), 0, SEQS)
    return jnp.where(jnp.arange(SEQS)[:, None] == chosen, spanning[None, :], free_rows).astype(jnp.int32)


def touch_ends(values, rng, low, top_value):
    place = [jax.random.randint(jax.random.fold_in(rng, axis), (), 0, length) for axis, length in enumerate(values.shape)]
    longest = values.shape.index(max(values.shape))
    neighbour = place[:longest] + [(place[longest] + 1) % values.shape[longest]] + place[longest + 1:]
    return values.at[tuple(place)].set(low).at[tuple(neighbour)].set(top_value)


def shard_levels(stream_key, dims, cuts, low, largest):
    level, own = 1.0, jax.random.fold_in(stream_key, 6)
    for dim, blocks in cuts:
        heights = jnp.exp(jax.random.uniform(jax.random.fold_in(own, dim), (blocks,), jnp.float32, low / len(cuts), largest / len(cuts)))
        level = level * jnp.repeat(heights, dims[dim] // blocks).reshape([-1 if axis == dim else 1 for axis in range(len(dims))])
    return level


def bell_draw(rng, extent, spread, bound, cuts=(), kind=jnp.bfloat16):
    values = jax.random.normal(rng, extent, jnp.float32) * spread
    if len(cuts) > 0:
        values = shard_levels(rng, extent, cuts, -0.22, 0.18) * values
    return jnp.clip(values, min=-bound, max=bound).astype(kind)


def setup_inputs(seed: int = 0) -> dict:
    key_list = jax.random.split(jax.random.key(seed), 23)
    inputs = bell_draw(key_list[0], (SEQS, LEN, D), 1.0, 6.0, ((1, 8), (2, 4)))
    cotangent = bell_draw(key_list[1], (SEQS, LEN, D), 1.0, 6.0, ((1, 8), (2, 4)))
    mixer_gain = jnp.clip(1.0 + 0.18 * jax.random.normal(key_list[2], (D,), jnp.float32), 0.099609375, 1.8984375).astype(jnp.bfloat16)
    in_weight = bell_draw(key_list[3], (D, 3, D), D ** -0.5, 0.15625, ((2, 4),))
    in_entry = bell_draw(key_list[4], (D, ADAPT * RANK), D ** -0.5, 0.15625, ((0, 4),))
    in_exit = bell_draw(key_list[5], (ADAPT * RANK, 3, D), (4 * RANK) ** -0.5, 0.75, ((2, 4),))
    conv_weight = bell_draw(key_list[6], (3, D), 3 ** -0.5, 3.5, ((1, 4),))
    out_weight = bell_draw(key_list[7], (D, D), D ** -0.5, 0.15625, ((0, 4),))
    out_entry = bell_draw(key_list[8], (D, ADAPT * RANK), D ** -0.5, 0.15625, ((0, 4),))
    out_exit = bell_draw(key_list[9], (ADAPT * RANK, D), (4 * RANK) ** -0.5, 0.75, ((1, 4),))
    ffn_gain = jnp.clip(1.0 + 0.18 * jax.random.normal(key_list[10], (D,), jnp.float32), 0.099609375, 1.8984375).astype(jnp.bfloat16)
    gate_weight = bell_draw(key_list[11], (D, FF), D ** -0.5, 0.15625, ((1, 4),))
    gate_entry = bell_draw(key_list[12], (D, ADAPT * RANK), D ** -0.5, 0.15625, ((0, 4),))
    gate_exit = bell_draw(key_list[13], (ADAPT * RANK, FF), (4 * RANK) ** -0.5, 0.75, ((1, 4),))
    up_weight = bell_draw(key_list[14], (D, FF), D ** -0.5, 0.15625, ((1, 4),))
    up_entry = bell_draw(key_list[15], (D, ADAPT * RANK), D ** -0.5, 0.15625, ((0, 4),))
    up_exit = bell_draw(key_list[16], (ADAPT * RANK, FF), (4 * RANK) ** -0.5, 0.75, ((1, 4),))
    down_weight = bell_draw(key_list[17], (FF, D), FF ** -0.5, 0.078125, ((0, 4),))
    down_entry = bell_draw(key_list[18], (FF, ADAPT * RANK), FF ** -0.5, 0.078125, ((0, 4),))
    down_exit = bell_draw(key_list[19], (ADAPT * RANK, D), (4 * RANK) ** -0.5, 0.75, ((1, 4),))
    doc_starts = draw_doc_starts(jax.random.fold_in(key_list[22], 71), 0)
    adapter_ids = touch_ends(jax.random.randint(key_list[21], (SEQS, NDOC), 0, ADAPT), jax.random.fold_in(key_list[21], 1), 0, ADAPT - 1).astype(jnp.int32)
    return dict(inputs=inputs, cotangent=cotangent, mixer_gain=mixer_gain, in_weight=in_weight, in_entry=in_entry, in_exit=in_exit, conv_weight=conv_weight, out_weight=out_weight, out_entry=out_entry, out_exit=out_exit, ffn_gain=ffn_gain, gate_weight=gate_weight, gate_entry=gate_entry, gate_exit=gate_exit, up_weight=up_weight, up_entry=up_entry, up_exit=up_exit, down_weight=down_weight, down_entry=down_entry, down_exit=down_exit, doc_starts=doc_starts, adapter_ids=adapter_ids)


EPS = 1e-05

@jax.custom_vjp
def low(v):
    return lax.optimization_barrier(v.astype(jnp.bfloat16)).astype(jnp.float32)

@jax.custom_vjp
def low_back(v):
    return v

def low_keep(v):
    return (low(v), None)

def low_pass(kept, grad):
    return (grad,)

def back_keep(v):
    return (v, None)

def back_low(kept, grad):
    return (low(grad),)
low.defvjp(low_keep, low_pass)
low_back.defvjp(back_keep, back_low)

def matmul(left, right):
    return jnp.dot(left, right, precision=lax.Precision.HIGHEST, preferred_element_type=jnp.float32)

def rms_norm(values, gain):
    return values * lax.rsqrt(lax.optimization_barrier(jnp.mean(values * values, axis=-1, keepdims=True)) + EPS) * gain

def reduced_rank(inputs, entry, exit_lookup, select):
    inner = matmul(inputs, entry)
    return matmul(select * low(low_back(inner)), exit_lookup)

def doc_tables(starts, ids):
    position = jnp.arange(LEN, dtype=jnp.int32)
    begins = jnp.any(starts[:, None] == position[None, :], axis=0).astype(jnp.float32)
    earlier = jnp.concatenate([jnp.ones((1,), jnp.float32), begins[:-1]])
    prev_one = 1.0 - begins
    prev_two = prev_one * (1.0 - earlier)
    segment = lax.optimization_barrier(jnp.sum((starts[:, None] <= position[None, :]).astype(jnp.int32), axis=0)) - 1
    document_onehot = (segment[:, None] == jnp.arange(NDOC, dtype=jnp.int32)[None, :]).astype(jnp.float32)
    adapter_onehot = (ids[:, None] == jnp.arange(ADAPT, dtype=jnp.int32)[None, :]).astype(jnp.float32)
    token_onehot = matmul(document_onehot, adapter_onehot)
    return (prev_one, prev_two, jnp.repeat(token_onehot, RANK, axis=1))

def block(tokens, adapt, frozen, prev_one, prev_two, select):
    mixer_gain, in_weight, conv_weight, out_weight, ffn_gain, gate_weight, up_weight, down_weight = frozen
    in_entry, in_exit, out_entry, out_exit, gate_entry, gate_exit, up_entry, up_exit, down_entry, down_exit = adapt
    width = tokens.shape[1]
    normed = low(rms_norm(tokens, mixer_gain))
    project = low_back(matmul(normed, in_weight.reshape(width, 3 * width)) + reduced_rank(normed, in_entry, in_exit.reshape(-1, 3 * width), select))
    input_gate = project[:, :width]
    output_gate = project[:, width:2 * width]
    values = project[:, 2 * width:]
    mixed = input_gate * values
    shift_one = jnp.concatenate([jnp.zeros((1, width), jnp.float32), mixed[:-1]], 0) * prev_one[:, None]
    shift_two = jnp.concatenate([jnp.zeros((2, width), jnp.float32), mixed[:-2]], 0) * prev_two[:, None]
    filtered = conv_weight[2] * mixed + conv_weight[1] * shift_one + conv_weight[0] * shift_two
    gated = low(output_gate * filtered)
    branch = low_back(matmul(gated, out_weight) + reduced_rank(gated, out_entry, out_exit, select))
    hidden = tokens + branch
    normed_two = low(rms_norm(hidden, ffn_gain))
    gate = low_back(matmul(normed_two, gate_weight) + reduced_rank(normed_two, gate_entry, gate_exit, select))
    up = low_back(matmul(normed_two, up_weight) + reduced_rank(normed_two, up_entry, up_exit, select))
    activated = low(jax.nn.silu(gate) * up)
    down = low_back(matmul(activated, down_weight) + reduced_rank(activated, down_entry, down_exit, select))
    return hidden + down

def reference(inputs, cotangent, mixer_gain, in_weight, in_entry, in_exit, conv_weight, out_weight, out_entry, out_exit, ffn_gain, gate_weight, gate_entry, gate_exit, up_weight, up_entry, up_exit, down_weight, down_entry, down_exit, doc_starts, adapter_ids):
    frozen = tuple((w.astype(jnp.float32) for w in (mixer_gain, in_weight, conv_weight, out_weight, ffn_gain, gate_weight, up_weight, down_weight)))
    adapters = tuple((a.astype(jnp.float32) for a in (in_entry, in_exit, out_entry, out_exit, gate_entry, gate_exit, up_entry, up_exit, down_entry, down_exit)))

    def one_sequence(totals, item):
        tokens, grad_out, starts, ids = item
        prev_one, prev_two, select = doc_tables(starts, ids)

        def forward(values, adapt):
            return block(values, adapt, frozen, prev_one, prev_two, select)
        result, pullback = jax.vjp(forward, tokens.astype(jnp.float32), adapters)
        grad_tokens, grad_adapt = pullback(grad_out.astype(jnp.float32))
        totals = tuple((total + grad for total, grad in zip(totals, grad_adapt)))
        return (totals, (result.astype(jnp.bfloat16), grad_tokens))
    zeros = tuple((jnp.zeros_like(a) for a in adapters))
    totals, outcome = lax.scan(one_sequence, zeros, (inputs, cotangent, doc_starts, adapter_ids))
    return (outcome[0], outcome[1], totals[0], totals[1], totals[2], totals[3], totals[4], totals[5], totals[6], totals[7], totals[8], totals[9])
```

```python
import jax
import jax.numpy as jnp
from jax import lax
from jax.sharding import PartitionSpec as P

RANK = 16
ADAPT = 8
NDOC = 8


EPS = 1e-05


def from_behind(x, axis, by):
    count = lax.axis_size(axis)
    pairs = [(i, i + by) for i in range(count) if 0 <= i + by < count]
    return lax.ppermute(x, axis, pairs)


def contract(left, right, left_dim, right_extent):
    return lax.dot_general(
        left, right, (((left_dim,), (right_extent,)), ((), ())), preferred_element_type=jnp.float32
    )


def row_total(values):
    return lax.psum(jnp.sum(values, axis=-1), "mp")


def mid_total(parts):
    return lax.psum(parts, "mp")


def share_total(partial_value):
    return lax.psum_scatter(partial_value, "mp", scatter_dimension=1, tiled=True)


def column_products(share, weights):
    piece = lax.all_gather(share, "mp", axis=1, tiled=True)
    return tuple((jnp.dot(piece, weight, preferred_element_type=jnp.float32) for weight in weights))


def row_products(share, weight):
    return contract(lax.all_gather(share, "mp", axis=1, tiled=True), weight, 1, 1)


def doc_tables(starts, ids, length, offset):
    position = offset + jnp.arange(length, dtype=jnp.int32)
    begins = jnp.any(starts[:, :, None] == position[None, None, :], axis=1).astype(jnp.float32)
    earlier = jnp.any(starts[:, :, None] == position[None, None, :] - 1, axis=1).astype(jnp.float32)
    prev_one = 1.0 - begins
    prev_two = prev_one * (1.0 - earlier)
    segment = jnp.sum((starts[:, :, None] <= position[None, None, :]).astype(jnp.int32), axis=1) - 1
    document_onehot = (
        segment[:, :, None] == jnp.arange(NDOC, dtype=jnp.int32)[None, None, :]
    ).astype(jnp.float32)
    adapter_onehot = (ids[:, :, None] == jnp.arange(ADAPT, dtype=jnp.int32)[None, None, :]).astype(
        jnp.float32
    )
    token_onehot = jnp.einsum("cxn,cnt->cxt", document_onehot, adapter_onehot)
    select = jnp.repeat(token_onehot, RANK, axis=2).reshape(-1, ADAPT * RANK)
    return (prev_one, prev_two, select.astype(jnp.bfloat16))


def general_local(
    inputs,
    cotangent,
    mixer_gain,
    in_weight,
    in_entry,
    in_exit,
    conv_weight,
    out_weight,
    out_entry,
    out_exit,
    ffn_gain,
    gate_weight,
    gate_entry,
    gate_exit,
    up_weight,
    up_entry,
    up_exit,
    down_weight,
    down_entry,
    down_exit,
    doc_starts,
    adapter_ids,
):
    seq_count, length, width_share = inputs.shape
    tokens = seq_count * length
    width = width_share * lax.axis_size("mp")
    column = lax.axis_index("mp") * width_share
    prev_one, prev_two, select = doc_tables(
        doc_starts, adapter_ids, length, lax.axis_index("seq") * length
    )
    mixer_share = lax.dynamic_slice_in_dim(mixer_gain, column, width_share, 0).astype(jnp.float32)
    ffn_full = ffn_gain.astype(jnp.float32)
    ffn_share = lax.dynamic_slice_in_dim(ffn_full, column, width_share, 0)
    residual = inputs.reshape(tokens, width_share).astype(jnp.float32)
    scale_one = lax.rsqrt(row_total(residual * residual) / width + EPS)
    normed = (residual * scale_one[:, None] * mixer_share).astype(jnp.bfloat16)
    in_flat = in_weight.reshape(width, 3 * width_share)
    exit_flat = in_exit.reshape(in_exit.shape[0], 3 * width_share)
    inner_in = mid_total((jnp.dot(normed, in_entry, preferred_element_type=jnp.float32),))[0]
    low_in = inner_in.astype(jnp.bfloat16) * select
    project = column_products(normed, (in_flat,))[0] + jnp.dot(
        low_in, exit_flat, preferred_element_type=jnp.float32
    )
    parts = project.reshape(seq_count, length, 3, width_share)
    input_gate = parts[:, :, 0]
    output_gate = parts[:, :, 1]
    values = parts[:, :, 2]
    mixed = input_gate * values
    edge = from_behind(mixed[:, length - 2 :], "seq", 1)
    extended = jnp.concatenate([edge, mixed], 1)
    taps = conv_weight.astype(jnp.float32)
    filtered = (
        taps[2] * mixed
        + taps[1] * prev_one[..., None] * extended[:, 1 : length + 1]
        + taps[0] * prev_two[..., None] * extended[:, :length]
    )
    gated = (output_gate * filtered).astype(jnp.bfloat16).reshape(tokens, width_share)
    inner_out = mid_total((jnp.dot(gated, out_entry, preferred_element_type=jnp.float32),))[0]
    low_out = inner_out.astype(jnp.bfloat16) * select
    branch_tail = jnp.dot(low_out, out_exit, preferred_element_type=jnp.float32)
    partial_value = jnp.dot(gated, out_weight, preferred_element_type=jnp.float32)
    own = lax.dynamic_slice_in_dim(partial_value, column, width_share, 1) + residual + branch_tail
    rows_total = lax.psum(lax.dynamic_update_slice_in_dim(partial_value, own, column, 1), "mp")
    hidden = lax.dynamic_slice_in_dim(rows_total, column, width_share, 1)
    scale_two = lax.rsqrt(jnp.sum(rows_total * rows_total, axis=1) / width + EPS)
    normed_full = (rows_total * scale_two[:, None] * ffn_full).astype(jnp.bfloat16)
    normed_two = lax.dynamic_slice_in_dim(normed_full, column, width_share, 1)
    gate = jnp.dot(normed_full, gate_weight, preferred_element_type=jnp.float32)
    up = jnp.dot(normed_full, up_weight, preferred_element_type=jnp.float32)
    inner_gate, inner_up = mid_total(
        (
            jnp.dot(normed_two, gate_entry, preferred_element_type=jnp.float32),
            jnp.dot(normed_two, up_entry, preferred_element_type=jnp.float32),
        )
    )
    low_gate = inner_gate.astype(jnp.bfloat16) * select
    low_up = inner_up.astype(jnp.bfloat16) * select
    gate = gate + jnp.dot(low_gate, gate_exit, preferred_element_type=jnp.float32)
    up = up + jnp.dot(low_up, up_exit, preferred_element_type=jnp.float32)
    sigma = jax.nn.sigmoid(gate)
    swish = gate * sigma
    activated = (swish * up).astype(jnp.bfloat16)
    inner_down = mid_total((jnp.dot(activated, down_entry, preferred_element_type=jnp.float32),))[0]
    low_down = inner_down.astype(jnp.bfloat16) * select
    outcome = (
        hidden
        + share_total(jnp.dot(activated, down_weight, preferred_element_type=jnp.float32))
        + jnp.dot(low_down, down_exit, preferred_element_type=jnp.float32)
    )
    output = outcome.astype(jnp.bfloat16).reshape(seq_count, length, width_share)
    grad_hidden = cotangent.reshape(tokens, width_share).astype(jnp.float32)
    grad_down = grad_hidden.astype(jnp.bfloat16)
    grad_act = row_products(grad_down, down_weight)
    back_down = mid_total((contract(grad_down, down_exit, 1, 1),))[0]
    low_back_down = back_down.astype(jnp.bfloat16) * select
    grad_act = grad_act + contract(low_back_down, down_entry, 1, 1)
    down_entry_grad = contract(activated, low_back_down, 0, 0)
    down_exit_grad = contract(low_down, grad_down, 0, 0)
    up_projection_gradient = (grad_act * swish).astype(jnp.bfloat16)
    grad_gate = (grad_act * up * sigma * (1.0 + gate * (1.0 - sigma))).astype(jnp.bfloat16)
    back_gate, back_up = mid_total(
        (contract(grad_gate, gate_exit, 1, 1), contract(up_projection_gradient, up_exit, 1, 1))
    )
    low_back_gate = back_gate.astype(jnp.bfloat16) * select
    low_back_up = back_up.astype(jnp.bfloat16) * select
    grad_normed_two = share_total(
        contract(grad_gate, gate_weight, 1, 1) + contract(up_projection_gradient, up_weight, 1, 1)
    )
    grad_normed_two = (
        grad_normed_two
        + contract(low_back_gate, gate_entry, 1, 1)
        + contract(low_back_up, up_entry, 1, 1)
    )
    gate_entry_grad = contract(normed_two, low_back_gate, 0, 0)
    gate_exit_grad = contract(low_gate, grad_gate, 0, 0)
    up_entry_gradient = contract(normed_two, low_back_up, 0, 0)
    up_exit_grad = contract(low_up, up_projection_gradient, 0, 0)
    weighted_two = grad_normed_two * ffn_share
    cube_two = scale_two * scale_two * scale_two
    grad_hidden = (
        grad_hidden
        + scale_two[:, None] * weighted_two
        - hidden * (cube_two * row_total(weighted_two * hidden) / width)[:, None]
    )
    grad_branch = grad_hidden.astype(jnp.bfloat16)
    grad_gated = row_products(grad_branch, out_weight)
    back_out = mid_total((contract(grad_branch, out_exit, 1, 1),))[0]
    low_back_out = back_out.astype(jnp.bfloat16) * select
    grad_gated = grad_gated + contract(low_back_out, out_entry, 1, 1)
    out_entry_grad = contract(gated, low_back_out, 0, 0)
    out_exit_grad = contract(low_out, grad_branch, 0, 0)
    grad_gated = grad_gated.reshape(seq_count, length, width_share)
    grad_output_gate = grad_gated * filtered
    grad_filtered = grad_gated * output_gate
    near = taps[1] * prev_one[..., None] * grad_filtered
    far = taps[0] * prev_two[..., None] * grad_filtered
    sent = jnp.concatenate([far[:, :1], near[:, :1] + far[:, 1:2]], 1)
    came = from_behind(sent, "seq", -1)
    zero_one = jnp.zeros((seq_count, 1, width_share), jnp.float32)
    zero_two = jnp.zeros((seq_count, 2, width_share), jnp.float32)
    spacer = jnp.zeros((seq_count, length - 2, width_share), jnp.float32)
    grad_mixed = (
        taps[2] * grad_filtered
        + jnp.concatenate([near[:, 1:], zero_one], 1)
        + jnp.concatenate([far[:, 2:], zero_two], 1)
        + jnp.concatenate([spacer, came], 1)
    )
    grad_project = (
        jnp.stack([grad_mixed * values, grad_output_gate, grad_mixed * input_gate], 2)
        .reshape(tokens, 3 * width_share)
        .astype(jnp.bfloat16)
    )
    back_in = mid_total((contract(grad_project, exit_flat, 1, 1),))[0]
    low_back_in = back_in.astype(jnp.bfloat16) * select
    grad_normed = share_total(contract(grad_project, in_flat, 1, 1)) + contract(
        low_back_in, in_entry, 1, 1
    )
    in_entry_grad = contract(normed, low_back_in, 0, 0)
    in_exit_grad = contract(low_in, grad_project, 0, 0).reshape(in_exit.shape)
    weighted_one = grad_normed * mixer_share
    cube_one = scale_one * scale_one * scale_one
    grad_inputs = (
        grad_hidden
        + scale_one[:, None] * weighted_one
        - residual * (cube_one * row_total(weighted_one * residual) / width)[:, None]
    )
    summed = (
        lax.psum(in_entry_grad.astype(jnp.bfloat16), "seq").astype(jnp.float32),
        lax.psum(in_exit_grad.astype(jnp.bfloat16), "seq").astype(jnp.float32),
        lax.psum(out_entry_grad.astype(jnp.bfloat16), "seq").astype(jnp.float32),
        lax.psum(out_exit_grad.astype(jnp.bfloat16), "seq").astype(jnp.float32),
        lax.psum(gate_entry_grad.astype(jnp.bfloat16), "seq").astype(jnp.float32),
        lax.psum(gate_exit_grad.astype(jnp.bfloat16), "seq").astype(jnp.float32),
        lax.psum(up_entry_gradient.astype(jnp.bfloat16), "seq").astype(jnp.float32),
        lax.psum(up_exit_grad.astype(jnp.bfloat16), "seq").astype(jnp.float32),
        lax.psum(down_entry_grad.astype(jnp.bfloat16), "seq").astype(jnp.float32),
        lax.psum(down_exit_grad.astype(jnp.bfloat16), "seq").astype(jnp.float32),
    )
    return (
        output,
        grad_inputs.reshape(seq_count, length, width_share),
        summed[0],
        summed[1],
        summed[2],
        summed[3],
        summed[4],
        summed[5],
        summed[6],
        summed[7],
        summed[8],
        summed[9],
    )


def swap(value, axis, bit):
    return lax.ppermute(value, axis, [(i, i ^ bit) for i in range(lax.axis_size(axis))])


def place(relative, me):
    stacked = jnp.stack(relative)
    return [lax.dynamic_index_in_dim(stacked, a ^ me, 0, keepdims=False) for a in range(len(relative))]


def halves(block, me):
    rows = block.shape[0] // 2
    return lax.dynamic_slice_in_dim(block, me * rows, rows, 0)


def gather_blocks(block, core):
    mine = halves(block, core)
    from_x = swap(mine, "mp", 1)
    from_y = swap(mine, "mp", 2)
    cut = (mine.shape[0] // 32) * 16
    from_g = jnp.concatenate([swap(from_x[:cut], "mp", 2), swap(from_y[cut:], "mp", 1)], 0)
    full = [block]
    for piece in (from_x, from_y, from_g):
        full.append(jnp.concatenate(place([piece, swap(piece, "seq", 1)], core), 0))
    return full


def fetch_block(block, quarter):
    rows = block.shape[0] // 4
    mine = swap(lax.dynamic_slice_in_dim(block, quarter * rows, rows, 0), "mp", 2)
    over = swap(mine, "seq", 2)
    both = swap(jnp.stack([mine, over]), "seq", 1)
    return jnp.concatenate(place([mine, both[0], over, both[1]], quarter), 0)


def dot(left, right):
    return jnp.dot(left, right, preferred_element_type=jnp.float32)


def low(value):
    return value.astype(jnp.bfloat16)


def fast_local(
    inputs,
    cotangent,
    mixer_gain,
    in_weight,
    in_entry,
    in_exit,
    conv_weight,
    out_weight,
    out_entry,
    out_exit,
    ffn_gain,
    gate_weight,
    gate_entry,
    gate_exit,
    up_weight,
    up_entry,
    up_exit,
    down_weight,
    down_entry,
    down_exit,
    doc_starts,
    adapter_ids,
):
    seqs, length, share = inputs.shape
    width = 4 * share
    rank = in_entry.shape[1]
    hidden_share = gate_weight.shape[1]
    m = lax.axis_index("mp")
    s = lax.axis_index("seq")
    x, y, core, quarter = m % 2, m // 2, s % 2, s % 4
    halo = 16

    edge = from_behind(inputs[:, length - 2 :], "seq", 1)
    extended = jnp.concatenate([jnp.zeros((seqs, halo - 2, share), inputs.dtype), edge, inputs], 1)

    def block_for(r):
        return lax.dynamic_index_in_dim(extended, m ^ r, 0, keepdims=False)

    tokens_ext = jnp.concatenate(
        place([block_for(0)] + [swap(block_for(r), "mp", r) for r in (1, 2, 3)], m), 1
    )
    in_flat = in_weight.reshape(width, 3 * share)
    in_blocks = gather_blocks(in_flat, core)
    exits = jnp.concatenate(
        [
            jnp.concatenate([in_exit.reshape(rank, 3 * share), out_exit, down_exit], 1),
            jnp.pad(conv_weight, ((0, 29), (0, 4 * share))),
        ],
        0,
    )
    exit_blocks = gather_blocks(exits, core)
    entries = jnp.concatenate([in_entry, out_entry, gate_entry, up_entry], 1)
    entry_blocks = gather_blocks(entries, core)
    out_blocks = gather_blocks(out_weight, core)
    entry_full = jnp.concatenate(place(entry_blocks, m), 0)
    in_entry_full, out_entry_full, gate_entry_full, up_entry_full = (
        entry_full[:, i * rank : (i + 1) * rank] for i in range(4)
    )
    out_exit_full = jnp.concatenate(place([b[:rank, 3 * share : 4 * share] for b in exit_blocks], m), 1)
    down_exit_full = jnp.concatenate(place([b[:rank, 4 * share :] for b in exit_blocks], m), 1)
    in_exit_blocks = [b[:rank, : 3 * share] for b in exit_blocks]
    tap_blocks = [b[rank : rank + 3, :share].astype(jnp.float32) for b in exit_blocks]

    row_of = lax.dynamic_slice_in_dim(cotangent, 2 * y, 2, 0)
    row_other = lax.dynamic_slice_in_dim(cotangent, 2 - 2 * y, 2, 0)
    both = jnp.stack([row_of, swap(row_other, "mp", 2)])
    ct_mine = lax.dynamic_index_in_dim(both, x, 1, keepdims=False)
    ct_next = lax.dynamic_index_in_dim(both, 1 - x, 1, keepdims=False)
    got_mine = swap(ct_next, "mp", 1)

    gate_ext = jnp.concatenate([gate_weight, gate_exit], 0)
    up_ext = jnp.concatenate([up_weight, up_exit], 0)
    down_ext = jnp.concatenate([down_weight, down_entry], 1)
    gate_far = fetch_block(gate_ext, quarter)
    up_far = fetch_block(up_ext, quarter)
    down_far = fetch_block(down_ext, quarter)

    starts = jnp.stack([doc_starts[m], doc_starts[m ^ 1]])
    ids = jnp.stack([adapter_ids[m], adapter_ids[m ^ 1]])
    prev_one, prev_two, select = doc_tables(starts, ids, length, s * length)
    prev_one, prev_two = prev_one[0][:, None], prev_two[0][:, None]
    select = select.reshape(2, length, rank)
    select_ext = jnp.concatenate([jnp.zeros((halo, rank), jnp.bfloat16), select[0]], 0)
    edge_starts, edge_ids = starts[:1], ids[:1]
    edge_select = doc_tables(edge_starts, edge_ids, halo, s * length - halo)[2]
    select_ext = jnp.concatenate([edge_select, select[0]], 0)

    gain_one = mixer_gain.astype(jnp.float32)
    gain_two = ffn_gain.astype(jnp.float32)
    residual_ext = tokens_ext.astype(jnp.float32)
    scale_ext = lax.rsqrt(jnp.sum(residual_ext * residual_ext, 1, keepdims=True) / width + EPS)
    normed_ext = low(residual_ext * scale_ext * gain_one)
    residual, scale_one, normed = residual_ext[halo:], scale_ext[halo:], normed_ext[halo:]
    low_in_ext = low(dot(normed_ext, in_entry_full)) * select_ext
    low_in = low_in_ext[halo:]
    kept = []
    branch = 0.0
    inner_out = 0.0
    for r in range(4):
        project = dot(normed_ext, in_blocks[r]) + dot(low_in_ext, in_exit_blocks[r])
        input_gate, output_gate, values = (project[:, i * share : (i + 1) * share] for i in range(3))
        mixed = input_gate * values
        taps = tap_blocks[r]
        filtered = (
            taps[2] * mixed[halo:]
            + taps[1] * prev_one * mixed[halo - 1 : halo - 1 + length]
            + taps[0] * prev_two * mixed[halo - 2 : halo - 2 + length]
        )
        output_gate = output_gate[halo:]
        gated = low(output_gate * filtered)
        kept.append((low(input_gate[halo:]), low(output_gate), low(values[halo:]), low(filtered), gated))
        branch = branch + dot(gated, out_blocks[r])
        inner_out = inner_out + dot(gated, entry_blocks[r][:, rank : 2 * rank])
    low_out = low(inner_out) * select[0]
    hidden = residual + branch + dot(low_out, out_exit_full)
    scale_two = lax.rsqrt(jnp.sum(hidden * hidden, 1, keepdims=True) / width + EPS)
    normed_two = low(hidden * scale_two * gain_two)
    normed_next = swap(normed_two, "mp", 1)
    got_next = swap(ct_mine, "mp", 1)

    def rows(first, second):
        return jnp.concatenate(place([first[0], second[0], first[1], second[1]], m), 1)

    grad_down = [rows(ct_mine, got_mine), rows(ct_next, got_next)]

    seen = [normed_two, normed_next]
    low_gates, low_ups, low_backs = [], [], []
    for t in range(2):
        low_gates.append(low(dot(seen[t], gate_entry_full)) * select[t])
        low_ups.append(low(dot(seen[t], up_entry_full)) * select[t])
        low_backs.append(low(contract(grad_down[t], down_exit_full, 1, 1)) * select[t])

    def feed(t, gate_w, up_w, down_w):
        gate = dot(jnp.concatenate([seen[t], low_gates[t]], 1), gate_w)
        up = dot(jnp.concatenate([seen[t], low_ups[t]], 1), up_w)
        sigma = jax.nn.sigmoid(gate)
        swish = gate * sigma
        activated = low(swish * up)
        grad_act = contract(jnp.concatenate([grad_down[t], low_backs[t]], 1), down_w, 1, 1)
        grad_up = low(grad_act * swish)
        grad_gate = low(grad_act * up * sigma * (1.0 + gate * (1.0 - sigma)))
        down = dot(activated, down_w)
        back = (contract(grad_gate, gate_w, 1, 1), contract(grad_up, up_w, 1, 1))
        adapters = (
            contract(low_gates[t], grad_gate, 0, 0),
            contract(low_ups[t], grad_up, 0, 0),
            contract(low_backs[t], activated, 0, 0),
        )
        return down, back, adapters

    def join(one, two):
        return jax.tree.map(jnp.add, one, two)

    near = (gate_ext, up_ext, down_ext)
    far = (gate_far, up_far, down_far)
    near_mine = feed(0, *near)
    near_next = feed(1, *near)
    far_next = feed(1, *far)
    down_next, back_next = join(near_next[:2], far_next[:2])
    packed = jnp.concatenate(
        [
            low(back_next[0][:, :width] + back_next[1][:, :width]),
            low(back_next[0][:, width:]),
            low(back_next[1][:, width:]),
        ],
        1,
    )
    got_back = swap(packed, "mp", 1).astype(jnp.float32)
    far_mine = feed(0, *far)
    down_mine, back_mine = join(near_mine[:2], far_mine[:2])
    near_grads = join(near_mine[2], near_next[2])
    far_grads = join(far_mine[2], far_next[2])
    far_sent = swap(low(jnp.stack(far_grads)), "mp", 2)
    ffn_grads = jnp.stack(near_grads) + far_sent.astype(jnp.float32)

    inner = low(jnp.stack([down_mine[:, width:], down_next[:, width:]]))
    inner_got = swap(inner, "mp", 1)
    inner_down = inner.astype(jnp.float32) + inner_got[::-1].astype(jnp.float32)
    low_down = low(inner_down) * select

    def quarter_stack(value):
        return jnp.stack([value[:, i * share : (i + 1) * share] for i in range(4)])

    def take(stack, r):
        return lax.dynamic_index_in_dim(stack, m ^ r, 0, keepdims=False)

    stack_mine = quarter_stack(hidden + down_mine[:, :width])
    stack_next = quarter_stack(down_next[:, :width])
    sent = low(jnp.stack([take(stack_mine, 1), take(stack_mine, 3), take(stack_next, 1), take(stack_next, 3)]))
    came = swap(sent, "mp", 1).astype(jnp.float32)
    exit_stack = quarter_stack(down_exit_full)
    results = []
    for i, r in ((0, 0), (1, 2)):
        for t, stack in ((0, stack_mine), (1, stack_next)):
            results.append(low(take(stack, r) + came[2 * (1 - t) + i] + dot(low_down[t], take(exit_stack, r))))
    kept_rows = jnp.stack(place(results[:2], x))
    sent_rows = jnp.stack(place(results[2:], x))
    output = jnp.concatenate(place([kept_rows, swap(sent_rows, "mp", 2)], y), 0)

    inner_back = got_back[:, width:] + jnp.concatenate([back_mine[0][:, width:], back_mine[1][:, width:]], 1)
    low_back_gate = low(inner_back[:, :rank]) * select[0]
    low_back_up = low(inner_back[:, rank:]) * select[0]
    grad_normed_two = (
        got_back[:, :width]
        + back_mine[0][:, :width]
        + back_mine[1][:, :width]
        + contract(low_back_gate, gate_entry_full, 1, 1)
        + contract(low_back_up, up_entry_full, 1, 1)
    )
    weighted_two = grad_normed_two * gain_two
    grad_hidden = (
        grad_down[0].astype(jnp.float32)
        + scale_two * weighted_two
        - hidden * (scale_two**3 * jnp.sum(weighted_two * hidden, 1, keepdims=True) / width)
    )
    grad_branch = low(grad_hidden)
    low_back_out = low(contract(grad_branch, out_exit_full, 1, 1)) * select[0]

    near_rows, far_rows, filtered_grads, gate_grads = [], [], [], []
    for r in range(4):
        grad_gated = contract(grad_branch, out_blocks[r], 1, 1) + contract(
            low_back_out, entry_blocks[r][:, rank : 2 * rank], 1, 1
        )
        input_gate, output_gate, values, filtered, gated = kept[r]
        grad_filtered = grad_gated * output_gate.astype(jnp.float32)
        gate_grads.append(low(grad_gated * filtered.astype(jnp.float32)))
        filtered_grads.append(grad_filtered)
    head_rows = jnp.concatenate([g[:2] for g in filtered_grads], 1)
    head_taps = jnp.concatenate(tap_blocks, 1)
    head_near = head_taps[1] * prev_one[:2] * head_rows
    head_far = head_taps[0] * prev_two[:2] * head_rows
    came_back = from_behind(jnp.concatenate([head_far[:1], head_near[:1] + head_far[1:2]], 0), "seq", -1)
    grad_normed = 0.0
    inner_back_in = 0.0
    in_exit_grads, out_entry_grads = [], []
    for r in range(4):
        input_gate, output_gate, values, filtered, gated = kept[r]
        taps = tap_blocks[r]
        grad_filtered = filtered_grads[r]
        near_part = taps[1] * prev_one * grad_filtered
        far_part = taps[0] * prev_two * grad_filtered
        tail = came_back[:, r * share : (r + 1) * share]
        near_part = jnp.concatenate([near_part[1:], tail[1:2]], 0)
        far_part = jnp.concatenate([far_part[2:], tail[0:1], jnp.zeros((1, share), jnp.float32)], 0)
        grad_mixed = taps[2] * grad_filtered + near_part + far_part
        grad_project = jnp.concatenate(
            [
                low(grad_mixed * values.astype(jnp.float32)),
                gate_grads[r],
                low(grad_mixed * input_gate.astype(jnp.float32)),
            ],
            1,
        )
        grad_normed = grad_normed + contract(grad_project, in_blocks[r], 1, 1)
        inner_back_in = inner_back_in + contract(grad_project, in_exit_blocks[r], 1, 1)
        in_exit_grads.append(contract(low_in, grad_project, 0, 0))
        out_entry_grads.append(contract(low_back_out, gated, 0, 0))
    low_back_in = low(inner_back_in) * select[0]
    grad_normed = grad_normed + contract(low_back_in, in_entry_full, 1, 1)
    weighted_one = grad_normed * gain_one
    grad_inputs = (
        grad_hidden
        + scale_one * weighted_one
        - residual * (scale_one**3 * jnp.sum(weighted_one * residual, 1, keepdims=True) / width)
    )
    grad_stack = quarter_stack(low(grad_inputs))
    grad_blocks = [take(grad_stack, 0)] + [swap(take(grad_stack, r), "mp", r) for r in (1, 2, 3)]
    grad_out = jnp.stack(place(grad_blocks, m)).astype(jnp.float32)

    wide = jnp.stack(
        [
            quarter_stack(contract(low_back_gate, normed_two, 0, 0)),
            quarter_stack(contract(low_back_up, normed_two, 0, 0)),
            quarter_stack(contract(low_out, grad_branch, 0, 0)),
            quarter_stack(contract(low_down[0], grad_down[0], 0, 0)),
            quarter_stack(contract(low_back_in, normed, 0, 0)),
        ],
        1,
    )
    own_wide = 0.0
    for r in range(4):
        exit_grad = in_exit_grads[r].reshape(rank, 3, share).swapaxes(0, 1)
        part = jnp.concatenate([take(wide, r), out_entry_grads[r][None], exit_grad], 0)
        own_wide = own_wide + (part if r == 0 else swap(low(part), "mp", r).astype(jnp.float32))
    wide_total = lax.psum(low(own_wide), "seq").astype(jnp.float32)
    ffn_total = lax.psum(low(ffn_grads), "seq").astype(jnp.float32)
    return (
        output,
        grad_out,
        wide_total[4].T,
        wide_total[6:9].swapaxes(0, 1),
        wide_total[5].T,
        wide_total[2],
        wide_total[0].T,
        ffn_total[0],
        wide_total[1].T,
        ffn_total[1],
        ffn_total[2].T,
        wide_total[3],
    )


def solution(mesh):
    fast = mesh.shape["mp"] == 4 and mesh.shape["seq"] % 4 == 0
    return jax.shard_map(
        fast_local if fast else general_local,
        mesh=mesh,
        in_specs=(
            P(None, "seq", "mp"),
            P(None, "seq", "mp"),
            P(),
            P(None, None, "mp"),
            P("mp", None),
            P(None, None, "mp"),
            P(None, "mp"),
            P("mp", None),
            P("mp", None),
            P(None, "mp"),
            P(),
            P(None, "mp"),
            P("mp", None),
            P(None, "mp"),
            P(None, "mp"),
            P("mp", None),
            P(None, "mp"),
            P("mp", None),
            P("mp", None),
            P(None, "mp"),
            P(),
            P(),
        ),
        out_specs=(
            P(None, "seq", "mp"),
            P(None, "seq", "mp"),
            P("mp", None),
            P(None, None, "mp"),
            P("mp", None),
            P(None, "mp"),
            P("mp", None),
            P(None, "mp"),
            P("mp", None),
            P(None, "mp"),
            P("mp", None),
            P(None, "mp"),
        ),
        check_vma=False,
    )
```

```python
import functools

import jax
import jax.numpy as jnp
from jax import lax
from jax.experimental import pallas as pl
from jax.experimental.pallas import tpu as pltpu
from jax.sharding import PartitionSpec as P

RANK = 16
ADAPT = 8
NDOC = 8


EPS = 1e-05


def from_behind(x, axis, by):
    count = lax.axis_size(axis)
    pairs = [(i, i + by) for i in range(count) if 0 <= i + by < count]
    return lax.ppermute(x, axis, pairs)


def contract(left, right, left_dim, right_extent):
    return lax.dot_general(
        left, right, (((left_dim,), (right_extent,)), ((), ())), preferred_element_type=jnp.float32
    )


def row_total(values):
    return lax.psum(jnp.sum(values, axis=-1), "mp")


def mid_total(parts):
    return lax.psum(parts, "mp")


def share_total(partial_value):
    return lax.psum_scatter(partial_value, "mp", scatter_dimension=1, tiled=True)


def column_products(share, weights):
    piece = lax.all_gather(share, "mp", axis=1, tiled=True)
    return tuple((jnp.dot(piece, weight, preferred_element_type=jnp.float32) for weight in weights))


def row_products(share, weight):
    return contract(lax.all_gather(share, "mp", axis=1, tiled=True), weight, 1, 1)


def doc_tables(starts, ids, length, offset):
    position = offset + jnp.arange(length, dtype=jnp.int32)
    begins = jnp.any(starts[:, :, None] == position[None, None, :], axis=1).astype(jnp.float32)
    earlier = jnp.any(starts[:, :, None] == position[None, None, :] - 1, axis=1).astype(jnp.float32)
    prev_one = 1.0 - begins
    prev_two = prev_one * (1.0 - earlier)
    segment = jnp.sum((starts[:, :, None] <= position[None, None, :]).astype(jnp.int32), axis=1) - 1
    document_onehot = (
        segment[:, :, None] == jnp.arange(NDOC, dtype=jnp.int32)[None, None, :]
    ).astype(jnp.float32)
    adapter_onehot = (ids[:, :, None] == jnp.arange(ADAPT, dtype=jnp.int32)[None, None, :]).astype(
        jnp.float32
    )
    token_onehot = jnp.einsum("cxn,cnt->cxt", document_onehot, adapter_onehot)
    select = jnp.repeat(token_onehot, RANK, axis=2).reshape(-1, ADAPT * RANK)
    return (prev_one, prev_two, select.astype(jnp.bfloat16))


def general_local(
    inputs,
    cotangent,
    mixer_gain,
    in_weight,
    in_entry,
    in_exit,
    conv_weight,
    out_weight,
    out_entry,
    out_exit,
    ffn_gain,
    gate_weight,
    gate_entry,
    gate_exit,
    up_weight,
    up_entry,
    up_exit,
    down_weight,
    down_entry,
    down_exit,
    doc_starts,
    adapter_ids,
):
    seq_count, length, width_share = inputs.shape
    tokens = seq_count * length
    width = width_share * lax.axis_size("mp")
    column = lax.axis_index("mp") * width_share
    prev_one, prev_two, select = doc_tables(
        doc_starts, adapter_ids, length, lax.axis_index("seq") * length
    )
    mixer_share = lax.dynamic_slice_in_dim(mixer_gain, column, width_share, 0).astype(jnp.float32)
    ffn_full = ffn_gain.astype(jnp.float32)
    ffn_share = lax.dynamic_slice_in_dim(ffn_full, column, width_share, 0)
    residual = inputs.reshape(tokens, width_share).astype(jnp.float32)
    scale_one = lax.rsqrt(row_total(residual * residual) / width + EPS)
    normed = (residual * scale_one[:, None] * mixer_share).astype(jnp.bfloat16)
    in_flat = in_weight.reshape(width, 3 * width_share)
    exit_flat = in_exit.reshape(in_exit.shape[0], 3 * width_share)
    inner_in = mid_total((jnp.dot(normed, in_entry, preferred_element_type=jnp.float32),))[0]
    low_in = inner_in.astype(jnp.bfloat16) * select
    project = column_products(normed, (in_flat,))[0] + jnp.dot(
        low_in, exit_flat, preferred_element_type=jnp.float32
    )
    parts = project.reshape(seq_count, length, 3, width_share)
    input_gate = parts[:, :, 0]
    output_gate = parts[:, :, 1]
    values = parts[:, :, 2]
    mixed = input_gate * values
    edge = from_behind(mixed[:, length - 2 :], "seq", 1)
    extended = jnp.concatenate([edge, mixed], 1)
    taps = conv_weight.astype(jnp.float32)
    filtered = (
        taps[2] * mixed
        + taps[1] * prev_one[..., None] * extended[:, 1 : length + 1]
        + taps[0] * prev_two[..., None] * extended[:, :length]
    )
    gated = (output_gate * filtered).astype(jnp.bfloat16).reshape(tokens, width_share)
    inner_out = mid_total((jnp.dot(gated, out_entry, preferred_element_type=jnp.float32),))[0]
    low_out = inner_out.astype(jnp.bfloat16) * select
    branch_tail = jnp.dot(low_out, out_exit, preferred_element_type=jnp.float32)
    partial_value = jnp.dot(gated, out_weight, preferred_element_type=jnp.float32)
    own = lax.dynamic_slice_in_dim(partial_value, column, width_share, 1) + residual + branch_tail
    rows_total = lax.psum(lax.dynamic_update_slice_in_dim(partial_value, own, column, 1), "mp")
    hidden = lax.dynamic_slice_in_dim(rows_total, column, width_share, 1)
    scale_two = lax.rsqrt(jnp.sum(rows_total * rows_total, axis=1) / width + EPS)
    normed_full = (rows_total * scale_two[:, None] * ffn_full).astype(jnp.bfloat16)
    normed_two = lax.dynamic_slice_in_dim(normed_full, column, width_share, 1)
    gate = jnp.dot(normed_full, gate_weight, preferred_element_type=jnp.float32)
    up = jnp.dot(normed_full, up_weight, preferred_element_type=jnp.float32)
    inner_gate, inner_up = mid_total(
        (
            jnp.dot(normed_two, gate_entry, preferred_element_type=jnp.float32),
            jnp.dot(normed_two, up_entry, preferred_element_type=jnp.float32),
        )
    )
    low_gate = inner_gate.astype(jnp.bfloat16) * select
    low_up = inner_up.astype(jnp.bfloat16) * select
    gate = gate + jnp.dot(low_gate, gate_exit, preferred_element_type=jnp.float32)
    up = up + jnp.dot(low_up, up_exit, preferred_element_type=jnp.float32)
    sigma = jax.nn.sigmoid(gate)
    swish = gate * sigma
    activated = (swish * up).astype(jnp.bfloat16)
    inner_down = mid_total((jnp.dot(activated, down_entry, preferred_element_type=jnp.float32),))[0]
    low_down = inner_down.astype(jnp.bfloat16) * select
    outcome = (
        hidden
        + share_total(jnp.dot(activated, down_weight, preferred_element_type=jnp.float32))
        + jnp.dot(low_down, down_exit, preferred_element_type=jnp.float32)
    )
    output = outcome.astype(jnp.bfloat16).reshape(seq_count, length, width_share)
    grad_hidden = cotangent.reshape(tokens, width_share).astype(jnp.float32)
    grad_down = grad_hidden.astype(jnp.bfloat16)
    grad_act = row_products(grad_down, down_weight)
    back_down = mid_total((contract(grad_down, down_exit, 1, 1),))[0]
    low_back_down = back_down.astype(jnp.bfloat16) * select
    grad_act = grad_act + contract(low_back_down, down_entry, 1, 1)
    down_entry_grad = contract(activated, low_back_down, 0, 0)
    down_exit_grad = contract(low_down, grad_down, 0, 0)
    up_projection_gradient = (grad_act * swish).astype(jnp.bfloat16)
    grad_gate = (grad_act * up * sigma * (1.0 + gate * (1.0 - sigma))).astype(jnp.bfloat16)
    back_gate, back_up = mid_total(
        (contract(grad_gate, gate_exit, 1, 1), contract(up_projection_gradient, up_exit, 1, 1))
    )
    low_back_gate = back_gate.astype(jnp.bfloat16) * select
    low_back_up = back_up.astype(jnp.bfloat16) * select
    grad_normed_two = share_total(
        contract(grad_gate, gate_weight, 1, 1) + contract(up_projection_gradient, up_weight, 1, 1)
    )
    grad_normed_two = (
        grad_normed_two
        + contract(low_back_gate, gate_entry, 1, 1)
        + contract(low_back_up, up_entry, 1, 1)
    )
    gate_entry_grad = contract(normed_two, low_back_gate, 0, 0)
    gate_exit_grad = contract(low_gate, grad_gate, 0, 0)
    up_entry_gradient = contract(normed_two, low_back_up, 0, 0)
    up_exit_grad = contract(low_up, up_projection_gradient, 0, 0)
    weighted_two = grad_normed_two * ffn_share
    cube_two = scale_two * scale_two * scale_two
    grad_hidden = (
        grad_hidden
        + scale_two[:, None] * weighted_two
        - hidden * (cube_two * row_total(weighted_two * hidden) / width)[:, None]
    )
    grad_branch = grad_hidden.astype(jnp.bfloat16)
    grad_gated = row_products(grad_branch, out_weight)
    back_out = mid_total((contract(grad_branch, out_exit, 1, 1),))[0]
    low_back_out = back_out.astype(jnp.bfloat16) * select
    grad_gated = grad_gated + contract(low_back_out, out_entry, 1, 1)
    out_entry_grad = contract(gated, low_back_out, 0, 0)
    out_exit_grad = contract(low_out, grad_branch, 0, 0)
    grad_gated = grad_gated.reshape(seq_count, length, width_share)
    grad_output_gate = grad_gated * filtered
    grad_filtered = grad_gated * output_gate
    near = taps[1] * prev_one[..., None] * grad_filtered
    far = taps[0] * prev_two[..., None] * grad_filtered
    sent = jnp.concatenate([far[:, :1], near[:, :1] + far[:, 1:2]], 1)
    came = from_behind(sent, "seq", -1)
    zero_one = jnp.zeros((seq_count, 1, width_share), jnp.float32)
    zero_two = jnp.zeros((seq_count, 2, width_share), jnp.float32)
    spacer = jnp.zeros((seq_count, length - 2, width_share), jnp.float32)
    grad_mixed = (
        taps[2] * grad_filtered
        + jnp.concatenate([near[:, 1:], zero_one], 1)
        + jnp.concatenate([far[:, 2:], zero_two], 1)
        + jnp.concatenate([spacer, came], 1)
    )
    grad_project = (
        jnp.stack([grad_mixed * values, grad_output_gate, grad_mixed * input_gate], 2)
        .reshape(tokens, 3 * width_share)
        .astype(jnp.bfloat16)
    )
    back_in = mid_total((contract(grad_project, exit_flat, 1, 1),))[0]
    low_back_in = back_in.astype(jnp.bfloat16) * select
    grad_normed = share_total(contract(grad_project, in_flat, 1, 1)) + contract(
        low_back_in, in_entry, 1, 1
    )
    in_entry_grad = contract(normed, low_back_in, 0, 0)
    in_exit_grad = contract(low_in, grad_project, 0, 0).reshape(in_exit.shape)
    weighted_one = grad_normed * mixer_share
    cube_one = scale_one * scale_one * scale_one
    grad_inputs = (
        grad_hidden
        + scale_one[:, None] * weighted_one
        - residual * (cube_one * row_total(weighted_one * residual) / width)[:, None]
    )
    summed = (
        lax.psum(in_entry_grad.astype(jnp.bfloat16), "seq").astype(jnp.float32),
        lax.psum(in_exit_grad.astype(jnp.bfloat16), "seq").astype(jnp.float32),
        lax.psum(out_entry_grad.astype(jnp.bfloat16), "seq").astype(jnp.float32),
        lax.psum(out_exit_grad.astype(jnp.bfloat16), "seq").astype(jnp.float32),
        lax.psum(gate_entry_grad.astype(jnp.bfloat16), "seq").astype(jnp.float32),
        lax.psum(gate_exit_grad.astype(jnp.bfloat16), "seq").astype(jnp.float32),
        lax.psum(up_entry_gradient.astype(jnp.bfloat16), "seq").astype(jnp.float32),
        lax.psum(up_exit_grad.astype(jnp.bfloat16), "seq").astype(jnp.float32),
        lax.psum(down_entry_grad.astype(jnp.bfloat16), "seq").astype(jnp.float32),
        lax.psum(down_exit_grad.astype(jnp.bfloat16), "seq").astype(jnp.float32),
    )
    return (
        output,
        grad_inputs.reshape(seq_count, length, width_share),
        summed[0],
        summed[1],
        summed[2],
        summed[3],
        summed[4],
        summed[5],
        summed[6],
        summed[7],
        summed[8],
        summed[9],
    )


VMEM_BYTES = 58 * 1024 * 1024


def product(left, right):
    return jnp.dot(left, right, preferred_element_type=jnp.float32)


def product_t(left, right):
    return lax.dot_general(left, right, (((1,), (1,)), ((), ())), preferred_element_type=jnp.float32)


def wide_value(value):
    return value.astype(jnp.float32)


def low(value):
    return value.astype(jnp.bfloat16)


def each_tile(total, size, body):
    whole = total // size
    if whole:

        @pl.loop(0, whole)
        def _(i):
            body(pl.multiple_of(i * size, size), size)

    if total % size:
        body(whole * size, total % size)


def spans(total, size):
    return [(at, min(size, total - at)) for at in range(0, total, size)]


class Mover:
    def __init__(self, sems):
        self.sems, self.count, self.pending = sems, 0, []

    def start(self, source, target):
        copy = pltpu.make_async_copy(source, target, self.sems.at[self.count])
        self.count += 1
        copy.start()
        self.pending.append(copy)
        return copy

    def wait(self, copies=None):
        for copy in list(self.pending if copies is None else copies):
            copy.wait()
            self.pending = [c for c in self.pending if c is not copy]


def piece_index(place_ref, kind, flip):
    return jnp.bitwise_xor(place_ref[1 if kind == "half" else 2], flip)


def start_in(mover, loads, own, located, target, width, share):
    for i in range(3):
        loads.append(mover.start(own.at[i], target.at[:, pl.ds(i * width, share)]))
    for ref, r, index, pack, _ in located:
        rows = pl.ds(pl.multiple_of(index * pack.in_rows, 16), pack.in_rows)
        for i in range(3):
            source = ref.at[pl.ds(i * pack.in_rows, pack.in_rows)]
            loads.append(mover.start(source, target.at[rows, pl.ds(i * width + r * share, share)]))


def start_out(mover, loads, own, located, target, width, share):
    loads.append(mover.start(own, target.at[pl.ds(0, share)]))
    for ref, r, index, pack, _ in located:
        rows = pl.ds(pl.multiple_of(r * share + index * pack.out_rows, 16), pack.out_rows)
        for i in range(4):
            source = ref.at[pl.ds(pack.out_at + i * pack.out_rows, pack.out_rows)]
            loads.append(mover.start(source, target.at[rows, pl.ds(i * share, share)]))


def kernel_call(body, name, args, kinds, outs, scratch, sems, flops, size, out_space=pl.ANY):
    spaces = {"s": pltpu.SMEM, "v": pltpu.VMEM, "a": pl.ANY}
    return pl.pallas_call(
        body,
        out_shape=tuple(outs),
        in_specs=[pl.BlockSpec(memory_space=spaces[k]) for k in kinds],
        out_specs=tuple(pl.BlockSpec(memory_space=out_space) for _ in outs),
        scratch_shapes=list(scratch) + [pltpu.SemaphoreType.DMA((sems,))],
        compiler_params=pltpu.CompilerParams(vmem_limit_bytes=VMEM_BYTES),
        cost_estimate=pl.CostEstimate(flops=flops, bytes_accessed=size, transcendentals=0),
        name=name,
    )(*args)


def shaped(shape, kind=jnp.bfloat16):
    return jax.ShapeDtypeStruct(shape, kind)


TAP_ROWS = 16


class Pack:
    def __init__(self, width, share, rank, count):
        self.in_rows, self.out_rows, self.side_rows = width // count, share // count, rank // count
        self.out_at = 3 * self.in_rows
        self.entry_at = self.out_at + 4 * self.out_rows
        self.side_at = self.entry_at + 2 * self.out_rows
        self.tap_at = self.side_at + 5 * self.side_rows
        self.rows = self.tap_at + TAP_ROWS


PACK_COUNT = {"half": 2, "quarter": 4}


def pack_first_kernel(place_ref, inputs, in_weight, out_weight, *refs):
    entries, (in_exit, out_exit, down_exit, taps), outs, sems = refs[:4], refs[4:8], refs[8:-1], refs[-1]
    share, width = out_weight.shape
    rank = entries[0].shape[1]
    mover = Mover(sems)
    for index, out in ((2, outs[0]), (1, outs[1])):
        pack = Pack(width, share, rank, 4 if index == 2 else 2)

        def part(rows):
            return pl.ds(pl.multiple_of(place_ref[index] * rows, 16), rows)

        for i in range(3):
            mover.start(in_weight.at[i, part(pack.in_rows)], out.at[pl.ds(i * pack.in_rows, pack.in_rows)])
        rows = part(pack.out_rows)
        for i in range(4):
            target = out.at[pl.ds(pack.out_at + i * pack.out_rows, pack.out_rows)]
            mover.start(out_weight.at[rows, pl.ds(i * share, share)], target)
            target = out.at[pl.ds(pack.entry_at + i // 3 * pack.out_rows, pack.out_rows), pl.ds(i % 3 * rank, rank)]
            mover.start(entries[i].at[rows], target)
        rows = part(pack.side_rows)
        for i, side in enumerate((in_exit.at[0], in_exit.at[1], in_exit.at[2], out_exit, down_exit)):
            mover.start(side.at[rows], out.at[pl.ds(pack.side_at + i * pack.side_rows, pack.side_rows)])
        mover.start(taps, out.at[pl.ds(pack.tap_at, TAP_ROWS)])
    for r in range(4):
        mover.start(inputs.at[jnp.bitwise_xor(place_ref[0], r)], outs[2 + r])
    mover.wait()


def pack_first(place_ids, inputs, in_weight, out_weight, entries, sides, taps):
    length, share = inputs.shape[1:]
    width, rank = in_weight.shape[1], entries[0].shape[1]
    args = [place_ids, inputs, in_weight, out_weight, *entries, *sides, taps]
    outs = [shaped((Pack(width, share, rank, count).rows, share)) for count in (4, 2)] + [shaped((length, share))] * 4
    return kernel_call(pack_first_kernel, "pack_first", args, "s" + "a" * 11, outs, [], 64, 0, 16_000_000, pltpu.VMEM)


def pack_second_kernel(cuts, place_ref, cotangent, *refs):
    near, (own, other, far_row), packs, sems = refs[:6], refs[6:9], refs[9:-1], refs[-1]
    mover = Mover(sems)
    mine = place_ref[0]
    mover.start(cotangent.at[jnp.bitwise_xor(mine, 2)], far_row.at[0])
    mover.start(cotangent.at[jnp.bitwise_xor(mine, 3)], far_row.at[1])
    mover.start(cotangent.at[mine], own)
    mover.start(cotangent.at[jnp.bitwise_xor(mine, 1)], other)
    quarter_rows = near[0].shape[0] // 4
    width = near[0].shape[1]
    for (at, n), pack in zip(cuts, packs):
        rows = pl.ds(pl.multiple_of(place_ref[2] * quarter_rows + at, 16), n)
        for i in range(3):
            mover.start(near[2 * i].at[rows], pack.at[i, :, pl.ds(0, width)])
            mover.start(near[2 * i + 1].at[rows], pack.at[i, :, pl.ds(width, near[1].shape[1])])
    mover.wait()


def pack_second(place_ids, cotangent, near, cuts):
    length, share = cotangent.shape[1:]
    outs = [shaped((length, share)), shaped((length, share)), shaped((2, length, share))]
    outs += [shaped((3, n, near[0].shape[1] + near[1].shape[1])) for _, n in cuts]
    return kernel_call(
        functools.partial(pack_second_kernel, cuts), "pack_second", [place_ids, cotangent, *near], "s" + "a" * 7, outs, [], 32, 0, 20_000_000, pltpu.VMEM
    )


def mixer_kernel(plan, *refs):
    refs = list(refs)

    def take(n):
        return [refs.pop(0) for _ in range(n)]

    place_ref, select, prev, gain_one, gain_two = take(5)
    head, in_own, out_own, *own = take(11)
    entries_own, (in_exit, out_exit, down_exit, taps_own) = own[:4], own[4:]
    blocks = take(4)
    pieces = take(len(plan))
    kept_out, gated_out, tokens_out, normed_out, hidden_out, two_out, lows_out, entry_out, column_out, exit_out, taps_out = take(11)
    (x_s, n_s, in_s, out_s, entry_s, col_s, exit_s, tap_s, taps_s, proj_s, mix_s) = take(11)
    kept_s, gated_s, hid_s, two_s, low_in_s, lows_s, sems = refs
    length, width = gated_s.shape
    share, rank, edge = width // 4, low_in_s.shape[1], head.shape[1]
    mover = Mover(sems)

    def absolute(r):
        return pl.multiple_of(jnp.bitwise_xor(place_ref[0], r) * share, 128)

    for r in range(4):
        lanes = pl.ds(absolute(r), share)
        mover.start(blocks[r], x_s.at[pl.ds(edge, length), lanes])
        mover.start(head.at[r], x_s.at[pl.ds(0, edge), lanes])
    token_loads = list(mover.pending)
    row_loads, column_loads, loads, out_loads = [], [], [], []
    for i, source in enumerate(entries_own):
        row_loads.append(mover.start(source, entry_s.at[pl.ds(absolute(0), share), pl.ds(i * rank, rank)]))
    for i, source in enumerate((in_exit.at[0], in_exit.at[1], in_exit.at[2], out_exit, down_exit)):
        column_loads.append(mover.start(source, col_s.at[pl.ds(i * rank, rank), pl.ds(0, share)]))
    column_loads.append(mover.start(taps_own, tap_s.at[:, pl.ds(0, share)]))
    located = [(ref, r, piece_index(place_ref, kind, flip), Pack(width, share, rank, PACK_COUNT[kind]), flip) for ref, (r, kind, flip) in zip(pieces, plan)]
    for ref, r, index, pack, flip in located:
        rows = pl.ds(pl.multiple_of(absolute(r) + index * pack.out_rows, 16), pack.out_rows)
        source = ref.at[pl.ds(pack.entry_at, pack.out_rows)]
        row_loads.append(mover.start(source, entry_s.at[rows, pl.ds(0, 3 * rank)]))
        source = ref.at[pl.ds(pack.entry_at + pack.out_rows, pack.out_rows), pl.ds(0, rank)]
        row_loads.append(mover.start(source, entry_s.at[rows, pl.ds(3 * rank, rank)]))
        lanes = pl.ds(r * share, share)
        for i in range(5):
            rows = pl.ds(pl.multiple_of(i * rank + index * pack.side_rows, 16), pack.side_rows)
            source = ref.at[pl.ds(pack.side_at + i * pack.side_rows, pack.side_rows)]
            column_loads.append(mover.start(source, col_s.at[rows, lanes]))
        if flip == 0:
            column_loads.append(mover.start(ref.at[pl.ds(pack.tap_at, TAP_ROWS)], tap_s.at[:, lanes]))
    start_in(mover, loads, in_own, located, in_s, width, share)
    start_out(mover, out_loads, out_own, located, out_s, width, share)
    mover.wait(token_loads)

    def norm(at, n):
        rows = pl.ds(at, n)
        x = wide_value(x_s[rows, :])
        scale = lax.rsqrt(jnp.sum(x * x, 1, keepdims=True) / width + EPS)
        n_s[rows, :] = low(x * scale * gain_one[...])

    each_tile(edge + length, 48, norm)
    main = pl.ds(edge, length)
    mover.start(x_s.at[main], tokens_out)
    mover.start(n_s.at[main], normed_out)
    mover.wait(row_loads)
    mover.start(entry_s, entry_out)
    low_in_s[...] = low(product(n_s[...], entry_s[:, pl.ds(0, rank)])) * select[...]
    lows_s[0] = low_in_s[main, :]
    mover.wait(column_loads)
    mover.start(col_s, column_out)
    taps_s[...] = wide_value(tap_s[...])[:8]
    mover.start(taps_s, taps_out)
    for r in range(4):
        exit_s[:, pl.ds(absolute(r), share)] = col_s[pl.ds(3 * rank, 2 * rank), pl.ds(r * share, share)]
    mover.start(exit_s, exit_out)
    mover.wait(loads)
    for i in range(3):

        def project(at, n):
            total = product(n_s[...], in_s[:, pl.ds(i * width + at, n)])
            total += product(low_in_s[...], col_s[pl.ds(i * rank, rank), pl.ds(at, n)])
            proj_s[:, pl.ds(i * width + at, n)] = total

        each_tile(width, width // 3, project)
    for r in range(4):
        lanes = pl.ds(r * share, share)
        mix_s[...] = proj_s[:, lanes] * proj_s[:, pl.ds(2 * width + r * share, share)]
        tap = [taps_s[pl.ds(i, 1), lanes] for i in range(3)]
        for at, n in spans(length, 128):
            rows, above = pl.ds(at, n), pl.ds(at + edge, n)
            filtered = (
                tap[2] * mix_s[above, :]
                + tap[1] * (prev[rows, pl.ds(0, 1)] * mix_s[pl.ds(at + edge - 1, n), :])
                + tap[0] * (prev[rows, pl.ds(1, 1)] * mix_s[pl.ds(at + edge - 2, n), :])
            )
            output_gate = proj_s[above, pl.ds(width + r * share, share)]
            gated_s[rows, lanes] = low(output_gate * filtered)
            kept_s[0, rows, lanes] = low(proj_s[above, lanes])
            kept_s[1, rows, lanes] = low(output_gate)
            kept_s[2, rows, lanes] = low(proj_s[above, pl.ds(2 * width + r * share, share)])
            kept_s[3, rows, lanes] = low(filtered)
    mover.start(kept_s, kept_out)
    mover.start(gated_s, gated_out)
    chosen = select[main, :]
    inner = 0.0
    for r in range(4):
        rows = pl.ds(absolute(r), share)
        inner = inner + product(gated_s[:, pl.ds(r * share, share)], entry_s[rows, pl.ds(rank, rank)])
    lows_s[1] = low(inner) * chosen
    mover.wait(out_loads)

    def branch(at, n):
        cols = pl.ds(at, n)
        total = product(gated_s[...], out_s[:, cols]) + product(lows_s[1], exit_s[pl.ds(0, rank), cols])
        hid_s[:, cols] = total + wide_value(x_s[main, cols])

    each_tile(width, width // 3, branch)
    mover.start(hid_s, hidden_out)

    def norm_two(at, n):
        rows = pl.ds(at, n)
        h = hid_s[rows, :]
        scale = lax.rsqrt(jnp.sum(h * h, 1, keepdims=True) / width + EPS)
        two_s[rows, :] = low(h * scale * gain_two[...])

    each_tile(length, 64, norm_two)
    mover.start(two_s, two_out)
    inner = product(two_s[...], entry_s[:, pl.ds(2 * rank, 2 * rank)])
    lows_s[2] = low(inner[:, :rank]) * chosen
    lows_s[3] = low(inner[:, rank:]) * chosen
    mover.start(lows_s, lows_out)
    mover.wait()


def mixer(place_ids, small, own, blocks, pieces):
    length, share = blocks[0].shape
    width, rank, edge = 4 * share, own[3].shape[1], own[0].shape[1]
    bf, f32 = jnp.bfloat16, jnp.float32
    args = [place_ids, *small, *own, *blocks] + [p[0] for p in pieces]
    kinds = "s" + "v" * len(small) + "a" * (len(args) - 1 - len(small))
    v = pltpu.VMEM
    columns, taps = 5 * rank, TAP_ROWS
    return kernel_call(
        functools.partial(mixer_kernel, [p[1:] for p in pieces]),
        "mixer",
        args,
        kinds,
        [
            shaped((4, length, width)),
            shaped((length, width)),
            shaped((length, width)),
            shaped((length, width)),
            shaped((length, width), f32),
            shaped((length, width)),
            shaped((4, length, rank)),
            shaped((width, 4 * rank)),
            shaped((columns, width)),
            shaped((2 * rank, width)),
            shaped((8, width), f32),
        ],
        [
            v((edge + length, width), bf),
            v((edge + length, width), bf),
            v((width, 3 * width), bf),
            v((width, width), bf),
            v((width, 4 * rank), bf),
            v((columns, width), bf),
            v((2 * rank, width), bf),
            v((taps, width), bf),
            v((8, width), f32),
            v((edge + length, 3 * width), f32),
            v((edge + length, share), f32),
            v((4, length, width), bf),
            v((length, width), bf),
            v((length, width), f32),
            v((length, width), bf),
            v((edge + length, rank), bf),
            v((4, length, rank), bf),
        ],
        200,
        2 * length * width * 4 * width,
        50_000_000,
    )


def ready_kernel(with_seen, *refs):
    refs = list(refs)

    def take(n):
        return [refs.pop(0) for _ in range(n)]

    place_ref, select, exits = take(3)
    seen, entry = take(2) if with_seen else (None, None)
    pieces = take(4)
    grad_out, lows_out, grad_s, lows_s, sems = refs
    share, rank = pieces[0].shape[1], select.shape[1]
    mover = Mover(sems)
    for r in range(4):
        at = pl.multiple_of(jnp.bitwise_xor(place_ref[0], r) * share, 128)
        mover.start(pieces[r], grad_s.at[:, pl.ds(at, share)])
    if with_seen:
        inner = product(seen[...], entry[:, pl.ds(2 * rank, 2 * rank)])
        lows_s[1] = low(inner[:, :rank]) * select[...]
        lows_s[2] = low(inner[:, rank:]) * select[...]
    mover.wait()
    mover.start(grad_s, grad_out)
    lows_s[0] = low(product_t(grad_s[...], exits[pl.ds(rank, rank), :])) * select[...]
    mover.start(lows_s, lows_out)
    mover.wait()


def ready(place_ids, select, exits, pieces, seen=None, entry=None):
    length, share = pieces[0].shape
    rank = select.shape[1]
    more = [] if seen is None else [seen, entry]
    count = 3 if more else 1
    bf = jnp.bfloat16
    return kernel_call(
        functools.partial(ready_kernel, bool(more)),
        "ready",
        [place_ids, select, exits, *more, *pieces],
        "svv" + "v" * len(more) + "aaaa",
        [shaped((length, 4 * share)), shaped((count, length, rank))],
        [pltpu.VMEM((length, 4 * share), bf), pltpu.VMEM((count, length, rank), bf)],
        8,
        2 * length * 4 * share * rank * count,
        6_000_000,
    )


FAR_FLIPS = (0, 2, 1, 3)


def feed_kernel(far, add_tokens, add_grads, settle, size, which, *refs):
    refs = list(refs)

    def take(n):
        return [refs.pop(0) for _ in range(n)]

    (quarter_ref,) = take(1) if far else (None,)
    seen, lows, grad, backs = take(4)
    low_gate, low_up, low_back = lows.at[which], lows.at[which + 1], backs.at[0]
    weights = take(4 if far else 6)
    down_prior, back_prior = take(2) if add_tokens else (None, None)
    (grads_prior,) = take(1) if add_grads else (None,)
    down_out, back_out, grads_out = take(3)
    gate_w, up_w, down_w, act_s, gg_s, gu_s, down_s, back_s, grads_s, sems = refs
    width, rank, units = seen.shape[1], low_gate.shape[1], gate_w.shape[0]
    whole, side = pl.ds(0, width), pl.ds(width, rank)
    steps = spans(units, size)
    quarter_rows = units // 4
    mover = Mover(sems)
    loads = []
    if far:
        for n, ref in enumerate(weights):
            rows = pl.ds(n * quarter_rows, quarter_rows)
            for i, dst in enumerate((gate_w, up_w, down_w)):
                loads.append((n * quarter_rows, mover.start(ref.at[i], dst.at[rows])))
    else:
        for at, n in steps:
            rows = pl.ds(at, n)
            for i, dst in enumerate((gate_w, up_w, down_w)):
                loads.append((at, mover.start(weights[2 * i].at[rows], dst.at[rows, whole])))
                loads.append((at, mover.start(weights[2 * i + 1].at[rows], dst.at[rows, side])))

    for at, n in steps:
        while loads and loads[0][0] < at + n:
            mover.wait([loads.pop(0)[1]])
        cols = pl.ds(at, n)
        gate = product_t(seen[...], gate_w[cols, whole]) + product_t(low_gate[...], gate_w[cols, side])
        up = product_t(seen[...], up_w[cols, whole]) + product_t(low_up[...], up_w[cols, side])
        ga = product_t(grad[...], down_w[cols, whole]) + product_t(low_back[...], down_w[cols, side])
        sigma = jax.nn.sigmoid(gate)
        swish = gate * sigma
        act_s[:, cols] = low(swish * up)
        gu_s[:, cols] = low(ga * swish)
        gg_s[:, cols] = low(ga * up * (sigma + swish * (1.0 - sigma)))

    for i, (left, right) in enumerate(((low_gate, gg_s), (low_up, gu_s), (low_back, act_s))):
        turned, lanes = left[...].T, pl.ds(i * rank, rank)

        def grad_tile(at, n):
            cols = pl.ds(at, n)
            total = product(turned, right[:, cols]).T
            if add_grads:
                total += grads_prior[cols, lanes]
            grads_s[cols, lanes] = total

        each_tile(units, 512, grad_tile)
    if settle:
        for n, flip in enumerate(FAR_FLIPS):
            at = jnp.bitwise_xor(quarter_ref[0], flip)
            mover.start(grads_s.at[pl.ds(n * quarter_rows, quarter_rows)], grads_out.at[at])
    else:
        mover.start(grads_s, grads_out)

    def back_tile(at, n):
        cols = pl.ds(at, n)
        total = product(gg_s[...], gate_w[:, cols]) + product(gu_s[...], up_w[:, cols])
        if add_tokens:
            total += wide_value(back_prior[:, cols])
        back_s[:, cols] = low(total)

    each_tile(width, 512, back_tile)
    for i, (left, right) in enumerate(((gg_s, gate_w), (gu_s, up_w))):
        total = product(left[...], right[:, side])
        cols = pl.ds(width + i * rank, rank)
        if add_tokens:
            total += wide_value(back_prior[:, cols])
        back_s[:, cols] = low(total)
    mover.start(back_s, back_out)

    def down_tile(at, n):
        cols = pl.ds(at, n)
        total = product(act_s[...], down_w[:, cols])
        if add_tokens:
            total += wide_value(down_prior[:, cols])
        down_s[:, cols] = low(total)

    each_tile(width + rank, 512, down_tile)
    mover.start(down_s, down_out)
    mover.wait()


def feed(tokens, which, weights, quarter=None, add_tokens=None, add_grads=None, settle=False, size=512):
    far = quarter is not None
    length, width = tokens[0].shape
    rank = tokens[1].shape[2]
    units = 4 * weights[0].shape[1] if far else weights[0].shape[0]
    bf, f32 = jnp.bfloat16, jnp.float32
    args = ([quarter] if far else []) + list(tokens) + list(weights)
    kinds = ("s" if far else "") + "v" * 4 + "a" * len(weights)
    for prior in (add_tokens or (), () if add_grads is None else (add_grads,)):
        args += list(prior)
        kinds += "v" * len(prior)
    shapes = [(length, width + rank), (length, width + 2 * rank), (units, 3 * rank)]
    kept = [bf, bf, f32]
    outs = [shaped(*pair) for pair in zip(shapes, kept)]
    if settle:
        outs[2] = shaped((4, units // 4, 3 * rank), f32)
    return kernel_call(
        functools.partial(feed_kernel, far, add_tokens is not None, add_grads is not None, settle, size, which),
        "feed_far" if far else "feed_near",
        args,
        kinds,
        outs,
        [pltpu.VMEM((units, width + rank), bf)] * 3
        + [pltpu.VMEM((length, units), bf)] * 3
        + [pltpu.VMEM(*pair) for pair in zip(shapes, kept)],
        40,
        12 * length * units * (width + 2 * rank),
        30_000_000,
    )


def branch_kernel(plan, *refs):
    refs = list(refs)

    def take(n):
        return [refs.pop(0) for _ in range(n)]

    place_ref, came, mine, hidden, grad, two, gated, lows, select, gain_two, entry, exits = take(12)
    kept, out_own = take(2)
    pieces = take(len(plan))
    grad_hidden_out, filtered_out, gates_out, edge_out, wide_out = take(5)
    out_s, kept_s, w_s, gb_s, lo_s, gf_s, gate_s, edge_s, wide_s, sems = refs
    length, width = hidden.shape
    share, rank = width // 4, select.shape[1]
    mover = Mover(sems)
    located = [(ref, r, piece_index(place_ref, kind, flip), Pack(width, share, rank, PACK_COUNT[kind]), flip) for ref, (r, kind, flip) in zip(pieces, plan)]
    start_out(mover, [], out_own, located, out_s, width, share)
    mover.start(kept.at[1], kept_s.at[0])
    mover.start(kept.at[3], kept_s.at[1])
    loads = list(mover.pending)
    side = pl.ds(width, 2 * rank)
    inner = wide_value(came[:, side]) + wide_value(mine[:, side])
    lo_s[0] = low(inner[:, :rank]) * select[...]
    lo_s[1] = low(inner[:, rank:]) * select[...]

    def combine(at, n):
        cols = pl.ds(at, n)
        total = wide_value(came[:, cols]) + wide_value(mine[:, cols])
        total += product_t(lo_s[0], entry[cols, pl.ds(2 * rank, rank)])
        total += product_t(lo_s[1], entry[cols, pl.ds(3 * rank, rank)])
        w_s[:, cols] = total * gain_two[:, cols]

    each_tile(width, width // 3, combine)

    def norm(at, n):
        rows = pl.ds(at, n)
        h, w = hidden[rows, :], w_s[rows, :]
        scale = lax.rsqrt(jnp.sum(h * h, 1, keepdims=True) / width + EPS)
        moment = jnp.sum(w * h, 1, keepdims=True) / width
        value = wide_value(grad[rows, :]) + scale * w - h * (scale * scale * scale * moment)
        w_s[rows, :] = value
        gb_s[rows, :] = low(value)

    each_tile(length, 32, norm)
    mover.start(w_s, grad_hidden_out)
    lo_s[2] = low(product_t(gb_s[...], exits[pl.ds(0, rank), :])) * select[...]
    mover.wait(loads)
    for r in range(4):
        cols = pl.ds(r * share, share)
        rows = pl.ds(pl.multiple_of(jnp.bitwise_xor(place_ref[0], r) * share, 128), share)
        gg = product_t(gb_s[...], out_s[cols, :]) + product_t(lo_s[2], entry[rows, pl.ds(rank, rank)])
        gf = gg * wide_value(kept_s[0, :, cols])
        gf_s[:, cols] = low(gf)
        edge_s[:, cols] = gf[:8]
        gate_s[:, cols] = low(gg * wide_value(kept_s[1, :, cols]))
    mover.start(gf_s, filtered_out)
    mover.start(gate_s, gates_out)
    mover.start(edge_s, edge_out)
    for i, (left, right) in enumerate(((lo_s.at[0], two), (lo_s.at[1], two), (lows.at[1], gb_s), (lo_s.at[2], gated))):
        turned = left[...].T

        def wide_tile(at, n):
            cols = pl.ds(at, n)
            wide_s[i, :, cols] = low(product(turned, right[:, cols]))

        each_tile(width, width // 3, wide_tile)
        for r in range(4):
            at = r * share if i == 3 else pl.multiple_of(jnp.bitwise_xor(place_ref[0], r) * share, 128)
            mover.start(wide_s.at[i, :, pl.ds(at, share)], wide_out.at[r, i])
    mover.wait()


def branch_back(place_ids, small, kept, own, pieces):
    length, width = small[2].shape
    share, rank = width // 4, small[6].shape[2]
    bf, f32, v = jnp.bfloat16, jnp.float32, pltpu.VMEM
    return kernel_call(
        functools.partial(branch_kernel, [p[1:] for p in pieces]),
        "branch_back",
        [place_ids, *small, kept, own, *[p[0] for p in pieces]],
        "s" + "v" * len(small) + "a" * (2 + len(pieces)),
        [
            shaped((length, width), f32),
            shaped((length, width)),
            shaped((length, width)),
            shaped((8, width), f32),
            shaped((4, 4, rank, share)),
        ],
        [
            v((width, width), bf),
            v((2, length, width), bf),
            v((length, width), f32),
            v((length, width), bf),
            v((3, length, rank), bf),
            v((length, width), bf),
            v((length, width), bf),
            v((8, width), f32),
            v((4, rank, width), bf),
        ],
        80,
        2 * length * width * width + 8 * length * rank * width,
        40_000_000,
    )


def input_kernel(plan, *refs):
    refs = list(refs)

    def take(n):
        return [refs.pop(0) for _ in range(n)]

    place_ref, filtered, gates, tail, taps, prev, grad_hidden, tokens, normed, lows, select, gain_one, entry, column = take(14)
    kept, in_own = take(2)
    pieces = take(len(plan))
    grad_out, wide_out = take(2)
    in_s, kept_s, near_s, far_s, gp_s, w_s, gi_s, lo_s, wide_s, entry_s, sems = refs
    length, width = filtered.shape
    share, rank = width // 4, select.shape[1]
    mover = Mover(sems)
    first = [mover.start(kept.at[0], kept_s.at[0]), mover.start(kept.at[2], kept_s.at[1])]
    loads = []
    located = [(ref, r, piece_index(place_ref, kind, flip), Pack(width, share, rank, PACK_COUNT[kind]), flip) for ref, (r, kind, flip) in zip(pieces, plan)]
    start_in(mover, loads, in_own, located, in_s, width, share)
    mover.wait(first)
    for r in range(4):
        lanes = pl.ds(r * share, share)
        tap = [taps[pl.ds(i, 1), lanes] for i in range(3)]
        for at, n in spans(length, 128):
            rows = pl.ds(at, n)
            value = wide_value(filtered[rows, lanes])
            near_s[rows, :] = tap[1] * (prev[rows, pl.ds(0, 1)] * value)
            far_s[rows, :] = tap[0] * (prev[rows, pl.ds(1, 1)] * value)
        near_s[pl.ds(length, 8), :] = jnp.zeros((8, share), jnp.float32)
        far_s[pl.ds(length, 8), :] = tail[:, lanes]
        for at, n in spans(length, 128):
            rows = pl.ds(at, n)
            mixed = tap[2] * wide_value(filtered[rows, lanes]) + near_s[pl.ds(at + 1, n), :] + far_s[pl.ds(at + 2, n), :]
            gp_s[rows, pl.ds(r * share, share)] = low(mixed * wide_value(kept_s[1, rows, lanes]))
            gp_s[rows, pl.ds(2 * width + r * share, share)] = low(mixed * wide_value(kept_s[0, rows, lanes]))
    gp_s[:, pl.ds(width, width)] = gates[...]
    inner = 0.0
    for i in range(3):
        inner = inner + product_t(gp_s[:, pl.ds(i * width, width)], column[pl.ds(i * rank, rank), :])
    lo_s[...] = low(inner) * select[...]
    turned = lows[0].T
    turned_back = lo_s[...].T

    def exit_tile(at, n):
        cols = pl.ds(at, n)
        wide_s[:, cols] = low(product(turned, gp_s[:, cols]))

    each_tile(3 * width, width // 3, exit_tile)

    def entry_tile(at, n):
        cols = pl.ds(at, n)
        entry_s[:, cols] = low(product(turned_back, normed[:, cols]))

    each_tile(width, width // 3, entry_tile)
    for r in range(4):
        at = pl.multiple_of(jnp.bitwise_xor(place_ref[0], r) * share, 128)
        mover.start(entry_s.at[:, pl.ds(at, share)], wide_out.at[r, 0])
        for i in range(3):
            mover.start(wide_s.at[:, pl.ds(i * width + r * share, share)], wide_out.at[r, 1 + i])
    mover.wait(loads)

    def back(at, n):
        cols = pl.ds(at, n)
        total = product_t(gp_s[...], in_s[cols, :]) + product_t(lo_s[...], entry[cols, pl.ds(0, rank)])
        w_s[:, cols] = total * gain_one[:, cols]

    each_tile(width, width // 3, back)

    def norm(at, n):
        rows = pl.ds(at, n)
        x, w = wide_value(tokens[rows, :]), w_s[rows, :]
        scale = lax.rsqrt(jnp.sum(x * x, 1, keepdims=True) / width + EPS)
        moment = jnp.sum(w * x, 1, keepdims=True) / width
        gi_s[rows, :] = low(grad_hidden[rows, :] + scale * w - x * (scale * scale * scale * moment))

    each_tile(length, 32, norm)
    for r in range(4):
        at = pl.multiple_of(jnp.bitwise_xor(place_ref[0], r) * share, 128)
        mover.start(gi_s.at[:, pl.ds(at, share)], grad_out.at[r])
    mover.wait()


def input_back(place_ids, small, kept, own, pieces):
    length, width = small[0].shape
    share, rank = width // 4, small[9].shape[1]
    bf, f32, v = jnp.bfloat16, jnp.float32, pltpu.VMEM
    return kernel_call(
        functools.partial(input_kernel, [p[1:] for p in pieces]),
        "input_back",
        [place_ids, *small, kept, own, *[p[0] for p in pieces]],
        "s" + "v" * len(small) + "a" * (2 + len(pieces)),
        [shaped((4, length, share)), shaped((4, 4, rank, share))],
        [
            v((width, 3 * width), bf),
            v((2, length, width), bf),
            v((length + 8, share), f32),
            v((length + 8, share), f32),
            v((length, 3 * width), bf),
            v((length, width), f32),
            v((length, width), bf),
            v((length, rank), bf),
            v((rank, 3 * width), bf),
            v((rank, width), bf),
        ],
        64,
        6 * length * width * width,
        40_000_000,
    )


def swap(value, axis, bit):
    return lax.ppermute(value, axis, [(i, i ^ bit) for i in range(lax.axis_size(axis))])


def after(value, *others):
    return lax.optimization_barrier((value, others))[0]


def place(relative, me):
    stacked = jnp.stack(relative)
    return [lax.dynamic_index_in_dim(stacked, a ^ me, 0, keepdims=False) for a in range(len(relative))]


def part_of(block, dim, index, count):
    rows = block.shape[dim] // count
    return lax.dynamic_slice_in_dim(block, index * rows, rows, dim)


def seq_step(value, bit):
    return low(wide_value(value) + wide_value(swap(value, "seq", bit)))


def seq_total(value, bits=None):
    for bit in bits or [2**k for k in range(1, 16) if 2**k < lax.axis_size("seq")]:
        value = seq_step(value, bit)
    return value


def chip_half(value, dim, core):
    other = swap(low(part_of(value, dim, 1 - core, 2)), "seq", 1)
    return low(wide_value(part_of(value, dim, core, 2)) + wide_value(other))


def own_block(chip):
    total = wide_value(chip[0])
    for r in (3, 1, 2):
        total = total + wide_value(swap(chip[r], "mp", r))
    return low(total)


def both_halves(own, core):
    return wide_value(jnp.concatenate(place([own, swap(own, "seq", 1)], core), 0))


def fast_local(
    inputs,
    cotangent,
    mixer_gain,
    in_weight,
    in_entry,
    in_exit,
    conv_weight,
    out_weight,
    out_entry,
    out_exit,
    ffn_gain,
    gate_weight,
    gate_entry,
    gate_exit,
    up_weight,
    up_entry,
    up_exit,
    down_weight,
    down_entry,
    down_exit,
    doc_starts,
    adapter_ids,
):
    seqs, length, share = inputs.shape
    width = 4 * share
    rank = in_entry.shape[1]
    units = gate_weight.shape[1]
    m = lax.axis_index("mp")
    s = lax.axis_index("seq")
    x, y, core, quarter = m % 2, m // 2, s % 2, s % 4
    place_ids = jnp.stack([m, core, quarter]).astype(jnp.int32)
    halo = 16

    def block_for(stack, r):
        return lax.dynamic_index_in_dim(stack, m ^ r, 0, keepdims=False)

    in_slabs = in_weight.swapaxes(0, 1)
    own_taps = jnp.pad(conv_weight, ((0, TAP_ROWS - 3), (0, 0)))
    entries = (in_entry, out_entry, gate_entry, up_entry)
    sides = (in_exit.swapaxes(0, 1), out_exit, down_exit)
    quarter_pack, half_pack, *own_blocks = pack_first(
        place_ids, inputs, in_slabs, out_weight, entries, sides, own_taps
    )
    from_g = swap(quarter_pack, "mp", 3)
    from_y = swap(quarter_pack, "mp", 2)
    from_x = swap(half_pack, "mp", 1)
    blocks = [own_blocks[0]] + [swap(own_blocks[r], "mp", r) for r in (1, 2, 3)]
    head = from_behind(jnp.stack([b[length - halo :] for b in blocks]), "seq", 1)
    over_g, over_y = swap(from_g, "seq", 2), swap(from_y, "seq", 2)
    pieces = []
    for r, got, over in ((3, from_g, over_g), (2, from_y, over_y)):
        pieces += [(got, r, "quarter", 0), (swap(got, "seq", 1), r, "quarter", 1)]
        pieces += [(over, r, "quarter", 2), (swap(over, "seq", 1), r, "quarter", 3)]
    pieces += [(from_x, 1, "half", 0), (swap(from_x, "seq", 1), 1, "half", 1)]

    near = [gate_weight.T, gate_exit.T, up_weight.T, up_exit.T, down_weight, down_entry]
    first_rows = units // 8 // 16 * 16 + 16
    cuts = ((0, first_rows), (first_rows, units // 4 - first_rows))
    ct_own, ct_other, ct_row, *packed = pack_second(after(place_ids, quarter_pack), cotangent, near, cuts)

    came_row = swap(after(ct_row, from_y), "mp", 2)
    came_own, came_other = came_row[0], came_row[1]
    mine_pieces = [ct_own, swap(ct_other, "mp", 1), came_own, swap(came_other, "mp", 1)]
    other_pieces = [ct_other, swap(ct_own, "mp", 1), came_other, swap(came_own, "mp", 1)]
    far_first = [swap(after(p, from_y), "mp", 2) for p in packed]

    starts = jnp.stack([doc_starts[m], doc_starts[m ^ 1]])[:, None, :]
    ids = jnp.stack([adapter_ids[m], adapter_ids[m ^ 1]])
    steps = (ids - jnp.pad(ids, ((0, 0), (1, 0)))[:, :-1])[:, None, :]
    position = (s * length - halo + jnp.arange(halo + length, dtype=jnp.int32))[None, :, None]
    adapter = jnp.sum(jnp.where(starts <= position, steps, 0), 2)
    lane = jnp.arange(rank, dtype=jnp.int32) // RANK
    select_ext = (adapter[:, :, None] == lane).astype(jnp.bfloat16)
    select = select_ext[:, halo:]
    begins = jnp.any(starts[0] == position[0], 1).astype(jnp.float32)
    prev_one = 1.0 - begins[halo:]
    prev_two = prev_one * (1.0 - begins[halo - 1 : halo - 1 + length])
    prev = jnp.stack([prev_one, prev_two], 1)
    gain_one = wide_value(mixer_gain)[None]
    gain_two = wide_value(ffn_gain)[None]

    kept, gated, tokens, normed, hidden, normed_two, lows, entry_full, column_full, exit_full, taps = mixer(
        place_ids,
        (select_ext[0], prev, gain_one, gain_two),
        (head, in_slabs, out_weight, *entries, *sides, own_taps),
        blocks,
        pieces,
    )
    normed_next = swap(normed_two, "mp", 1)
    grad_mine, back_low_mine = ready(place_ids, select[0], exit_full, mine_pieces)
    grad_other, lows_other = ready(place_ids, select[1], exit_full, other_pieces, normed_next, entry_full)
    mine = (normed_two, lows, grad_mine, back_low_mine), 2
    other = (normed_next, lows_other, grad_other, lows_other), 1
    at_quarter = jnp.full((1,), quarter, jnp.int32)

    def spread(first, then, last):
        over = swap(after(first, then), "seq", 2)
        return [first, over, swap(after(first, last), "seq", 1), swap(after(over, last), "seq", 1)]

    near_mine = feed(*mine, near)
    near_next = feed(*other, near, add_grads=near_mine[2])
    far_zero = spread(far_first[0], near_mine[2], near_next[2])
    next_zero = feed(*other, far_zero, at_quarter, add_tokens=near_next[:2])
    mine_zero = feed(*mine, far_zero, at_quarter, add_tokens=near_mine[:2], add_grads=next_zero[2], settle=True)
    far_one = spread(far_first[1], near_next[2], next_zero[2])
    down_next, back_next, grads_one = feed(*other, far_one, at_quarter, add_tokens=next_zero[:2])
    got_back = swap(back_next, "mp", 1)
    down_mine, back_mine, grads_one = feed(
        *mine, far_one, at_quarter, add_tokens=mine_zero[:2], add_grads=grads_one, settle=True
    )
    far_grads = jnp.concatenate([mine_zero[2], grads_one], 1).reshape(units, 3 * rank)
    unit_chip = chip_half(jnp.stack([near_next[2], far_grads]), 1, core)

    grad_hidden, grad_filtered, grad_gates, top_rows, wide_one = branch_back(
        place_ids,
        (got_back, after(back_mine, unit_chip), hidden, grad_mine, normed_two, gated, lows, select[0], gain_two, entry_full, exit_full),
        kept,
        out_weight,
        pieces,
    )
    unit_came = after(swap(unit_chip[1], "mp", 2), top_rows)
    unit_own = low(wide_value(unit_chip[0]) + wide_value(unit_came))

    down_mine, down_next = after((down_mine, down_next), grad_hidden)
    inner = jnp.stack([down_mine[:, width:], down_next[:, width:]])
    inner_got = swap(inner, "mp", 1)
    low_down = low(wide_value(inner) + wide_value(inner_got[::-1])) * select

    def quarter_stack(value):
        return jnp.stack([value[:, i * share : (i + 1) * share] for i in range(4)])

    stack_mine = quarter_stack(hidden + wide_value(down_mine[:, :width]))
    stack_next = quarter_stack(down_next[:, :width])
    sent = [block_for(stack_mine, 1), block_for(stack_mine, 3), block_for(stack_next, 1), block_for(stack_next, 3)]
    came = swap(after(jnp.stack([low(v) for v in sent]), back_mine), "mp", 1)

    near_row = taps[1] * prev_one[:2, None] * top_rows[:2]
    far_row = taps[0] * prev_two[:2, None] * top_rows[:2]
    edge = jnp.concatenate([far_row[:1], near_row[:1] + far_row[1:], jnp.zeros((6, width), jnp.float32)], 0)
    came_edge = from_behind(edge, "seq", -1)
    down_exit_grad = low(contract(low_down[0], grad_mine, 0, 0))
    exit_parts = quarter_stack(down_exit_grad)
    wide_one = jnp.concatenate([wide_one, jnp.stack([block_for(exit_parts, r) for r in range(4)])[:, None]], 1)
    chip_one = chip_half(wide_one.reshape(4, 5 * rank, share), 1, core)
    grad_blocks, wide_two = input_back(
        place_ids,
        (grad_filtered, grad_gates, after(came_edge, unit_own, chip_one), taps, prev, grad_hidden, tokens, normed, lows, select[0], gain_one, entry_full, column_full),
        kept,
        in_slabs,
        pieces,
    )
    grad_rows = [grad_blocks[0]] + [swap(grad_blocks[r], "mp", r) for r in (1, 2, 3)]
    grad_inputs = wide_value(jnp.stack(place(grad_rows, m)))
    chip_two = chip_half(wide_two.reshape(4, 4 * rank, share), 1, core)
    wide_own = jnp.concatenate([own_block(chip_one), own_block(chip_two)], 0)
    unit_own, wide_own = seq_total(unit_own), seq_total(wide_own)
    unit_grads = both_halves(unit_own, core)
    cut = 5 * rank // 2
    wide_one = both_halves(wide_own[:cut], core).reshape(5, rank, share)
    wide_two = both_halves(wide_own[cut:], core).reshape(4, rank, share)

    came = wide_value(after(came, grad_blocks))
    exit_stack = quarter_stack(exit_full[rank:])
    results = []
    for i, r in ((0, 0), (1, 2)):
        for t, stack in ((0, stack_mine), (1, stack_next)):
            tail = product(low_down[t], block_for(exit_stack, r))
            results.append(low(wide_value(block_for(stack, r)) + came[2 * (1 - t) + i] + tail))
    kept_rows = jnp.stack(place(results[:2], x))
    sent_rows = jnp.stack(place(results[2:], x))
    output = jnp.concatenate(place([kept_rows, swap(sent_rows, "mp", 2)], y), 0)
    return (
        output,
        grad_inputs,
        wide_two[0].T,
        wide_two[1:].swapaxes(0, 1),
        wide_one[3].T,
        wide_one[2],
        wide_one[0].T,
        unit_grads[:, :rank].T,
        wide_one[1].T,
        unit_grads[:, rank : 2 * rank].T,
        unit_grads[:, 2 * rank :],
        wide_one[4],
    )


def solution(mesh):
    fast = mesh.shape["mp"] == 4 and mesh.shape["seq"] % 4 == 0
    return jax.shard_map(
        fast_local if fast else general_local,
        mesh=mesh,
        in_specs=(
            P(None, "seq", "mp"),
            P(None, "seq", "mp"),
            P(),
            P(None, None, "mp"),
            P("mp", None),
            P(None, None, "mp"),
            P(None, "mp"),
            P("mp", None),
            P("mp", None),
            P(None, "mp"),
            P(),
            P(None, "mp"),
            P("mp", None),
            P(None, "mp"),
            P(None, "mp"),
            P("mp", None),
            P(None, "mp"),
            P("mp", None),
            P("mp", None),
            P(None, "mp"),
            P(),
            P(),
        ),
        out_specs=(
            P(None, "seq", "mp"),
            P(None, "seq", "mp"),
            P("mp", None),
            P(None, None, "mp"),
            P("mp", None),
            P(None, "mp"),
            P("mp", None),
            P(None, "mp"),
            P("mp", None),
            P(None, "mp"),
            P("mp", None),
            P(None, "mp"),
        ),
        check_vma=False,
    )
```

```python
import functools

import jax
import jax.numpy as jnp
from jax import lax
from jax.experimental import pallas as pl
from jax.experimental.pallas import tpu as pltpu
from jax.sharding import PartitionSpec as P

RANK = 16
ADAPT = 8
NDOC = 8


EPS = 1e-05


def from_behind(x, axis, by):
    count = lax.axis_size(axis)
    pairs = [(i, i + by) for i in range(count) if 0 <= i + by < count]
    return lax.ppermute(x, axis, pairs)


def contract(left, right, left_dim, right_extent):
    return lax.dot_general(
        left, right, (((left_dim,), (right_extent,)), ((), ())), preferred_element_type=jnp.float32
    )


def row_total(values):
    return lax.psum(jnp.sum(values, axis=-1), "mp")


def mid_total(parts):
    return lax.psum(parts, "mp")


def share_total(partial_value):
    return lax.psum_scatter(partial_value, "mp", scatter_dimension=1, tiled=True)


def column_products(share, weights):
    piece = lax.all_gather(share, "mp", axis=1, tiled=True)
    return tuple((jnp.dot(piece, weight, preferred_element_type=jnp.float32) for weight in weights))


def row_products(share, weight):
    return contract(lax.all_gather(share, "mp", axis=1, tiled=True), weight, 1, 1)


def doc_tables(starts, ids, length, offset):
    position = offset + jnp.arange(length, dtype=jnp.int32)
    begins = jnp.any(starts[:, :, None] == position[None, None, :], axis=1).astype(jnp.float32)
    earlier = jnp.any(starts[:, :, None] == position[None, None, :] - 1, axis=1).astype(jnp.float32)
    prev_one = 1.0 - begins
    prev_two = prev_one * (1.0 - earlier)
    segment = jnp.sum((starts[:, :, None] <= position[None, None, :]).astype(jnp.int32), axis=1) - 1
    document_onehot = (
        segment[:, :, None] == jnp.arange(NDOC, dtype=jnp.int32)[None, None, :]
    ).astype(jnp.float32)
    adapter_onehot = (ids[:, :, None] == jnp.arange(ADAPT, dtype=jnp.int32)[None, None, :]).astype(
        jnp.float32
    )
    token_onehot = jnp.einsum("cxn,cnt->cxt", document_onehot, adapter_onehot)
    select = jnp.repeat(token_onehot, RANK, axis=2).reshape(-1, ADAPT * RANK)
    return (prev_one, prev_two, select.astype(jnp.bfloat16))


def general_local(
    inputs,
    cotangent,
    mixer_gain,
    in_weight,
    in_entry,
    in_exit,
    conv_weight,
    out_weight,
    out_entry,
    out_exit,
    ffn_gain,
    gate_weight,
    gate_entry,
    gate_exit,
    up_weight,
    up_entry,
    up_exit,
    down_weight,
    down_entry,
    down_exit,
    doc_starts,
    adapter_ids,
):
    seq_count, length, width_share = inputs.shape
    tokens = seq_count * length
    width = width_share * lax.axis_size("mp")
    column = lax.axis_index("mp") * width_share
    prev_one, prev_two, select = doc_tables(
        doc_starts, adapter_ids, length, lax.axis_index("seq") * length
    )
    mixer_share = lax.dynamic_slice_in_dim(mixer_gain, column, width_share, 0).astype(jnp.float32)
    ffn_full = ffn_gain.astype(jnp.float32)
    ffn_share = lax.dynamic_slice_in_dim(ffn_full, column, width_share, 0)
    residual = inputs.reshape(tokens, width_share).astype(jnp.float32)
    scale_one = lax.rsqrt(row_total(residual * residual) / width + EPS)
    normed = (residual * scale_one[:, None] * mixer_share).astype(jnp.bfloat16)
    in_flat = in_weight.reshape(width, 3 * width_share)
    exit_flat = in_exit.reshape(in_exit.shape[0], 3 * width_share)
    inner_in = mid_total((jnp.dot(normed, in_entry, preferred_element_type=jnp.float32),))[0]
    low_in = inner_in.astype(jnp.bfloat16) * select
    project = column_products(normed, (in_flat,))[0] + jnp.dot(
        low_in, exit_flat, preferred_element_type=jnp.float32
    )
    parts = project.reshape(seq_count, length, 3, width_share)
    input_gate = parts[:, :, 0]
    output_gate = parts[:, :, 1]
    values = parts[:, :, 2]
    mixed = input_gate * values
    edge = from_behind(mixed[:, length - 2 :], "seq", 1)
    extended = jnp.concatenate([edge, mixed], 1)
    taps = conv_weight.astype(jnp.float32)
    filtered = (
        taps[2] * mixed
        + taps[1] * prev_one[..., None] * extended[:, 1 : length + 1]
        + taps[0] * prev_two[..., None] * extended[:, :length]
    )
    gated = (output_gate * filtered).astype(jnp.bfloat16).reshape(tokens, width_share)
    inner_out = mid_total((jnp.dot(gated, out_entry, preferred_element_type=jnp.float32),))[0]
    low_out = inner_out.astype(jnp.bfloat16) * select
    branch_tail = jnp.dot(low_out, out_exit, preferred_element_type=jnp.float32)
    partial_value = jnp.dot(gated, out_weight, preferred_element_type=jnp.float32)
    own = lax.dynamic_slice_in_dim(partial_value, column, width_share, 1) + residual + branch_tail
    rows_total = lax.psum(lax.dynamic_update_slice_in_dim(partial_value, own, column, 1), "mp")
    hidden = lax.dynamic_slice_in_dim(rows_total, column, width_share, 1)
    scale_two = lax.rsqrt(jnp.sum(rows_total * rows_total, axis=1) / width + EPS)
    normed_full = (rows_total * scale_two[:, None] * ffn_full).astype(jnp.bfloat16)
    normed_two = lax.dynamic_slice_in_dim(normed_full, column, width_share, 1)
    gate = jnp.dot(normed_full, gate_weight, preferred_element_type=jnp.float32)
    up = jnp.dot(normed_full, up_weight, preferred_element_type=jnp.float32)
    inner_gate, inner_up = mid_total(
        (
            jnp.dot(normed_two, gate_entry, preferred_element_type=jnp.float32),
            jnp.dot(normed_two, up_entry, preferred_element_type=jnp.float32),
        )
    )
    low_gate = inner_gate.astype(jnp.bfloat16) * select
    low_up = inner_up.astype(jnp.bfloat16) * select
    gate = gate + jnp.dot(low_gate, gate_exit, preferred_element_type=jnp.float32)
    up = up + jnp.dot(low_up, up_exit, preferred_element_type=jnp.float32)
    sigma = jax.nn.sigmoid(gate)
    swish = gate * sigma
    activated = (swish * up).astype(jnp.bfloat16)
    inner_down = mid_total((jnp.dot(activated, down_entry, preferred_element_type=jnp.float32),))[0]
    low_down = inner_down.astype(jnp.bfloat16) * select
    outcome = (
        hidden
        + share_total(jnp.dot(activated, down_weight, preferred_element_type=jnp.float32))
        + jnp.dot(low_down, down_exit, preferred_element_type=jnp.float32)
    )
    output = outcome.astype(jnp.bfloat16).reshape(seq_count, length, width_share)
    grad_hidden = cotangent.reshape(tokens, width_share).astype(jnp.float32)
    grad_down = grad_hidden.astype(jnp.bfloat16)
    grad_act = row_products(grad_down, down_weight)
    back_down = mid_total((contract(grad_down, down_exit, 1, 1),))[0]
    low_back_down = back_down.astype(jnp.bfloat16) * select
    grad_act = grad_act + contract(low_back_down, down_entry, 1, 1)
    down_entry_grad = contract(activated, low_back_down, 0, 0)
    down_exit_grad = contract(low_down, grad_down, 0, 0)
    up_projection_gradient = (grad_act * swish).astype(jnp.bfloat16)
    grad_gate = (grad_act * up * sigma * (1.0 + gate * (1.0 - sigma))).astype(jnp.bfloat16)
    back_gate, back_up = mid_total(
        (contract(grad_gate, gate_exit, 1, 1), contract(up_projection_gradient, up_exit, 1, 1))
    )
    low_back_gate = back_gate.astype(jnp.bfloat16) * select
    low_back_up = back_up.astype(jnp.bfloat16) * select
    grad_normed_two = share_total(
        contract(grad_gate, gate_weight, 1, 1) + contract(up_projection_gradient, up_weight, 1, 1)
    )
    grad_normed_two = (
        grad_normed_two
        + contract(low_back_gate, gate_entry, 1, 1)
        + contract(low_back_up, up_entry, 1, 1)
    )
    gate_entry_grad = contract(normed_two, low_back_gate, 0, 0)
    gate_exit_grad = contract(low_gate, grad_gate, 0, 0)
    up_entry_gradient = contract(normed_two, low_back_up, 0, 0)
    up_exit_grad = contract(low_up, up_projection_gradient, 0, 0)
    weighted_two = grad_normed_two * ffn_share
    cube_two = scale_two * scale_two * scale_two
    grad_hidden = (
        grad_hidden
        + scale_two[:, None] * weighted_two
        - hidden * (cube_two * row_total(weighted_two * hidden) / width)[:, None]
    )
    grad_branch = grad_hidden.astype(jnp.bfloat16)
    grad_gated = row_products(grad_branch, out_weight)
    back_out = mid_total((contract(grad_branch, out_exit, 1, 1),))[0]
    low_back_out = back_out.astype(jnp.bfloat16) * select
    grad_gated = grad_gated + contract(low_back_out, out_entry, 1, 1)
    out_entry_grad = contract(gated, low_back_out, 0, 0)
    out_exit_grad = contract(low_out, grad_branch, 0, 0)
    grad_gated = grad_gated.reshape(seq_count, length, width_share)
    grad_output_gate = grad_gated * filtered
    grad_filtered = grad_gated * output_gate
    near = taps[1] * prev_one[..., None] * grad_filtered
    far = taps[0] * prev_two[..., None] * grad_filtered
    sent = jnp.concatenate([far[:, :1], near[:, :1] + far[:, 1:2]], 1)
    came = from_behind(sent, "seq", -1)
    zero_one = jnp.zeros((seq_count, 1, width_share), jnp.float32)
    zero_two = jnp.zeros((seq_count, 2, width_share), jnp.float32)
    spacer = jnp.zeros((seq_count, length - 2, width_share), jnp.float32)
    grad_mixed = (
        taps[2] * grad_filtered
        + jnp.concatenate([near[:, 1:], zero_one], 1)
        + jnp.concatenate([far[:, 2:], zero_two], 1)
        + jnp.concatenate([spacer, came], 1)
    )
    grad_project = (
        jnp.stack([grad_mixed * values, grad_output_gate, grad_mixed * input_gate], 2)
        .reshape(tokens, 3 * width_share)
        .astype(jnp.bfloat16)
    )
    back_in = mid_total((contract(grad_project, exit_flat, 1, 1),))[0]
    low_back_in = back_in.astype(jnp.bfloat16) * select
    grad_normed = share_total(contract(grad_project, in_flat, 1, 1)) + contract(
        low_back_in, in_entry, 1, 1
    )
    in_entry_grad = contract(normed, low_back_in, 0, 0)
    in_exit_grad = contract(low_in, grad_project, 0, 0).reshape(in_exit.shape)
    weighted_one = grad_normed * mixer_share
    cube_one = scale_one * scale_one * scale_one
    grad_inputs = (
        grad_hidden
        + scale_one[:, None] * weighted_one
        - residual * (cube_one * row_total(weighted_one * residual) / width)[:, None]
    )
    summed = (
        lax.psum(in_entry_grad.astype(jnp.bfloat16), "seq").astype(jnp.float32),
        lax.psum(in_exit_grad.astype(jnp.bfloat16), "seq").astype(jnp.float32),
        lax.psum(out_entry_grad.astype(jnp.bfloat16), "seq").astype(jnp.float32),
        lax.psum(out_exit_grad.astype(jnp.bfloat16), "seq").astype(jnp.float32),
        lax.psum(gate_entry_grad.astype(jnp.bfloat16), "seq").astype(jnp.float32),
        lax.psum(gate_exit_grad.astype(jnp.bfloat16), "seq").astype(jnp.float32),
        lax.psum(up_entry_gradient.astype(jnp.bfloat16), "seq").astype(jnp.float32),
        lax.psum(up_exit_grad.astype(jnp.bfloat16), "seq").astype(jnp.float32),
        lax.psum(down_entry_grad.astype(jnp.bfloat16), "seq").astype(jnp.float32),
        lax.psum(down_exit_grad.astype(jnp.bfloat16), "seq").astype(jnp.float32),
    )
    return (
        output,
        grad_inputs.reshape(seq_count, length, width_share),
        summed[0],
        summed[1],
        summed[2],
        summed[3],
        summed[4],
        summed[5],
        summed[6],
        summed[7],
        summed[8],
        summed[9],
    )


VMEM_BYTES = 58 * 1024 * 1024


def product(left, right):
    return jnp.dot(left, right, preferred_element_type=jnp.float32)


def product_t(left, right):
    return lax.dot_general(left, right, (((1,), (1,)), ((), ())), preferred_element_type=jnp.float32)


def wide_value(value):
    return value.astype(jnp.float32)


def low(value):
    return value.astype(jnp.bfloat16)


def each_tile(total, size, body):
    whole = total // size
    if whole:

        @pl.loop(0, whole)
        def _(i):
            body(pl.multiple_of(i * size, size), size)

    if total % size:
        body(whole * size, total % size)


def spans(total, size):
    return [(at, min(size, total - at)) for at in range(0, total, size)]


class Mover:
    def __init__(self, sems):
        self.sems, self.count, self.pending = sems, 0, []

    def start(self, source, target):
        copy = pltpu.make_async_copy(source, target, self.sems.at[self.count])
        self.count += 1
        copy.start()
        self.pending.append(copy)
        return copy

    def wait(self, copies=None):
        for copy in list(self.pending if copies is None else copies):
            copy.wait()
            self.pending = [c for c in self.pending if c is not copy]


def piece_index(place_ref, kind, flip):
    return jnp.bitwise_xor(place_ref[1 if kind == "half" else 2], flip)


def start_in(mover, loads, own, pieces, plan, place_ref, target, width, share):
    for i in range(3):
        loads.append(mover.start(own.at[i], target.at[:, pl.ds(i * width, share)]))
    for ref, (r, kind, flip, _) in zip(pieces, plan):
        n = width // COUNT[kind]
        rows = pl.ds(pl.multiple_of(piece_index(place_ref, kind, flip) * n, 16), n)
        for i in range(3):
            loads.append(mover.start(ref.at[pl.ds(i * n, n)], target.at[rows, pl.ds(i * width + r * share, share)]))


def start_out(mover, loads, own, pieces, plan, place_ref, target, share):
    loads.append(mover.start(own, target.at[pl.ds(0, share)]))
    for ref, (r, kind, flip, base) in zip(pieces, plan):
        n = share // COUNT[kind]
        rows = pl.ds(pl.multiple_of(r * share + piece_index(place_ref, kind, flip) * n, 16), n)
        for i in range(4):
            loads.append(mover.start(ref.at[pl.ds(base + i * n, n)], target.at[rows, pl.ds(i * share, share)]))


def kernel_call(body, name, args, kinds, outs, scratch, sems, flops, size, out_space=pl.ANY):
    spaces = {"s": pltpu.SMEM, "v": pltpu.VMEM, "a": pl.ANY}
    return pl.pallas_call(
        body,
        out_shape=tuple(outs),
        in_specs=[pl.BlockSpec(memory_space=spaces[k]) for k in kinds],
        out_specs=tuple(pl.BlockSpec(memory_space=out_space) for _ in outs),
        scratch_shapes=list(scratch) + [pltpu.SemaphoreType.DMA((sems,))],
        compiler_params=pltpu.CompilerParams(vmem_limit_bytes=VMEM_BYTES),
        cost_estimate=pl.CostEstimate(flops=flops, bytes_accessed=size, transcendentals=0),
        name=name,
    )(*args)


def shaped(shape, kind=jnp.bfloat16):
    return jax.ShapeDtypeStruct(shape, kind)


TAP_ROWS = 16


class Rest:
    def __init__(self, share, rank, count):
        self.out_rows, self.side_rows = share // count, rank // count
        self.entry_at = 4 * self.out_rows
        self.side_at = self.entry_at + 2 * self.out_rows
        self.tap_at = self.side_at + 5 * self.side_rows
        self.rows = self.tap_at + TAP_ROWS


COUNT = {"half": 2, "quarter": 4}


def pack_in_kernel(place_ref, in_weight, out, sems):
    rows = in_weight.shape[1] // 4
    mover = Mover(sems)
    for i in range(3):
        part = pl.ds(pl.multiple_of(place_ref[2] * rows, 16), rows)
        mover.start(in_weight.at[i, part], out.at[pl.ds(i * rows, rows)])
    mover.wait()


def pack_in(place_ids, in_weight):
    _, width, share = in_weight.shape
    return kernel_call(
        pack_in_kernel, "pack_in", [place_ids, in_weight], "sa", [shaped((3 * width // 4, share))], [], 4, 0, 2_000_000, pltpu.VMEM
    )[0]


def pack_first_kernel(place_ref, inputs, cotangent, in_weight, out_weight, *refs):
    entries, (in_exit, out_exit, down_exit, taps), outs, sems = refs[:4], refs[4:8], refs[8:-1], refs[-1]
    far, beside, below, own_block, ct_rows, ct_far = outs
    share, width = out_weight.shape
    length, rank = inputs.shape[1], entries[0].shape[1]
    mover = Mover(sems)

    def part(index, rows):
        return pl.ds(pl.multiple_of(place_ref[index] * rows, 16), rows)

    in_rows = width // 4
    for i in range(3):
        mover.start(in_weight.at[i, part(2, in_rows)], far.at[pl.ds(i * in_rows, in_rows)])
    for index, target, base in ((2, far, 3 * in_rows), (1, beside, length), (1, below, length)):
        rest = Rest(share, rank, 4 if index == 2 else 2)
        rows = part(index, rest.out_rows)
        for i in range(4):
            spot = target.at[pl.ds(base + i * rest.out_rows, rest.out_rows)]
            mover.start(out_weight.at[rows, pl.ds(i * share, share)], spot)
            spot = target.at[pl.ds(base + rest.entry_at + i // 3 * rest.out_rows, rest.out_rows), pl.ds(i % 3 * rank, rank)]
            mover.start(entries[i].at[rows], spot)
        rows = part(index, rest.side_rows)
        for i, side in enumerate((in_exit.at[0], in_exit.at[1], in_exit.at[2], out_exit, down_exit)):
            mover.start(side.at[rows], target.at[pl.ds(base + rest.side_at + i * rest.side_rows, rest.side_rows)])
        mover.start(taps, target.at[pl.ds(base + rest.tap_at, TAP_ROWS)])
    far_block = far.at[pl.ds(far.shape[0] - length, length)]
    for r, target in enumerate((own_block, beside.at[pl.ds(0, length)], below.at[pl.ds(0, length)], far_block)):
        index = jnp.bitwise_xor(place_ref[0], r)
        mover.start(inputs.at[index], target)
        mover.start(cotangent.at[index], (ct_rows, ct_far)[r // 2].at[r % 2])
    mover.wait()


def pack_first(place_ids, inputs, cotangent, in_weight, out_weight, entries, sides, taps):
    length, share = inputs.shape[1:]
    width, rank = in_weight.shape[1], entries[0].shape[1]
    args = [place_ids, inputs, cotangent, in_weight, out_weight, *entries, *sides, taps]
    in_rows = 3 * width // 4
    heights = [in_rows + Rest(share, rank, 4).rows + length] + [length + Rest(share, rank, 2).rows] * 2 + [length]
    outs = [shaped((n, share)) for n in heights] + [shaped((2, length, share))] * 2
    return kernel_call(pack_first_kernel, "pack_first", args, "s" + "a" * 12, outs, [], 80, 0, 16_000_000, pltpu.VMEM)


def pack_second_kernel(cuts, place_ref, *refs):
    near, packs, sems = refs[:6], refs[6:-1], refs[-1]
    mover = Mover(sems)
    quarter_rows = near[0].shape[0] // 4
    width = near[0].shape[1]
    for (at, n), pack in zip(cuts, packs):
        rows = pl.ds(pl.multiple_of(place_ref[2] * quarter_rows + at, 16), n)
        for i in range(3):
            mover.start(near[2 * i].at[rows], pack.at[i, :, pl.ds(0, width)])
            mover.start(near[2 * i + 1].at[rows], pack.at[i, :, pl.ds(width, near[1].shape[1])])
    mover.wait()


def pack_second(place_ids, near, cuts):
    outs = [shaped((3, n, near[0].shape[1] + near[1].shape[1])) for _, n in cuts]
    return kernel_call(
        functools.partial(pack_second_kernel, cuts), "pack_second", [place_ids, *near], "s" + "a" * 6, outs, [], 32, 0, 20_000_000, pltpu.VMEM
    )


def mixer_kernel(in_plan, rest_plan, *refs):
    refs = list(refs)

    def take(n):
        return [refs.pop(0) for _ in range(n)]

    place_ref, select, prev, gain_one, gain_two = take(5)
    head, in_own, out_own, *own = take(11)
    entries_own, (in_exit, out_exit, down_exit, taps_own) = own[:4], own[4:]
    blocks = take(4)
    in_pieces, rest_pieces = take(len(in_plan)), take(len(rest_plan))
    kept_out, gated_out, tokens_out, normed_out, hidden_out, two_out, lows_out, entry_out, column_out, exit_out, taps_out = take(11)
    (x_s, n_s, in_s, out_s, entry_s, col_s, exit_s, tap_s, taps_s, proj_s, mix_s) = take(11)
    kept_s, gated_s, hid_s, two_s, low_in_s, lows_s, sems = refs
    length, width = gated_s.shape
    share, rank, edge = width // 4, low_in_s.shape[1], head.shape[1]
    mover = Mover(sems)

    def absolute(r):
        return pl.multiple_of(jnp.bitwise_xor(place_ref[0], r) * share, 128)

    for r in range(4):
        lanes = pl.ds(absolute(r), share)
        first = blocks[r].shape[0] - length if r == 3 else 0
        mover.start(blocks[r].at[pl.ds(first, length)], x_s.at[pl.ds(edge, length), lanes])
        mover.start(head.at[r], x_s.at[pl.ds(0, edge), lanes])
    token_loads = list(mover.pending)
    row_loads, column_loads, loads, out_loads = [], [], [], []
    for i, source in enumerate(entries_own):
        row_loads.append(mover.start(source, entry_s.at[pl.ds(absolute(0), share), pl.ds(i * rank, rank)]))
    for i, source in enumerate((in_exit.at[0], in_exit.at[1], in_exit.at[2], out_exit, down_exit)):
        column_loads.append(mover.start(source, col_s.at[pl.ds(i * rank, rank), pl.ds(0, share)]))
    column_loads.append(mover.start(taps_own, tap_s.at[:, pl.ds(0, share)]))
    for ref, (r, kind, flip, base) in zip(rest_pieces, rest_plan):
        rest, index, lanes = Rest(share, rank, COUNT[kind]), piece_index(place_ref, kind, flip), pl.ds(r * share, share)
        rows = pl.ds(pl.multiple_of(absolute(r) + index * rest.out_rows, 16), rest.out_rows)
        source = ref.at[pl.ds(base + rest.entry_at, rest.out_rows)]
        row_loads.append(mover.start(source, entry_s.at[rows, pl.ds(0, 3 * rank)]))
        source = ref.at[pl.ds(base + rest.entry_at + rest.out_rows, rest.out_rows), pl.ds(0, rank)]
        row_loads.append(mover.start(source, entry_s.at[rows, pl.ds(3 * rank, rank)]))
        for i in range(5):
            rows = pl.ds(pl.multiple_of(i * rank + index * rest.side_rows, 16), rest.side_rows)
            source = ref.at[pl.ds(base + rest.side_at + i * rest.side_rows, rest.side_rows)]
            column_loads.append(mover.start(source, col_s.at[rows, lanes]))
        if flip == 0:
            column_loads.append(mover.start(ref.at[pl.ds(base + rest.tap_at, TAP_ROWS)], tap_s.at[:, lanes]))
    start_in(mover, loads, in_own, in_pieces, in_plan, place_ref, in_s, width, share)
    start_out(mover, out_loads, out_own, rest_pieces, rest_plan, place_ref, out_s, share)
    mover.wait(token_loads)

    def norm(at, n):
        rows = pl.ds(at, n)
        x = wide_value(x_s[rows, :])
        scale = lax.rsqrt(jnp.sum(x * x, 1, keepdims=True) / width + EPS)
        n_s[rows, :] = low(x * scale * gain_one[...])

    each_tile(edge + length, 48, norm)
    main = pl.ds(edge, length)
    mover.start(x_s.at[main], tokens_out)
    mover.start(n_s.at[main], normed_out)
    mover.wait(row_loads)
    mover.start(entry_s, entry_out)
    low_in_s[...] = low(product(n_s[...], entry_s[:, pl.ds(0, rank)])) * select[...]
    lows_s[0] = low_in_s[main, :]
    mover.wait(column_loads)
    mover.start(col_s, column_out)
    taps_s[...] = wide_value(tap_s[...])[:8]
    mover.start(taps_s, taps_out)
    for r in range(4):
        exit_s[:, pl.ds(absolute(r), share)] = col_s[pl.ds(3 * rank, 2 * rank), pl.ds(r * share, share)]
    mover.start(exit_s, exit_out)
    mover.wait(loads)
    for i in range(3):

        def project(at, n):
            total = product(n_s[...], in_s[:, pl.ds(i * width + at, n)])
            total += product(low_in_s[...], col_s[pl.ds(i * rank, rank), pl.ds(at, n)])
            proj_s[:, pl.ds(i * width + at, n)] = total

        each_tile(width, width // 3, project)
    for r in range(4):
        lanes = pl.ds(r * share, share)
        mix_s[...] = proj_s[:, lanes] * proj_s[:, pl.ds(2 * width + r * share, share)]
        tap = [taps_s[pl.ds(i, 1), lanes] for i in range(3)]
        for at, n in spans(length, 128):
            rows, above = pl.ds(at, n), pl.ds(at + edge, n)
            filtered = (
                tap[2] * mix_s[above, :]
                + tap[1] * (prev[rows, pl.ds(0, 1)] * mix_s[pl.ds(at + edge - 1, n), :])
                + tap[0] * (prev[rows, pl.ds(1, 1)] * mix_s[pl.ds(at + edge - 2, n), :])
            )
            output_gate = proj_s[above, pl.ds(width + r * share, share)]
            gated_s[rows, lanes] = low(output_gate * filtered)
            kept_s[0, rows, lanes] = low(proj_s[above, lanes])
            kept_s[1, rows, lanes] = low(output_gate)
            kept_s[2, rows, lanes] = low(proj_s[above, pl.ds(2 * width + r * share, share)])
            kept_s[3, rows, lanes] = low(filtered)
    mover.start(kept_s, kept_out)
    mover.start(gated_s, gated_out)
    chosen = select[main, :]
    inner = 0.0
    for r in range(4):
        rows = pl.ds(absolute(r), share)
        inner = inner + product(gated_s[:, pl.ds(r * share, share)], entry_s[rows, pl.ds(rank, rank)])
    lows_s[1] = low(inner) * chosen
    mover.wait(out_loads)

    def branch(at, n):
        cols = pl.ds(at, n)
        total = product(gated_s[...], out_s[:, cols]) + product(lows_s[1], exit_s[pl.ds(0, rank), cols])
        hid_s[:, cols] = total + wide_value(x_s[main, cols])

    each_tile(width, width // 3, branch)
    mover.start(hid_s, hidden_out)

    def norm_two(at, n):
        rows = pl.ds(at, n)
        h = hid_s[rows, :]
        scale = lax.rsqrt(jnp.sum(h * h, 1, keepdims=True) / width + EPS)
        two_s[rows, :] = low(h * scale * gain_two[...])

    each_tile(length, 64, norm_two)
    mover.start(two_s, two_out)
    inner = product(two_s[...], entry_s[:, pl.ds(2 * rank, 2 * rank)])
    lows_s[2] = low(inner[:, :rank]) * chosen
    lows_s[3] = low(inner[:, rank:]) * chosen
    mover.start(lows_s, lows_out)
    mover.wait()


def mixer(place_ids, small, own, blocks, in_pieces, rest_pieces):
    length, share = blocks[0].shape
    width, rank, edge = 4 * share, own[3].shape[1], own[0].shape[1]
    bf, f32 = jnp.bfloat16, jnp.float32
    args = [place_ids, *small, *own, *blocks] + [p[0] for p in in_pieces + rest_pieces]
    kinds = "s" + "v" * len(small) + "a" * (len(args) - 1 - len(small))
    v = pltpu.VMEM
    columns, taps = 5 * rank, TAP_ROWS
    return kernel_call(
        functools.partial(mixer_kernel, [p[1:] for p in in_pieces], [p[1:] for p in rest_pieces]),
        "mixer",
        args,
        kinds,
        [
            shaped((4, length, width)),
            shaped((length, width)),
            shaped((length, width)),
            shaped((length, width)),
            shaped((length, width), f32),
            shaped((length, width)),
            shaped((4, length, rank)),
            shaped((width, 4 * rank)),
            shaped((columns, width)),
            shaped((2 * rank, width)),
            shaped((8, width), f32),
        ],
        [
            v((edge + length, width), bf),
            v((edge + length, width), bf),
            v((width, 3 * width), bf),
            v((width, width), bf),
            v((width, 4 * rank), bf),
            v((columns, width), bf),
            v((2 * rank, width), bf),
            v((taps, width), bf),
            v((8, width), f32),
            v((edge + length, 3 * width), f32),
            v((edge + length, share), f32),
            v((4, length, width), bf),
            v((length, width), bf),
            v((length, width), f32),
            v((length, width), bf),
            v((edge + length, rank), bf),
            v((4, length, rank), bf),
        ],
        200,
        2 * length * width * 4 * width,
        50_000_000,
    )


def ready_kernel(place_ref, select, exits, rows_mine, rows_far, rows_x, rows_far_x, grad_out, back_out, grad_s, back_s, sems):
    share, rank = rows_mine.shape[2], select.shape[2]
    mover = Mover(sems)
    for t in range(2):
        for r, source in enumerate((rows_mine.at[t], rows_x.at[1 - t], rows_far.at[t], rows_far_x.at[1 - t])):
            at = pl.multiple_of(jnp.bitwise_xor(place_ref[0], r) * share, 128)
            mover.start(source, grad_s.at[t, :, pl.ds(at, share)])
    mover.wait()
    mover.start(grad_s, grad_out)
    for t in range(2):
        back_s[t] = low(product_t(grad_s[t], exits[pl.ds(rank, rank), :])) * select[t]
    mover.start(back_s, back_out)
    mover.wait()


def ready(place_ids, select, exits, cotangents):
    length, share = cotangents[0].shape[1:]
    rank, width = select.shape[2], 4 * share
    shapes = [(2, length, width), (2, length, rank)]
    return kernel_call(
        ready_kernel,
        "ready",
        [place_ids, select, exits, *cotangents],
        "svvaaaa",
        [shaped(v) for v in shapes],
        [pltpu.VMEM(v, jnp.bfloat16) for v in shapes],
        16,
        4 * length * width * rank,
        10_000_000,
    )


def lows_kernel(select, seen, entry, lows):
    rank = select.shape[1]
    inner = product(seen[...], entry[:, pl.ds(2 * rank, 2 * rank)])
    lows[0] = low(inner[:, :rank]) * select[...]
    lows[1] = low(inner[:, rank:]) * select[...]


def lows_of(select, seen, entry):
    length, rank = select.shape
    return pl.pallas_call(
        lows_kernel,
        out_shape=shaped((2, length, rank)),
        in_specs=[pl.BlockSpec(memory_space=pltpu.VMEM)] * 3,
        out_specs=pl.BlockSpec(memory_space=pltpu.VMEM),
        cost_estimate=pl.CostEstimate(flops=4 * length * rank * seen.shape[1], bytes_accessed=3_000_000, transcendentals=0),
        compiler_params=pltpu.CompilerParams(vmem_limit_bytes=16 * 1024 * 1024),
        name="lows",
    )(select, seen, entry)


FAR_FLIPS = (0, 2, 1, 3)


def feed_kernel(far, add_tokens, add_grads, settle, sizes, which, turn, *refs):
    refs = list(refs)

    def take(n):
        return [refs.pop(0) for _ in range(n)]

    (quarter_ref,) = take(1) if far else (None,)
    token_refs = take(4)
    weights = take(4 if far else 6)
    prior_refs = take(2 * add_tokens + add_grads)
    down_out, back_out, grads_out = take(3)
    seen, lows, grad, low_back, gate_w, up_w, down_w, act_s, gg_s, gu_s, down_s, back_s, grads_s, *prior, sems = refs
    low_gate, low_up = lows.at[0], lows.at[1]
    width, rank, units = seen.shape[1], low_back.shape[1], gate_w.shape[0]
    whole, side = pl.ds(0, width), pl.ds(width, rank)
    steps = []
    for size in sizes:
        steps.append((sum(n for _, n in steps), size))
    quarter_rows = units // 4
    mover = Mover(sems)
    token_refs[1] = token_refs[1].at[pl.ds(which, 2)]
    token_refs[2], token_refs[3] = token_refs[2].at[turn], token_refs[3].at[turn]
    token_loads = [mover.start(a, b) for a, b in zip(token_refs, (seen, lows, grad, low_back))]
    loads = []
    if far:
        for n, ref in enumerate(weights):
            rows = pl.ds(n * quarter_rows, quarter_rows)
            for i, dst in enumerate((gate_w, up_w, down_w)):
                loads.append((n * quarter_rows, mover.start(ref.at[i], dst.at[rows])))
    else:
        for at, n in steps:
            rows = pl.ds(at, n)
            for i, dst in enumerate((gate_w, up_w, down_w)):
                loads.append((at, mover.start(weights[2 * i].at[rows], dst.at[rows, whole])))
                loads.append((at, mover.start(weights[2 * i + 1].at[rows], dst.at[rows, side])))
    prior_loads = [mover.start(a, b) for a, b in zip(prior_refs, prior)]
    if add_tokens:
        down_prior, back_prior = prior[:2]
    if add_grads:
        grads_prior = prior[-1]
    mover.wait(token_loads)

    for at, n in steps:
        while loads and loads[0][0] < at + n:
            mover.wait([loads.pop(0)[1]])
        cols = pl.ds(at, n)
        gate = product_t(seen[...], gate_w[cols, whole]) + product_t(low_gate[...], gate_w[cols, side])
        up = product_t(seen[...], up_w[cols, whole]) + product_t(low_up[...], up_w[cols, side])
        ga = product_t(grad[...], down_w[cols, whole]) + product_t(low_back[...], down_w[cols, side])
        sigma = jax.nn.sigmoid(gate)
        swish = gate * sigma
        act_s[:, cols] = low(swish * up)
        gu_s[:, cols] = low(ga * swish)
        gg_s[:, cols] = low(ga * up * (sigma + swish * (1.0 - sigma)))

    mover.wait(prior_loads)
    for i, (left, right) in enumerate(((low_gate, gg_s), (low_up, gu_s), (low_back, act_s))):
        turned, lanes = left[...].T, pl.ds(i * rank, rank)

        def grad_tile(at, n):
            cols = pl.ds(at, n)
            total = product(turned, right[:, cols]).T
            if add_grads:
                total += grads_prior[cols, lanes]
            grads_s[cols, lanes] = total

        each_tile(units, units if units < 640 else 512, grad_tile)
    if settle:
        for n, flip in enumerate(FAR_FLIPS):
            at = jnp.bitwise_xor(quarter_ref[0], flip)
            mover.start(grads_s.at[pl.ds(n * quarter_rows, quarter_rows)], grads_out.at[at])
    else:
        mover.start(grads_s, grads_out)

    def back_tile(at, n):
        cols = pl.ds(at, n)
        total = product(gg_s[...], gate_w[:, cols]) + product(gu_s[...], up_w[:, cols])
        if add_tokens:
            total += wide_value(back_prior[:, cols])
        back_s[:, cols] = low(total)

    each_tile(width, 512, back_tile)
    for i, (left, right) in enumerate(((gg_s, gate_w), (gu_s, up_w))):
        total = product(left[...], right[:, side])
        cols = pl.ds(width + i * rank, rank)
        if add_tokens:
            total += wide_value(back_prior[:, cols])
        back_s[:, cols] = low(total)
    mover.start(back_s, back_out)

    def down_tile(at, n):
        cols = pl.ds(at, n)
        total = product(act_s[...], down_w[:, cols])
        if add_tokens:
            total += wide_value(down_prior[:, cols])
        down_s[:, cols] = low(total)

    each_tile(width + rank, 512, down_tile)
    mover.start(down_s, down_out)
    mover.wait()


def feed(tokens, which, turn, weights, quarter=None, add_tokens=None, add_grads=None, settle=False):
    far = quarter is not None
    length, width = tokens[0].shape
    rank = tokens[1].shape[2]
    units = 4 * weights[0].shape[1] if far else weights[0].shape[0]
    sizes = [n for _, n in spans(units, 512)]
    if len(sizes) > 1 and sizes[-1] < 256:
        sizes[-2:] = [256, sizes[-2] + sizes[-1] - 256]
    bf, f32, v = jnp.bfloat16, jnp.float32, pltpu.VMEM
    args = ([quarter] if far else []) + list(tokens) + list(weights)
    shapes = [((length, width + rank), bf), ((length, width + 2 * rank), bf), ((units, 3 * rank), f32)]
    prior = list(add_tokens or ()) + ([] if add_grads is None else [add_grads])
    prior_scratch = (shapes[:2] if add_tokens else []) + ([] if add_grads is None else shapes[2:])
    outs = [shaped(*pair) for pair in shapes]
    if settle:
        outs[2] = shaped((4, units // 4, 3 * rank), f32)
    return kernel_call(
        functools.partial(
            feed_kernel, far, add_tokens is not None, add_grads is not None, settle, tuple(sizes), which, turn
        ),
        "feed_far" if far else "feed_near",
        args + prior,
        ("s" if far else "") + "a" * (4 + len(weights) + len(prior)),
        outs,
        [v((length, width), bf), v((2, length, rank), bf), v((length, width), bf), v((length, rank), bf)]
        + [v((units, width + rank), bf)] * 3
        + [v((length, units), bf)] * 3
        + [v(*pair) for pair in shapes + prior_scratch],
        48,
        12 * length * units * (width + 2 * rank),
        30_000_000,
    )


def branch_kernel(plan, *refs):
    refs = list(refs)

    def take(n):
        return [refs.pop(0) for _ in range(n)]

    place_ref, came, mine, hidden, grad, two, gated, lows, select, gain_two, entry, exits, taps, prev, down_mine, down_next = take(16)
    kept, near, far_0, far_1, far_2, out_own = take(6)
    pieces = take(len(plan))
    grad_hidden_out, filtered_out, gates_out, edge_out, keep_out, give_out, sent_out, own_out = take(8)
    near_s, far_s, pack_s, part_s, out_s, kept_s, w_s, gb_s, lo_s, gf_s, gate_s, edge_s, wide_s, sems = refs
    length, width = hidden.shape
    share, rank = width // 4, select.shape[1]
    mover = Mover(sems)
    start_out(mover, [], out_own, pieces, plan, place_ref, out_s, share)
    mover.start(kept.at[1], kept_s.at[0])
    mover.start(kept.at[3], kept_s.at[1])
    loads = list(mover.pending)
    unit_loads = [mover.start(near, near_s)]
    quarter_rows, at = near.shape[0] // 4, 0
    for far in (far_0, far_1, far_2):
        n = far.shape[1]
        for q in range(4):
            unit_loads.append(mover.start(far.at[q], far_s.at[pl.ds(q * quarter_rows + at, n)]))
        at += n
    part_s[0] = low(hidden[...] + wide_value(down_mine[:, pl.ds(0, width)]))
    part_s[1] = down_next[:, pl.ds(0, width)]
    for t in range(2):
        for r in range(4):
            lanes = pl.ds(pl.multiple_of(jnp.bitwise_xor(place_ref[0], r) * share, 128), share)
            target = (own_out if r % 2 == 0 else sent_out).at[2 * t + r // 2]
            mover.start(part_s.at[t, :, lanes], target)
    side = pl.ds(width, 2 * rank)
    inner = wide_value(came[:, side]) + wide_value(mine[:, side])
    lo_s[0] = low(inner[:, :rank]) * select[...]
    lo_s[1] = low(inner[:, rank:]) * select[...]

    def combine(at, n):
        cols = pl.ds(at, n)
        total = wide_value(came[:, cols]) + wide_value(mine[:, cols])
        total += product_t(lo_s[0], entry[cols, pl.ds(2 * rank, rank)])
        total += product_t(lo_s[1], entry[cols, pl.ds(3 * rank, rank)])
        w_s[:, cols] = total * gain_two[:, cols]

    each_tile(width, width // 3, combine)

    def norm(at, n):
        rows = pl.ds(at, n)
        h, w = hidden[rows, :], w_s[rows, :]
        scale = lax.rsqrt(jnp.sum(h * h, 1, keepdims=True) / width + EPS)
        moment = jnp.sum(w * h, 1, keepdims=True) / width
        value = wide_value(grad[0, rows, :]) + scale * w - h * (scale * scale * scale * moment)
        w_s[rows, :] = value
        gb_s[rows, :] = low(value)

    each_tile(length, 32, norm)
    mover.start(w_s, grad_hidden_out)
    lo_s[2] = low(product_t(gb_s[...], exits[pl.ds(0, rank), :])) * select[...]
    mover.wait(loads)
    for r in range(4):
        cols = pl.ds(r * share, share)
        rows = pl.ds(pl.multiple_of(jnp.bitwise_xor(place_ref[0], r) * share, 128), share)
        gg = product_t(gb_s[...], out_s[cols, :]) + product_t(lo_s[2], entry[rows, pl.ds(rank, rank)])
        gf = gg * wide_value(kept_s[0, :, cols])
        gf_s[:, cols] = low(gf)
        first = gf[:8]
        beside = taps[pl.ds(1, 1), cols] * (prev[pl.ds(0, 8), pl.ds(0, 1)] * first)
        beyond = taps[pl.ds(0, 1), cols] * (prev[pl.ds(0, 8), pl.ds(1, 1)] * first)
        edge_s[pl.ds(0, 1), cols] = beyond[0:1]
        edge_s[pl.ds(1, 1), cols] = beside[0:1] + beyond[1:2]
        edge_s[pl.ds(2, 6), cols] = jnp.zeros((6, share), jnp.float32)
        gate_s[:, cols] = low(gg * wide_value(kept_s[1, :, cols]))
    mover.start(gf_s, filtered_out)
    mover.start(gate_s, gates_out)
    mover.start(edge_s, edge_out)
    for i, (left, right) in enumerate(((lo_s.at[0], two), (lo_s.at[1], two), (lows.at[1], gb_s))):
        turned = left[...].T

        def wide_tile(at, n):
            cols = pl.ds(at, n)
            wide_s[i, :, cols] = low(product(turned, right[:, cols]))

        each_tile(width, width // 3, wide_tile)
    turned = lo_s[2].T
    for r in range(4):
        lanes = pl.ds(pl.multiple_of(jnp.bitwise_xor(place_ref[0], r) * share, 128), share)
        wide_s[3, :, lanes] = low(product(turned, gated[:, pl.ds(r * share, share)]))
    mover.wait(unit_loads)
    half = near.shape[0] // 2
    for h, out in ((0, keep_out), (1, give_out)):
        mine = jnp.bitwise_xor(place_ref[1], h)
        rows = pl.ds(pl.multiple_of(mine * half, 16), half)
        at = 0
        for r, units in ((0, near_s), (2, far_s), (1, None), (3, None)):
            lanes = pl.ds(pl.multiple_of(jnp.bitwise_xor(place_ref[0], r) * share, 128), share)
            for j in range(2):
                pack_s[h, pl.ds(at + j * rank, rank), :] = wide_s[mine * 2 + j, :, lanes]
            at += 2 * rank
            if units is not None:
                pack_s[h, pl.ds(at, half), :] = low(units[rows, :])
                at += half
        mover.start(pack_s.at[h], out)
    mover.wait()


def branch_back(place_ids, small, kept, units, own, pieces):
    length, width = small[2].shape
    share, rank, unit_rows = width // 4, small[7].shape[1], units[0].shape[0]
    bf, f32, v = jnp.bfloat16, jnp.float32, pltpu.VMEM
    return kernel_call(
        functools.partial(branch_kernel, [p[1:] for p in pieces]),
        "branch_back",
        [place_ids, *small, kept, *units, own, *[p[0] for p in pieces]],
        "s" + "v" * len(small) + "a" * (2 + len(units) + len(pieces)),
        [
            shaped((length, width), f32),
            shaped((length, width)),
            shaped((length, width)),
            shaped((8, width), f32),
            shaped((unit_rows + 8 * rank, share)),
            shaped((unit_rows + 8 * rank, share)),
            shaped((4, length, share)),
            shaped((4, length, share)),
        ],
        [
            v((unit_rows, share), f32),
            v((unit_rows, share), f32),
            v((2, unit_rows + 8 * rank, share), bf),
            v((2, length, width), bf),
            v((width, width), bf),
            v((2, length, width), bf),
            v((length, width), f32),
            v((length, width), bf),
            v((3, length, rank), bf),
            v((length, width), bf),
            v((length, width), bf),
            v((8, width), f32),
            v((4, rank, width), bf),
        ],
        80,
        2 * length * width * width + 8 * length * rank * width,
        40_000_000,
    )


def input_kernel(plan, *refs):
    refs = list(refs)

    def take(n):
        return [refs.pop(0) for _ in range(n)]

    place_ref, filtered, gates, tail, taps, prev, grad_hidden, tokens, normed, lows, select, gain_one, entry, column, low_down, grad_down = take(16)
    kept, in_own = take(2)
    pieces = take(len(plan))
    grad_out, keep_out, give_out = take(3)
    in_s, kept_s, near_s, far_s, gp_s, w_s, gi_s, lo_s, wide_s, entry_s, down_s, block_s, pack_s, sems = refs
    length, width = filtered.shape
    share, rank = width // 4, select.shape[1]
    mover = Mover(sems)
    first = [mover.start(kept.at[0], kept_s.at[0]), mover.start(kept.at[2], kept_s.at[1])]
    loads = []
    start_in(mover, loads, in_own, pieces, plan, place_ref, in_s, width, share)
    mover.wait(first)
    for r in range(4):
        lanes = pl.ds(r * share, share)
        tap = [taps[pl.ds(i, 1), lanes] for i in range(3)]
        for at, n in spans(length, 128):
            rows = pl.ds(at, n)
            value = wide_value(filtered[rows, lanes])
            near_s[rows, :] = tap[1] * (prev[rows, pl.ds(0, 1)] * value)
            far_s[rows, :] = tap[0] * (prev[rows, pl.ds(1, 1)] * value)
        near_s[pl.ds(length, 8), :] = jnp.zeros((8, share), jnp.float32)
        far_s[pl.ds(length, 8), :] = tail[:, lanes]
        for at, n in spans(length, 128):
            rows = pl.ds(at, n)
            mixed = tap[2] * wide_value(filtered[rows, lanes]) + near_s[pl.ds(at + 1, n), :] + far_s[pl.ds(at + 2, n), :]
            gp_s[rows, pl.ds(r * share, share)] = low(mixed * wide_value(kept_s[1, rows, lanes]))
            gp_s[rows, pl.ds(2 * width + r * share, share)] = low(mixed * wide_value(kept_s[0, rows, lanes]))
    gp_s[:, pl.ds(width, width)] = gates[...]
    inner = 0.0
    for i in range(3):
        inner = inner + product_t(gp_s[:, pl.ds(i * width, width)], column[pl.ds(i * rank, rank), :])
    lo_s[...] = low(inner) * select[...]
    turned = lows[0].T
    turned_back = lo_s[...].T

    def exit_tile(at, n):
        cols = pl.ds(at, n)
        wide_s[:, cols] = low(product(turned, gp_s[:, cols]))

    each_tile(3 * width, width // 3, exit_tile)

    def entry_tile(at, n):
        cols = pl.ds(at, n)
        entry_s[:, cols] = low(product(turned_back, normed[:, cols]))

    each_tile(width, width // 3, entry_tile)
    turned_down = low_down[0].T

    def down_tile(at, n):
        cols = pl.ds(at, n)
        down_s[:, cols] = low(product(turned_down, grad_down[0, :, cols]))

    each_tile(width, width // 3, down_tile)
    half = 5 * rank // 2
    for r in range(4):
        lanes = pl.ds(pl.multiple_of(jnp.bitwise_xor(place_ref[0], r) * share, 128), share)
        block_s[pl.ds(0, rank), :] = entry_s[:, lanes]
        for i in range(3):
            block_s[pl.ds((1 + i) * rank, rank), :] = wide_s[:, pl.ds(i * width + r * share, share)]
        block_s[pl.ds(4 * rank, rank), :] = down_s[:, lanes]
        for h in range(2):
            rows = pl.ds(pl.multiple_of(jnp.bitwise_xor(place_ref[1], h) * half, 16), half)
            pack_s[h, pl.ds(r * half, half), :] = block_s[rows, :]
    mover.start(pack_s.at[0], keep_out)
    mover.start(pack_s.at[1], give_out)
    mover.wait(loads)

    def back(at, n):
        cols = pl.ds(at, n)
        total = product_t(gp_s[...], in_s[cols, :]) + product_t(lo_s[...], entry[cols, pl.ds(0, rank)])
        w_s[:, cols] = total * gain_one[:, cols]

    each_tile(width, width // 3, back)

    def norm(at, n):
        rows = pl.ds(at, n)
        x, w = wide_value(tokens[rows, :]), w_s[rows, :]
        scale = lax.rsqrt(jnp.sum(x * x, 1, keepdims=True) / width + EPS)
        moment = jnp.sum(w * x, 1, keepdims=True) / width
        gi_s[rows, :] = low(grad_hidden[rows, :] + scale * w - x * (scale * scale * scale * moment))

    each_tile(length, 32, norm)
    for r in range(4):
        at = pl.multiple_of(jnp.bitwise_xor(place_ref[0], r) * share, 128)
        mover.start(gi_s.at[:, pl.ds(at, share)], grad_out.at[r])
    mover.wait()


def input_back(place_ids, small, kept, own, pieces):
    length, width = small[0].shape
    share, rank = width // 4, small[9].shape[1]
    bf, f32, v = jnp.bfloat16, jnp.float32, pltpu.VMEM
    return kernel_call(
        functools.partial(input_kernel, [p[1:] for p in pieces]),
        "input_back",
        [place_ids, *small, kept, own, *[p[0] for p in pieces]],
        "s" + "v" * len(small) + "a" * (2 + len(pieces)),
        [shaped((4, length, share)), shaped((10 * rank, share)), shaped((10 * rank, share))],
        [
            v((width, 3 * width), bf),
            v((2, length, width), bf),
            v((length + 8, share), f32),
            v((length + 8, share), f32),
            v((length, 3 * width), bf),
            v((length, width), f32),
            v((length, width), bf),
            v((length, rank), bf),
            v((rank, 3 * width), bf),
            v((rank, width), bf),
            v((rank, width), bf),
            v((5 * rank, share), bf),
            v((2, 10 * rank, share), bf),
        ],
        64,
        6 * length * width * width,
        40_000_000,
    )


def results_kernel(place_ref, own, came, low_down, exits, kept_out, sent_out, out_s, sems):
    share, rank = own.shape[2], low_down.shape[2]
    mover = Mover(sems)
    for i, out in ((0, kept_out), (1, sent_out)):
        lanes = pl.ds(pl.multiple_of(jnp.bitwise_xor(place_ref[0], 2 * i) * share, 128), share)
        for t in range(2):
            total = wide_value(own[2 * t + i]) + wide_value(came[2 * (1 - t) + i])
            out_s[2 * i + t] = low(total + product(low_down[t], exits[pl.ds(rank, rank), lanes]))
            mover.start(out_s.at[2 * i + t], out.at[jnp.bitwise_xor(place_ref[3], t)])
    mover.wait()


def results_of(place_ids, own, came, low_down, exits):
    count, length, share = own.shape
    return kernel_call(
        results_kernel,
        "results",
        [place_ids, own, came, low_down, exits],
        "svvvv",
        [shaped((2, length, share))] * 2,
        [pltpu.VMEM((count, length, share), jnp.bfloat16)],
        8,
        8 * length * share * low_down.shape[2],
        8_000_000,
    )


def finish_kernel(place_ref, one_own, one_other, two_own, two_other, *refs):
    in_entry, in_exit, out_entry, out_exit, gate_entry, gate_exit, up_entry, up_exit, down_entry, down_exit = refs[:10]
    one_s, two_s, sems = refs[10:]
    rank = in_entry.shape[1]
    mover = Mover(sems)
    for h, one, two in ((0, one_own, two_own), (1, one_other, two_other)):
        at = jnp.bitwise_xor(place_ref[1], h)
        mover.start(one, one_s.at[at])
        mover.start(two, two_s.at[at])
    mover.wait()
    first, second = pl.ds(0, rank), pl.ds(rank, rank)
    gate_entry[...] = wide_value(one_s[0, first, :]).T
    up_entry[...] = wide_value(one_s[0, second, :]).T
    out_exit[...] = wide_value(one_s[1, first, :])
    out_entry[...] = wide_value(one_s[1, second, :]).T
    half = gate_exit.shape[0] // 2
    for h in range(2):
        rows = pl.ds(h * half, half)
        for i, out in enumerate((gate_exit, up_exit, down_entry)):
            out[rows, :] = wide_value(one_s[h, pl.ds(2 * rank, half), pl.ds(i * rank, rank)])
    cut = rank // 2
    in_entry[...] = wide_value(two_s[0, first, :]).T
    in_exit[0] = wide_value(two_s[0, second, :])
    in_exit[1, pl.ds(0, cut), :] = wide_value(two_s[0, pl.ds(2 * rank, cut), :])
    in_exit[1, pl.ds(cut, cut), :] = wide_value(two_s[1, pl.ds(0, cut), :])
    in_exit[2] = wide_value(two_s[1, pl.ds(cut, rank), :])
    down_exit[...] = wide_value(two_s[1, pl.ds(cut + rank, rank), :])


def finish(place_ids, one_own, one_other, two_own, two_other, units, rank):
    share, f32, bf = one_own.shape[1], jnp.float32, jnp.bfloat16
    entry, exits, unit = (share, rank), (rank, share), (units, rank)
    shapes = [entry, (3, rank, share), entry, exits, entry, unit, entry, unit, unit, exits]
    return kernel_call(
        finish_kernel,
        "finish",
        [place_ids, one_own, one_other, two_own, two_other],
        "saaaa",
        [shaped(v, f32) for v in shapes],
        [pltpu.VMEM((2, *one_own.shape), bf), pltpu.VMEM((2, *two_own.shape), bf)],
        4,
        0,
        8_000_000,
        pltpu.VMEM,
    )


def swap(value, axis, bit):
    return lax.ppermute(value, axis, [(i, i ^ bit) for i in range(lax.axis_size(axis))])


def after(value, *others):
    return lax.optimization_barrier((value, others))[0]


def together(*values):
    return lax.optimization_barrier(values)


def place(relative, me):
    stacked = jnp.stack(relative)
    return [lax.dynamic_index_in_dim(stacked, a ^ me, 0, keepdims=False) for a in range(len(relative))]


def part_of(block, dim, index, count):
    rows = block.shape[dim] // count
    return lax.dynamic_slice_in_dim(block, index * rows, rows, dim)


def seq_step(value, bit):
    return low(wide_value(value) + wide_value(swap(value, "seq", bit)))


def seq_bits():
    return [2**k for k in range(1, 16) if 2**k < lax.axis_size("seq")]


def seq_total(value):
    for bit in seq_bits():
        value = seq_step(value, bit)
    return value


def seq_total_parts(value):
    s = lax.axis_index("seq")
    for bit in seq_bits():
        keep = s // bit % 2
        other = swap(part_of(value, 0, 1 - keep, 2), "seq", bit)
        value = low(wide_value(part_of(value, 0, keep, 2)) + wide_value(other))
    for bit in seq_bits()[::-1]:
        value = jnp.concatenate(place([value, swap(value, "seq", bit)], s // bit % 2), 0)
    return value


def chip_half(value, dim, core):
    other = swap(low(part_of(value, dim, 1 - core, 2)), "seq", 1)
    return low(wide_value(part_of(value, dim, core, 2)) + wide_value(other))


def own_block(chip):
    total = wide_value(chip[0])
    for r in (3, 1, 2):
        total = total + wide_value(swap(chip[r], "mp", r))
    return low(total)


def both_halves(own, core):
    return wide_value(jnp.concatenate(place([own, swap(own, "seq", 1)], core), 0))


def fast_local(
    inputs,
    cotangent,
    mixer_gain,
    in_weight,
    in_entry,
    in_exit,
    conv_weight,
    out_weight,
    out_entry,
    out_exit,
    ffn_gain,
    gate_weight,
    gate_entry,
    gate_exit,
    up_weight,
    up_entry,
    up_exit,
    down_weight,
    down_entry,
    down_exit,
    doc_starts,
    adapter_ids,
):
    seqs, length, share = inputs.shape
    width = 4 * share
    rank = in_entry.shape[1]
    units = gate_weight.shape[1]
    m = lax.axis_index("mp")
    s = lax.axis_index("seq")
    x, y, core, quarter = m % 2, m // 2, s % 2, s % 4
    place_ids = jnp.stack([m, core, quarter, x]).astype(jnp.int32)
    halo = 16

    def block_for(stack, r):
        return lax.dynamic_index_in_dim(stack, m ^ r, 0, keepdims=False)

    in_slabs = in_weight.swapaxes(0, 1)
    own_taps = jnp.pad(conv_weight, ((0, TAP_ROWS - 3), (0, 0)))
    entries = (in_entry, out_entry, gate_entry, up_entry)
    sides = (in_exit.swapaxes(0, 1), out_exit, down_exit)
    in_quarter = pack_in(place_ids, in_slabs)
    far_pack, beside, below, own_block_rows, ct_rows, ct_far = pack_first(
        after(place_ids, in_quarter), inputs, cotangent, in_slabs, out_weight, entries, sides, own_taps
    )
    near = [gate_weight.T, gate_exit.T, up_weight.T, up_exit.T, down_weight, down_entry]
    count = units // 4 // 16
    rows = (count * 3 // 10 * 16, count * 3 // 10 * 16)
    cuts = ((0, rows[0]), (rows[0], rows[1]), (rows[0] + rows[1], units // 4 - rows[0] - rows[1]))

    def spread(got, over, r, base):
        return [
            (got, r, "quarter", 0, base),
            (swap(got, "seq", 1), r, "quarter", 1, base),
            (over, r, "quarter", 2, base),
            (swap(over, "seq", 1), r, "quarter", 3, base),
        ]

    in_x, in_y = swap(in_quarter, "mp", 1), swap(in_quarter, "mp", 2)
    far_pack = swap(after(far_pack, in_x, in_y), "mp", 3)
    over_x, over_y = swap(in_x, "seq", 2), swap(in_y, "seq", 2)
    packed = pack_second(after(place_ids, in_x, in_y), near, cuts)
    beside, below = after((beside, below), in_x, in_y)
    beside, below = swap(beside, "mp", 1), swap(below, "mp", 2)
    in_pieces = spread(in_x, over_x, 1, 0) + spread(in_y, over_y, 2, 0)
    far_count = far_pack.shape[0] - length
    far_weights = far_pack[:far_count]
    over_far = swap(after(far_weights, [p[0] for p in in_pieces]), "seq", 2)
    row_blocks = [own_block_rows, beside, below, far_pack]
    ends = [length, length, length, far_pack.shape[0]]
    head = from_behind(jnp.stack([b[e - halo : e] for b, e in zip(row_blocks, ends)]), "seq", 1)
    far_pieces = spread(far_weights, over_far, 3, 3 * width // 4)
    in_pieces += [p[:4] + (0,) for p in far_pieces]
    rest_pieces = list(far_pieces)
    for got, r in ((beside, 1), (below, 2)):
        rest_pieces += [(got, r, "half", 0, length), (swap(got, "seq", 1), r, "half", 1, length)]
    ct_rows, ct_far, *packed = after((ct_rows, ct_far, *packed), [p[0] for p in rest_pieces])
    ct_x, ct_y, ct_g = swap(ct_rows, "mp", 1), swap(ct_far, "mp", 2), swap(ct_far, "mp", 3)
    packed = [packed[0], *after(tuple(packed[1:]), ct_x)]
    far_first = [swap(p, "mp", 2) for p in packed]

    starts = jnp.stack([doc_starts[m], doc_starts[m ^ 1]])[:, None, :]
    ids = jnp.stack([adapter_ids[m], adapter_ids[m ^ 1]])
    steps = (ids - jnp.pad(ids, ((0, 0), (1, 0)))[:, :-1])[:, None, :]
    position = (s * length - halo + jnp.arange(halo + length, dtype=jnp.int32))[None, :, None]
    adapter = jnp.sum(jnp.where(starts <= position, steps, 0), 2)
    lane = jnp.arange(rank, dtype=jnp.int32) // RANK
    select_ext = (adapter[:, :, None] == lane).astype(jnp.bfloat16)
    select = select_ext[:, halo:]
    begins = jnp.any(starts[0] == position[0], 1).astype(jnp.float32)
    prev_one = 1.0 - begins[halo:]
    prev_two = prev_one * (1.0 - begins[halo - 1 : halo - 1 + length])
    prev = jnp.stack([prev_one, prev_two], 1)
    gain_one = wide_value(mixer_gain)[None]
    gain_two = wide_value(ffn_gain)[None]

    kept, gated, tokens, normed, hidden, normed_two, lows, entry_full, column_full, exit_full, taps = mixer(
        place_ids,
        (select_ext[0], prev, gain_one, gain_two),
        (head, in_slabs, out_weight, *entries, *sides, own_taps),
        row_blocks,
        in_pieces,
        rest_pieces,
    )
    normed_next = swap(normed_two, "mp", 1)
    grad_down, back_lows = ready(place_ids, select, exit_full, (ct_rows, ct_y, ct_x, ct_g))
    lows_next = lows_of(select[1], normed_next, entry_full)
    mine = (normed_two, lows, grad_down, back_lows), 2, 0
    other = (normed_next, lows_next, grad_down, back_lows), 0, 1
    at_quarter = jnp.full((1,), quarter, jnp.int32)

    def spread_far(first, then, last):
        over = swap(after(first, then), "seq", 2)
        return [first, over, swap(after(first, last), "seq", 1), swap(after(over, last), "seq", 1)]

    near_mine = feed(*mine, near)
    near_next = feed(*other, near, add_grads=near_mine[2])
    far_zero = spread_far(far_first[0], near_mine[2], near_next[2])
    next_zero = feed(*other, far_zero, at_quarter, add_tokens=near_next[:2])
    mine_zero = feed(*mine, far_zero, at_quarter, add_tokens=near_mine[:2], add_grads=next_zero[2], settle=True)
    far_one = spread_far(far_first[1], near_mine[2], next_zero[2])
    next_one = feed(*other, far_one, at_quarter, add_tokens=next_zero[:2])
    far_two = spread_far(far_first[2], near_next[2], mine_zero[2])
    down_next, back_next, next_grads = feed(*other, far_two, at_quarter, add_tokens=next_one[:2])
    got_back = swap(back_next, "mp", 1)
    mine_one = feed(*mine, far_one, at_quarter, add_tokens=mine_zero[:2], add_grads=next_one[2], settle=True)
    down_mine, back_mine, mine_grads = feed(
        *mine, far_two, at_quarter, add_tokens=mine_one[:2], add_grads=next_grads, settle=True
    )

    grad_hidden, grad_filtered, grad_gates, edge, one_keep, one_give, sent, own_parts = branch_back(
        place_ids,
        (got_back, back_mine, hidden, grad_down, normed_two, gated, lows, select[0], gain_two, entry_full, exit_full, taps, prev, down_mine, down_next),
        kept,
        (near_next[2], mine_zero[2], mine_one[2], mine_grads),
        out_weight,
        rest_pieces,
    )
    came_edge = from_behind(edge, "seq", -1)
    came = swap(sent, "mp", 1)
    inner = after(jnp.stack([down_mine[:, width:], down_next[:, width:]]), got_back)
    inner_got = swap(inner, "mp", 1)
    low_down = low(wide_value(inner) + wide_value(inner_got[::-1])) * select

    def chip_sum(keep, give):
        return low(wide_value(keep) + wide_value(swap(give, "seq", 1)))

    one = chip_sum(one_keep, one_give)
    head_rows, unit_rows = 2 * rank, units // 2
    cut = head_rows + unit_rows
    one_x = swap(one[2 * cut : 2 * cut + head_rows], "mp", 1)
    one_y = swap(one[cut : 2 * cut], "mp", 2)
    one_g = swap(one[2 * cut + head_rows :], "mp", 3)
    grad_blocks, two_keep, two_give = input_back(
        place_ids,
        (grad_filtered, grad_gates, came_edge, taps, prev, grad_hidden, tokens, normed, lows, select[0], gain_one, entry_full, column_full, low_down, grad_down),
        kept,
        in_slabs,
        in_pieces,
    )
    one_own = wide_value(one[:cut]) + wide_value(one_y)
    one_own = one_own.at[:head_rows].add(wide_value(one_x) + wide_value(one_g))
    one_own = low(one_own)
    two = chip_sum(two_keep, two_give).reshape(4, 5 * rank // 2, share)
    two_own = own_block(two)
    grad_rows = [grad_blocks[0]] + [swap(after(grad_blocks[r], two_own), "mp", r) for r in (1, 2, 3)]
    grad_inputs = wide_value(jnp.stack(place(grad_rows, m)))
    one_own, two_own = seq_total_parts(one_own), seq_total(two_own)
    grads = finish(place_ids, one_own, swap(one_own, "seq", 1), two_own, swap(two_own, "seq", 1), units, rank)

    kept_rows, sent_rows = results_of(place_ids, own_parts, came, low_down, exit_full)
    output = jnp.concatenate(place([kept_rows, swap(sent_rows, "mp", 2)], y), 0)
    in_entry_grad, in_exit_grad, out_entry_grad, out_exit_grad, gate_entry_grad, gate_exit_grad = grads[:6]
    up_entry_grad, up_exit_grad, down_entry_grad, down_exit_grad = grads[6:]
    return (
        output,
        grad_inputs,
        in_entry_grad,
        in_exit_grad.swapaxes(0, 1),
        out_entry_grad,
        out_exit_grad,
        gate_entry_grad,
        gate_exit_grad.T,
        up_entry_grad,
        up_exit_grad.T,
        down_entry_grad,
        down_exit_grad,
    )


def solution(mesh):
    fast = mesh.shape["mp"] == 4 and mesh.shape["seq"] % 4 == 0
    return jax.shard_map(
        fast_local if fast else general_local,
        mesh=mesh,
        in_specs=(
            P(None, "seq", "mp"),
            P(None, "seq", "mp"),
            P(),
            P(None, None, "mp"),
            P("mp", None),
            P(None, None, "mp"),
            P(None, "mp"),
            P("mp", None),
            P("mp", None),
            P(None, "mp"),
            P(),
            P(None, "mp"),
            P("mp", None),
            P(None, "mp"),
            P(None, "mp"),
            P("mp", None),
            P(None, "mp"),
            P("mp", None),
            P("mp", None),
            P(None, "mp"),
            P(),
            P(),
        ),
        out_specs=(
            P(None, "seq", "mp"),
            P(None, "seq", "mp"),
            P("mp", None),
            P(None, None, "mp"),
            P("mp", None),
            P(None, "mp"),
            P("mp", None),
            P(None, "mp"),
            P("mp", None),
            P(None, "mp"),
            P("mp", None),
            P(None, "mp"),
        ),
        check_vma=False,
    )
```

```python
import functools

import jax
import jax.numpy as jnp
from jax import lax
from jax.experimental import pallas as pl
from jax.experimental.pallas import tpu as pltpu
from jax.sharding import PartitionSpec as P

RANK = 16
ADAPT = 8
NDOC = 8


EPS = 1e-05


def from_behind(x, axis, by):
    count = lax.axis_size(axis)
    pairs = [(i, i + by) for i in range(count) if 0 <= i + by < count]
    return lax.ppermute(x, axis, pairs)


def contract(left, right, left_dim, right_extent):
    return lax.dot_general(
        left, right, (((left_dim,), (right_extent,)), ((), ())), preferred_element_type=jnp.float32
    )


def row_total(values):
    return lax.psum(jnp.sum(values, axis=-1), "mp")


def mid_total(parts):
    return lax.psum(parts, "mp")


def share_total(partial_value):
    return lax.psum_scatter(partial_value, "mp", scatter_dimension=1, tiled=True)


def column_products(share, weights):
    piece = lax.all_gather(share, "mp", axis=1, tiled=True)
    return tuple((jnp.dot(piece, weight, preferred_element_type=jnp.float32) for weight in weights))


def row_products(share, weight):
    return contract(lax.all_gather(share, "mp", axis=1, tiled=True), weight, 1, 1)


def doc_tables(starts, ids, length, offset):
    position = offset + jnp.arange(length, dtype=jnp.int32)
    begins = jnp.any(starts[:, :, None] == position[None, None, :], axis=1).astype(jnp.float32)
    earlier = jnp.any(starts[:, :, None] == position[None, None, :] - 1, axis=1).astype(jnp.float32)
    prev_one = 1.0 - begins
    prev_two = prev_one * (1.0 - earlier)
    segment = jnp.sum((starts[:, :, None] <= position[None, None, :]).astype(jnp.int32), axis=1) - 1
    document_onehot = (
        segment[:, :, None] == jnp.arange(NDOC, dtype=jnp.int32)[None, None, :]
    ).astype(jnp.float32)
    adapter_onehot = (ids[:, :, None] == jnp.arange(ADAPT, dtype=jnp.int32)[None, None, :]).astype(
        jnp.float32
    )
    token_onehot = jnp.einsum("cxn,cnt->cxt", document_onehot, adapter_onehot)
    select = jnp.repeat(token_onehot, RANK, axis=2).reshape(-1, ADAPT * RANK)
    return (prev_one, prev_two, select.astype(jnp.bfloat16))


def general_local(
    inputs,
    cotangent,
    mixer_gain,
    in_weight,
    in_entry,
    in_exit,
    conv_weight,
    out_weight,
    out_entry,
    out_exit,
    ffn_gain,
    gate_weight,
    gate_entry,
    gate_exit,
    up_weight,
    up_entry,
    up_exit,
    down_weight,
    down_entry,
    down_exit,
    doc_starts,
    adapter_ids,
):
    seq_count, length, width_share = inputs.shape
    tokens = seq_count * length
    width = width_share * lax.axis_size("mp")
    column = lax.axis_index("mp") * width_share
    prev_one, prev_two, select = doc_tables(
        doc_starts, adapter_ids, length, lax.axis_index("seq") * length
    )
    mixer_share = lax.dynamic_slice_in_dim(mixer_gain, column, width_share, 0).astype(jnp.float32)
    ffn_full = ffn_gain.astype(jnp.float32)
    ffn_share = lax.dynamic_slice_in_dim(ffn_full, column, width_share, 0)
    residual = inputs.reshape(tokens, width_share).astype(jnp.float32)
    scale_one = lax.rsqrt(row_total(residual * residual) / width + EPS)
    normed = (residual * scale_one[:, None] * mixer_share).astype(jnp.bfloat16)
    in_flat = in_weight.reshape(width, 3 * width_share)
    exit_flat = in_exit.reshape(in_exit.shape[0], 3 * width_share)
    inner_in = mid_total((jnp.dot(normed, in_entry, preferred_element_type=jnp.float32),))[0]
    low_in = inner_in.astype(jnp.bfloat16) * select
    project = column_products(normed, (in_flat,))[0] + jnp.dot(
        low_in, exit_flat, preferred_element_type=jnp.float32
    )
    parts = project.reshape(seq_count, length, 3, width_share)
    input_gate = parts[:, :, 0]
    output_gate = parts[:, :, 1]
    values = parts[:, :, 2]
    mixed = input_gate * values
    edge = from_behind(mixed[:, length - 2 :], "seq", 1)
    extended = jnp.concatenate([edge, mixed], 1)
    taps = conv_weight.astype(jnp.float32)
    filtered = (
        taps[2] * mixed
        + taps[1] * prev_one[..., None] * extended[:, 1 : length + 1]
        + taps[0] * prev_two[..., None] * extended[:, :length]
    )
    gated = (output_gate * filtered).astype(jnp.bfloat16).reshape(tokens, width_share)
    inner_out = mid_total((jnp.dot(gated, out_entry, preferred_element_type=jnp.float32),))[0]
    low_out = inner_out.astype(jnp.bfloat16) * select
    branch_tail = jnp.dot(low_out, out_exit, preferred_element_type=jnp.float32)
    partial_value = jnp.dot(gated, out_weight, preferred_element_type=jnp.float32)
    own = lax.dynamic_slice_in_dim(partial_value, column, width_share, 1) + residual + branch_tail
    rows_total = lax.psum(lax.dynamic_update_slice_in_dim(partial_value, own, column, 1), "mp")
    hidden = lax.dynamic_slice_in_dim(rows_total, column, width_share, 1)
    scale_two = lax.rsqrt(jnp.sum(rows_total * rows_total, axis=1) / width + EPS)
    normed_full = (rows_total * scale_two[:, None] * ffn_full).astype(jnp.bfloat16)
    normed_two = lax.dynamic_slice_in_dim(normed_full, column, width_share, 1)
    gate = jnp.dot(normed_full, gate_weight, preferred_element_type=jnp.float32)
    up = jnp.dot(normed_full, up_weight, preferred_element_type=jnp.float32)
    inner_gate, inner_up = mid_total(
        (
            jnp.dot(normed_two, gate_entry, preferred_element_type=jnp.float32),
            jnp.dot(normed_two, up_entry, preferred_element_type=jnp.float32),
        )
    )
    low_gate = inner_gate.astype(jnp.bfloat16) * select
    low_up = inner_up.astype(jnp.bfloat16) * select
    gate = gate + jnp.dot(low_gate, gate_exit, preferred_element_type=jnp.float32)
    up = up + jnp.dot(low_up, up_exit, preferred_element_type=jnp.float32)
    sigma = jax.nn.sigmoid(gate)
    swish = gate * sigma
    activated = (swish * up).astype(jnp.bfloat16)
    inner_down = mid_total((jnp.dot(activated, down_entry, preferred_element_type=jnp.float32),))[0]
    low_down = inner_down.astype(jnp.bfloat16) * select
    outcome = (
        hidden
        + share_total(jnp.dot(activated, down_weight, preferred_element_type=jnp.float32))
        + jnp.dot(low_down, down_exit, preferred_element_type=jnp.float32)
    )
    output = outcome.astype(jnp.bfloat16).reshape(seq_count, length, width_share)
    grad_hidden = cotangent.reshape(tokens, width_share).astype(jnp.float32)
    grad_down = grad_hidden.astype(jnp.bfloat16)
    grad_act = row_products(grad_down, down_weight)
    back_down = mid_total((contract(grad_down, down_exit, 1, 1),))[0]
    low_back_down = back_down.astype(jnp.bfloat16) * select
    grad_act = grad_act + contract(low_back_down, down_entry, 1, 1)
    down_entry_grad = contract(activated, low_back_down, 0, 0)
    down_exit_grad = contract(low_down, grad_down, 0, 0)
    up_projection_gradient = (grad_act * swish).astype(jnp.bfloat16)
    grad_gate = (grad_act * up * sigma * (1.0 + gate * (1.0 - sigma))).astype(jnp.bfloat16)
    back_gate, back_up = mid_total(
        (contract(grad_gate, gate_exit, 1, 1), contract(up_projection_gradient, up_exit, 1, 1))
    )
    low_back_gate = back_gate.astype(jnp.bfloat16) * select
    low_back_up = back_up.astype(jnp.bfloat16) * select
    grad_normed_two = share_total(
        contract(grad_gate, gate_weight, 1, 1) + contract(up_projection_gradient, up_weight, 1, 1)
    )
    grad_normed_two = (
        grad_normed_two
        + contract(low_back_gate, gate_entry, 1, 1)
        + contract(low_back_up, up_entry, 1, 1)
    )
    gate_entry_grad = contract(normed_two, low_back_gate, 0, 0)
    gate_exit_grad = contract(low_gate, grad_gate, 0, 0)
    up_entry_gradient = contract(normed_two, low_back_up, 0, 0)
    up_exit_grad = contract(low_up, up_projection_gradient, 0, 0)
    weighted_two = grad_normed_two * ffn_share
    cube_two = scale_two * scale_two * scale_two
    grad_hidden = (
        grad_hidden
        + scale_two[:, None] * weighted_two
        - hidden * (cube_two * row_total(weighted_two * hidden) / width)[:, None]
    )
    grad_branch = grad_hidden.astype(jnp.bfloat16)
    grad_gated = row_products(grad_branch, out_weight)
    back_out = mid_total((contract(grad_branch, out_exit, 1, 1),))[0]
    low_back_out = back_out.astype(jnp.bfloat16) * select
    grad_gated = grad_gated + contract(low_back_out, out_entry, 1, 1)
    out_entry_grad = contract(gated, low_back_out, 0, 0)
    out_exit_grad = contract(low_out, grad_branch, 0, 0)
    grad_gated = grad_gated.reshape(seq_count, length, width_share)
    grad_output_gate = grad_gated * filtered
    grad_filtered = grad_gated * output_gate
    near = taps[1] * prev_one[..., None] * grad_filtered
    far = taps[0] * prev_two[..., None] * grad_filtered
    sent = jnp.concatenate([far[:, :1], near[:, :1] + far[:, 1:2]], 1)
    came = from_behind(sent, "seq", -1)
    zero_one = jnp.zeros((seq_count, 1, width_share), jnp.float32)
    zero_two = jnp.zeros((seq_count, 2, width_share), jnp.float32)
    spacer = jnp.zeros((seq_count, length - 2, width_share), jnp.float32)
    grad_mixed = (
        taps[2] * grad_filtered
        + jnp.concatenate([near[:, 1:], zero_one], 1)
        + jnp.concatenate([far[:, 2:], zero_two], 1)
        + jnp.concatenate([spacer, came], 1)
    )
    grad_project = (
        jnp.stack([grad_mixed * values, grad_output_gate, grad_mixed * input_gate], 2)
        .reshape(tokens, 3 * width_share)
        .astype(jnp.bfloat16)
    )
    back_in = mid_total((contract(grad_project, exit_flat, 1, 1),))[0]
    low_back_in = back_in.astype(jnp.bfloat16) * select
    grad_normed = share_total(contract(grad_project, in_flat, 1, 1)) + contract(
        low_back_in, in_entry, 1, 1
    )
    in_entry_grad = contract(normed, low_back_in, 0, 0)
    in_exit_grad = contract(low_in, grad_project, 0, 0).reshape(in_exit.shape)
    weighted_one = grad_normed * mixer_share
    cube_one = scale_one * scale_one * scale_one
    grad_inputs = (
        grad_hidden
        + scale_one[:, None] * weighted_one
        - residual * (cube_one * row_total(weighted_one * residual) / width)[:, None]
    )
    summed = (
        lax.psum(in_entry_grad.astype(jnp.bfloat16), "seq").astype(jnp.float32),
        lax.psum(in_exit_grad.astype(jnp.bfloat16), "seq").astype(jnp.float32),
        lax.psum(out_entry_grad.astype(jnp.bfloat16), "seq").astype(jnp.float32),
        lax.psum(out_exit_grad.astype(jnp.bfloat16), "seq").astype(jnp.float32),
        lax.psum(gate_entry_grad.astype(jnp.bfloat16), "seq").astype(jnp.float32),
        lax.psum(gate_exit_grad.astype(jnp.bfloat16), "seq").astype(jnp.float32),
        lax.psum(up_entry_gradient.astype(jnp.bfloat16), "seq").astype(jnp.float32),
        lax.psum(up_exit_grad.astype(jnp.bfloat16), "seq").astype(jnp.float32),
        lax.psum(down_entry_grad.astype(jnp.bfloat16), "seq").astype(jnp.float32),
        lax.psum(down_exit_grad.astype(jnp.bfloat16), "seq").astype(jnp.float32),
    )
    return (
        output,
        grad_inputs.reshape(seq_count, length, width_share),
        summed[0],
        summed[1],
        summed[2],
        summed[3],
        summed[4],
        summed[5],
        summed[6],
        summed[7],
        summed[8],
        summed[9],
    )


VMEM_BYTES = 58 * 1024 * 1024


def product(left, right):
    return jnp.dot(left, right, preferred_element_type=jnp.float32)


def product_t(left, right):
    return lax.dot_general(left, right, (((1,), (1,)), ((), ())), preferred_element_type=jnp.float32)


def wide_value(value):
    return value.astype(jnp.float32)


def low(value):
    return value.astype(jnp.bfloat16)


def each_tile(total, size, body):
    whole = total // size
    if whole:

        @pl.loop(0, whole)
        def _(i):
            body(pl.multiple_of(i * size, size), size)

    if total % size:
        body(whole * size, total % size)


def spans(total, size):
    return [(at, min(size, total - at)) for at in range(0, total, size)]


class Mover:
    def __init__(self, sems):
        self.sems, self.count, self.pending = sems, 0, []

    def start(self, source, target):
        copy = pltpu.make_async_copy(source, target, self.sems.at[self.count])
        self.count += 1
        copy.start()
        self.pending.append(copy)
        return copy

    def wait(self, copies=None):
        for copy in list(self.pending if copies is None else copies):
            copy.wait()
            self.pending = [c for c in self.pending if c is not copy]


def piece_index(place_ref, kind, flip):
    return jnp.bitwise_xor(place_ref[1 if kind == "half" else 2], flip)


def start_in(mover, loads, own, pieces, plan, place_ref, target, width, share):
    for i in range(3):
        loads.append(mover.start(own.at[i], target.at[:, pl.ds(i * width, share)]))
    for ref, (r, kind, flip, _) in zip(pieces, plan):
        n = width // COUNT[kind]
        rows = pl.ds(pl.multiple_of(piece_index(place_ref, kind, flip) * n, 16), n)
        for i in range(3):
            loads.append(mover.start(ref.at[pl.ds(i * n, n)], target.at[rows, pl.ds(i * width + r * share, share)]))


def start_out(mover, loads, own, pieces, plan, place_ref, target, share):
    loads.append(mover.start(own, target.at[pl.ds(0, share)]))
    for ref, (r, kind, flip, base) in zip(pieces, plan):
        n = share // COUNT[kind]
        rows = pl.ds(pl.multiple_of(r * share + piece_index(place_ref, kind, flip) * n, 16), n)
        for i in range(4):
            loads.append(mover.start(ref.at[pl.ds(base + i * n, n)], target.at[rows, pl.ds(i * share, share)]))


def kernel_call(body, name, args, kinds, outs, scratch, sems, flops, size, out_space=pl.ANY):
    spaces = {"s": pltpu.SMEM, "v": pltpu.VMEM, "a": pl.ANY}
    return pl.pallas_call(
        body,
        out_shape=tuple(outs),
        in_specs=[pl.BlockSpec(memory_space=spaces[k]) for k in kinds],
        out_specs=tuple(pl.BlockSpec(memory_space=out_space) for _ in outs),
        scratch_shapes=list(scratch) + [pltpu.SemaphoreType.DMA((sems,))],
        compiler_params=pltpu.CompilerParams(vmem_limit_bytes=VMEM_BYTES),
        cost_estimate=pl.CostEstimate(flops=flops, bytes_accessed=size, transcendentals=0),
        name=name,
    )(*args)


def shaped(shape, kind=jnp.bfloat16):
    return jax.ShapeDtypeStruct(shape, kind)


TAP_ROWS = 16


class Rest:
    def __init__(self, share, rank, count):
        self.out_rows, self.side_rows = share // count, rank // count
        self.entry_at = 4 * self.out_rows
        self.side_at = self.entry_at + 2 * self.out_rows
        self.tap_at = self.side_at + 5 * self.side_rows
        self.rows = self.tap_at + TAP_ROWS


COUNT = {"half": 2, "quarter": 4}


def pack_in_kernel(place_ref, in_weight, out, sems):
    rows = in_weight.shape[1] // 4
    mover = Mover(sems)
    for i in range(3):
        part = pl.ds(pl.multiple_of(place_ref[2] * rows, 16), rows)
        mover.start(in_weight.at[i, part], out.at[pl.ds(i * rows, rows)])
    mover.wait()


def pack_in(place_ids, in_weight):
    _, width, share = in_weight.shape
    return kernel_call(
        pack_in_kernel, "pack_in", [place_ids, in_weight], "sa", [shaped((3 * width // 4, share))], [], 4, 0, 2_000_000, pltpu.VMEM
    )[0]


def pack_first_kernel(place_ref, inputs, cotangent, in_weight, out_weight, *refs):
    entries, (in_exit, out_exit, down_exit, taps), outs, sems = refs[:4], refs[4:8], refs[8:-1], refs[-1]
    far, beside, below, own_block, ct_rows, ct_far = outs
    share, width = out_weight.shape
    length, rank = inputs.shape[1], entries[0].shape[1]
    mover = Mover(sems)

    def part(index, rows):
        return pl.ds(pl.multiple_of(place_ref[index] * rows, 16), rows)

    in_rows = width // 4
    for i in range(3):
        mover.start(in_weight.at[i, part(2, in_rows)], far.at[pl.ds(i * in_rows, in_rows)])
    for index, target, base in ((2, far, 3 * in_rows), (1, beside, length), (1, below, length)):
        rest = Rest(share, rank, 4 if index == 2 else 2)
        rows = part(index, rest.out_rows)
        for i in range(4):
            spot = target.at[pl.ds(base + i * rest.out_rows, rest.out_rows)]
            mover.start(out_weight.at[rows, pl.ds(i * share, share)], spot)
            spot = target.at[pl.ds(base + rest.entry_at + i // 3 * rest.out_rows, rest.out_rows), pl.ds(i % 3 * rank, rank)]
            mover.start(entries[i].at[rows], spot)
        rows = part(index, rest.side_rows)
        for i, side in enumerate((in_exit.at[0], in_exit.at[1], in_exit.at[2], out_exit, down_exit)):
            mover.start(side.at[rows], target.at[pl.ds(base + rest.side_at + i * rest.side_rows, rest.side_rows)])
        mover.start(taps, target.at[pl.ds(base + rest.tap_at, TAP_ROWS)])
    far_block = far.at[pl.ds(far.shape[0] - length, length)]
    for r, target in enumerate((own_block, beside.at[pl.ds(0, length)], below.at[pl.ds(0, length)], far_block)):
        index = jnp.bitwise_xor(place_ref[0], r)
        mover.start(inputs.at[index], target)
        mover.start(cotangent.at[index], (ct_rows, ct_far)[r // 2].at[r % 2])
    mover.wait()


def pack_first(place_ids, inputs, cotangent, in_weight, out_weight, entries, sides, taps):
    length, share = inputs.shape[1:]
    width, rank = in_weight.shape[1], entries[0].shape[1]
    args = [place_ids, inputs, cotangent, in_weight, out_weight, *entries, *sides, taps]
    in_rows = 3 * width // 4
    heights = [in_rows + Rest(share, rank, 4).rows + length] + [length + Rest(share, rank, 2).rows] * 2 + [length]
    outs = [shaped((n, share)) for n in heights] + [shaped((2, length, share))] * 2
    return kernel_call(pack_first_kernel, "pack_first", args, "s" + "a" * 12, outs, [], 80, 0, 16_000_000, pltpu.VMEM)


def pack_second_kernel(cuts, place_ref, *refs):
    near, packs, sems = refs[:6], refs[6:-1], refs[-1]
    mover = Mover(sems)
    quarter_rows = near[0].shape[0] // 4
    width = near[0].shape[1]
    for (at, n), pack in zip(cuts, packs):
        rows = pl.ds(pl.multiple_of(place_ref[2] * quarter_rows + at, 16), n)
        for i in range(3):
            mover.start(near[2 * i].at[rows], pack.at[i, :, pl.ds(0, width)])
            mover.start(near[2 * i + 1].at[rows], pack.at[i, :, pl.ds(width, near[1].shape[1])])
    mover.wait()


def pack_second(place_ids, near, cuts):
    outs = [shaped((3, n, near[0].shape[1] + near[1].shape[1])) for _, n in cuts]
    return kernel_call(
        functools.partial(pack_second_kernel, cuts), "pack_second", [place_ids, *near], "s" + "a" * 6, outs, [], 32, 0, 20_000_000, pltpu.VMEM
    )


def mixer_kernel(in_plan, rest_plan, *refs):
    refs = list(refs)

    def take(n):
        return [refs.pop(0) for _ in range(n)]

    place_ref, select, prev, gain_one, gain_two = take(5)
    head, in_own, out_own, *own = take(11)
    entries_own, (in_exit, out_exit, down_exit, taps_own) = own[:4], own[4:]
    blocks = take(4)
    in_pieces, rest_pieces = take(len(in_plan)), take(len(rest_plan))
    kept_out, gated_out, tokens_out, normed_out, hidden_out, two_out, lows_out, entry_out, column_out, exit_out, taps_out = take(11)
    (x_s, n_s, in_s, out_s, entry_s, col_s, exit_s, tap_s, taps_s, proj_s, mix_s) = take(11)
    kept_s, gated_s, hid_s, two_s, low_in_s, lows_s, sems = refs
    length, width = gated_s.shape
    share, rank, edge = width // 4, low_in_s.shape[1], head.shape[1]
    mover = Mover(sems)

    def absolute(r):
        return pl.multiple_of(jnp.bitwise_xor(place_ref[0], r) * share, 128)

    for r in range(4):
        lanes = pl.ds(absolute(r), share)
        first = blocks[r].shape[0] - length if r == 3 else 0
        mover.start(blocks[r].at[pl.ds(first, length)], x_s.at[pl.ds(edge, length), lanes])
        mover.start(head.at[r], x_s.at[pl.ds(0, edge), lanes])
    token_loads = list(mover.pending)
    row_loads, column_loads, loads, out_loads = [], [], [], []
    for i, source in enumerate(entries_own):
        row_loads.append(mover.start(source, entry_s.at[pl.ds(absolute(0), share), pl.ds(i * rank, rank)]))
    for i, source in enumerate((in_exit.at[0], in_exit.at[1], in_exit.at[2], out_exit, down_exit)):
        column_loads.append(mover.start(source, col_s.at[pl.ds(i * rank, rank), pl.ds(0, share)]))
    column_loads.append(mover.start(taps_own, tap_s.at[:, pl.ds(0, share)]))
    for ref, (r, kind, flip, base) in zip(rest_pieces, rest_plan):
        rest, index, lanes = Rest(share, rank, COUNT[kind]), piece_index(place_ref, kind, flip), pl.ds(r * share, share)
        rows = pl.ds(pl.multiple_of(absolute(r) + index * rest.out_rows, 16), rest.out_rows)
        source = ref.at[pl.ds(base + rest.entry_at, rest.out_rows)]
        row_loads.append(mover.start(source, entry_s.at[rows, pl.ds(0, 3 * rank)]))
        source = ref.at[pl.ds(base + rest.entry_at + rest.out_rows, rest.out_rows), pl.ds(0, rank)]
        row_loads.append(mover.start(source, entry_s.at[rows, pl.ds(3 * rank, rank)]))
        for i in range(5):
            rows = pl.ds(pl.multiple_of(i * rank + index * rest.side_rows, 16), rest.side_rows)
            source = ref.at[pl.ds(base + rest.side_at + i * rest.side_rows, rest.side_rows)]
            column_loads.append(mover.start(source, col_s.at[rows, lanes]))
        if flip == 0:
            column_loads.append(mover.start(ref.at[pl.ds(base + rest.tap_at, TAP_ROWS)], tap_s.at[:, lanes]))
    start_in(mover, loads, in_own, in_pieces, in_plan, place_ref, in_s, width, share)
    start_out(mover, out_loads, out_own, rest_pieces, rest_plan, place_ref, out_s, share)
    mover.wait(token_loads)

    def norm(at, n):
        rows = pl.ds(at, n)
        x = wide_value(x_s[rows, :])
        scale = lax.rsqrt(jnp.sum(x * x, 1, keepdims=True) / width + EPS)
        n_s[rows, :] = low(x * scale * gain_one[...])

    each_tile(edge + length, 48, norm)
    main = pl.ds(edge, length)
    mover.start(x_s.at[main], tokens_out)
    mover.start(n_s.at[main], normed_out)
    mover.wait(row_loads)
    mover.start(entry_s, entry_out)
    low_in_s[...] = low(product(n_s[...], entry_s[:, pl.ds(0, rank)])) * select[...]
    lows_s[0] = low_in_s[main, :]
    mover.wait(column_loads)
    mover.start(col_s, column_out)
    taps_s[...] = wide_value(tap_s[...])[:8]
    mover.start(taps_s, taps_out)
    for r in range(4):
        exit_s[:, pl.ds(absolute(r), share)] = col_s[pl.ds(3 * rank, 2 * rank), pl.ds(r * share, share)]
    mover.start(exit_s, exit_out)
    mover.wait(loads)
    for i in range(3):

        def project(at, n):
            total = product(n_s[...], in_s[:, pl.ds(i * width + at, n)])
            total += product(low_in_s[...], col_s[pl.ds(i * rank, rank), pl.ds(at, n)])
            proj_s[:, pl.ds(i * width + at, n)] = total

        each_tile(width, width // 3, project)
    for r in range(4):
        lanes = pl.ds(r * share, share)
        mix_s[...] = proj_s[:, lanes] * proj_s[:, pl.ds(2 * width + r * share, share)]
        tap = [taps_s[pl.ds(i, 1), lanes] for i in range(3)]
        for at, n in spans(length, 128):
            rows, above = pl.ds(at, n), pl.ds(at + edge, n)
            filtered = (
                tap[2] * mix_s[above, :]
                + tap[1] * (prev[rows, pl.ds(0, 1)] * mix_s[pl.ds(at + edge - 1, n), :])
                + tap[0] * (prev[rows, pl.ds(1, 1)] * mix_s[pl.ds(at + edge - 2, n), :])
            )
            output_gate = proj_s[above, pl.ds(width + r * share, share)]
            gated_s[rows, lanes] = low(output_gate * filtered)
            kept_s[0, rows, lanes] = low(proj_s[above, lanes])
            kept_s[1, rows, lanes] = low(output_gate)
            kept_s[2, rows, lanes] = low(proj_s[above, pl.ds(2 * width + r * share, share)])
            kept_s[3, rows, lanes] = low(filtered)
    mover.start(kept_s, kept_out)
    mover.start(gated_s, gated_out)
    chosen = select[main, :]
    inner = 0.0
    for r in range(4):
        rows = pl.ds(absolute(r), share)
        inner = inner + product(gated_s[:, pl.ds(r * share, share)], entry_s[rows, pl.ds(rank, rank)])
    lows_s[1] = low(inner) * chosen
    mover.wait(out_loads)

    def branch(at, n):
        cols = pl.ds(at, n)
        total = product(gated_s[...], out_s[:, cols]) + product(lows_s[1], exit_s[pl.ds(0, rank), cols])
        hid_s[:, cols] = total + wide_value(x_s[main, cols])

    each_tile(width, width // 3, branch)
    mover.start(hid_s, hidden_out)

    def norm_two(at, n):
        rows = pl.ds(at, n)
        h = hid_s[rows, :]
        scale = lax.rsqrt(jnp.sum(h * h, 1, keepdims=True) / width + EPS)
        two_s[rows, :] = low(h * scale * gain_two[...])

    each_tile(length, 64, norm_two)
    mover.start(two_s, two_out)
    inner = product(two_s[...], entry_s[:, pl.ds(2 * rank, 2 * rank)])
    lows_s[2] = low(inner[:, :rank]) * chosen
    lows_s[3] = low(inner[:, rank:]) * chosen
    mover.start(lows_s, lows_out)
    mover.wait()


def mixer(place_ids, small, own, blocks, in_pieces, rest_pieces):
    length, share = blocks[0].shape
    width, rank, edge = 4 * share, own[3].shape[1], own[0].shape[1]
    bf, f32 = jnp.bfloat16, jnp.float32
    args = [place_ids, *small, *own, *blocks] + [p[0] for p in in_pieces + rest_pieces]
    kinds = "s" + "v" * len(small) + "a" * (len(args) - 1 - len(small))
    v = pltpu.VMEM
    columns, taps = 5 * rank, TAP_ROWS
    return kernel_call(
        functools.partial(mixer_kernel, [p[1:] for p in in_pieces], [p[1:] for p in rest_pieces]),
        "mixer",
        args,
        kinds,
        [
            shaped((4, length, width)),
            shaped((length, width)),
            shaped((length, width)),
            shaped((length, width)),
            shaped((length, width), f32),
            shaped((length, width)),
            shaped((4, length, rank)),
            shaped((width, 4 * rank)),
            shaped((columns, width)),
            shaped((2 * rank, width)),
            shaped((8, width), f32),
        ],
        [
            v((edge + length, width), bf),
            v((edge + length, width), bf),
            v((width, 3 * width), bf),
            v((width, width), bf),
            v((width, 4 * rank), bf),
            v((columns, width), bf),
            v((2 * rank, width), bf),
            v((taps, width), bf),
            v((8, width), f32),
            v((edge + length, 3 * width), f32),
            v((edge + length, share), f32),
            v((4, length, width), bf),
            v((length, width), bf),
            v((length, width), f32),
            v((length, width), bf),
            v((edge + length, rank), bf),
            v((4, length, rank), bf),
        ],
        200,
        2 * length * width * 4 * width,
        50_000_000,
    )


def ready_kernel(place_ref, select, exits, rows_mine, rows_far, rows_x, rows_far_x, grad_out, back_out, grad_s, back_s, sems):
    share, rank = rows_mine.shape[2], select.shape[2]
    mover = Mover(sems)
    for t in range(2):
        for r, source in enumerate((rows_mine.at[t], rows_x.at[1 - t], rows_far.at[t], rows_far_x.at[1 - t])):
            at = pl.multiple_of(jnp.bitwise_xor(place_ref[0], r) * share, 128)
            mover.start(source, grad_s.at[t, :, pl.ds(at, share)])
    mover.wait()
    mover.start(grad_s, grad_out)
    for t in range(2):
        back_s[t] = low(product_t(grad_s[t], exits[pl.ds(rank, rank), :])) * select[t]
    mover.start(back_s, back_out)
    mover.wait()


def ready(place_ids, select, exits, cotangents):
    length, share = cotangents[0].shape[1:]
    rank, width = select.shape[2], 4 * share
    shapes = [(2, length, width), (2, length, rank)]
    return kernel_call(
        ready_kernel,
        "ready",
        [place_ids, select, exits, *cotangents],
        "svvaaaa",
        [shaped(v) for v in shapes],
        [pltpu.VMEM(v, jnp.bfloat16) for v in shapes],
        16,
        4 * length * width * rank,
        10_000_000,
    )


def lows_kernel(select, seen, entry, lows):
    rank = select.shape[1]
    inner = product(seen[...], entry[:, pl.ds(2 * rank, 2 * rank)])
    lows[0] = low(inner[:, :rank]) * select[...]
    lows[1] = low(inner[:, rank:]) * select[...]


def lows_of(select, seen, entry):
    length, rank = select.shape
    return pl.pallas_call(
        lows_kernel,
        out_shape=shaped((2, length, rank)),
        in_specs=[pl.BlockSpec(memory_space=pltpu.VMEM)] * 3,
        out_specs=pl.BlockSpec(memory_space=pltpu.VMEM),
        cost_estimate=pl.CostEstimate(flops=4 * length * rank * seen.shape[1], bytes_accessed=3_000_000, transcendentals=0),
        compiler_params=pltpu.CompilerParams(vmem_limit_bytes=16 * 1024 * 1024),
        name="lows",
    )(select, seen, entry)


FAR_FLIPS = (0, 2, 1, 3)


def feed_kernel(far, add_tokens, add_grads, settle, sizes, which, turn, *refs):
    refs = list(refs)

    def take(n):
        return [refs.pop(0) for _ in range(n)]

    (quarter_ref,) = take(1) if far else (None,)
    token_refs = take(4)
    weights = take(4 if far else 6)
    prior_refs = take(2 * add_tokens + add_grads)
    down_out, back_out, grads_out = take(3)
    seen, lows, grad, low_back, gate_w, up_w, down_w, act_s, gg_s, gu_s, down_s, back_s, grads_s, *prior, sems = refs
    low_gate, low_up = lows.at[0], lows.at[1]
    width, rank, units = seen.shape[1], low_back.shape[1], gate_w.shape[0]
    whole, side = pl.ds(0, width), pl.ds(width, rank)
    steps = []
    for size in sizes:
        steps.append((sum(n for _, n in steps), size))
    quarter_rows = units // 4
    mover = Mover(sems)
    token_refs[1] = token_refs[1].at[pl.ds(which, 2)]
    token_refs[2], token_refs[3] = token_refs[2].at[turn], token_refs[3].at[turn]
    token_loads = [mover.start(a, b) for a, b in zip(token_refs, (seen, lows, grad, low_back))]
    loads = []
    if far:
        for n, ref in enumerate(weights):
            rows = pl.ds(n * quarter_rows, quarter_rows)
            for i, dst in enumerate((gate_w, up_w, down_w)):
                loads.append((n * quarter_rows, mover.start(ref.at[i], dst.at[rows])))
    else:
        for at, n in steps:
            rows = pl.ds(at, n)
            for i, dst in enumerate((gate_w, up_w, down_w)):
                loads.append((at, mover.start(weights[2 * i].at[rows], dst.at[rows, whole])))
                loads.append((at, mover.start(weights[2 * i + 1].at[rows], dst.at[rows, side])))
    prior_loads = [mover.start(a, b) for a, b in zip(prior_refs, prior)]
    if add_tokens:
        down_prior, back_prior = prior[:2]
    if add_grads:
        grads_prior = prior[-1]
    mover.wait(token_loads)

    for at, n in steps:
        while loads and loads[0][0] < at + n:
            mover.wait([loads.pop(0)[1]])
        cols = pl.ds(at, n)
        gate = product_t(seen[...], gate_w[cols, whole]) + product_t(low_gate[...], gate_w[cols, side])
        up = product_t(seen[...], up_w[cols, whole]) + product_t(low_up[...], up_w[cols, side])
        ga = product_t(grad[...], down_w[cols, whole]) + product_t(low_back[...], down_w[cols, side])
        sigma = jax.nn.sigmoid(gate)
        swish = gate * sigma
        act_s[:, cols] = low(swish * up)
        gu_s[:, cols] = low(ga * swish)
        gg_s[:, cols] = low(ga * up * (sigma + swish * (1.0 - sigma)))

    mover.wait(prior_loads)
    for i, (left, right) in enumerate(((low_gate, gg_s), (low_up, gu_s), (low_back, act_s))):
        turned, lanes = left[...].T, pl.ds(i * rank, rank)

        def grad_tile(at, n):
            cols = pl.ds(at, n)
            total = product(turned, right[:, cols]).T
            if add_grads:
                total += grads_prior[cols, lanes]
            grads_s[cols, lanes] = total

        each_tile(units, units if units < 640 else 512, grad_tile)
    if settle:
        for n, flip in enumerate(FAR_FLIPS):
            at = jnp.bitwise_xor(quarter_ref[0], flip)
            mover.start(grads_s.at[pl.ds(n * quarter_rows, quarter_rows)], grads_out.at[at])
    else:
        mover.start(grads_s, grads_out)

    def back_tile(at, n):
        cols = pl.ds(at, n)
        total = product(gg_s[...], gate_w[:, cols]) + product(gu_s[...], up_w[:, cols])
        if add_tokens:
            total += wide_value(back_prior[:, cols])
        back_s[:, cols] = low(total)

    each_tile(width, 512, back_tile)
    for i, (left, right) in enumerate(((gg_s, gate_w), (gu_s, up_w))):
        total = product(left[...], right[:, side])
        cols = pl.ds(width + i * rank, rank)
        if add_tokens:
            total += wide_value(back_prior[:, cols])
        back_s[:, cols] = low(total)
    mover.start(back_s, back_out)

    def down_tile(at, n):
        cols = pl.ds(at, n)
        total = product(act_s[...], down_w[:, cols])
        if add_tokens:
            total += wide_value(down_prior[:, cols])
        down_s[:, cols] = low(total)

    each_tile(width + rank, 512, down_tile)
    mover.start(down_s, down_out)
    mover.wait()


def feed(tokens, which, turn, weights, quarter=None, add_tokens=None, add_grads=None, settle=False):
    far = quarter is not None
    length, width = tokens[0].shape
    rank = tokens[1].shape[2]
    units = 4 * weights[0].shape[1] if far else weights[0].shape[0]
    sizes = [n for _, n in spans(units, 512)]
    if len(sizes) > 1 and sizes[-1] < 256:
        sizes[-2:] = [256, sizes[-2] + sizes[-1] - 256]
    bf, f32, v = jnp.bfloat16, jnp.float32, pltpu.VMEM
    args = ([quarter] if far else []) + list(tokens) + list(weights)
    shapes = [((length, width + rank), bf), ((length, width + 2 * rank), bf), ((units, 3 * rank), f32)]
    prior = list(add_tokens or ()) + ([] if add_grads is None else [add_grads])
    prior_scratch = (shapes[:2] if add_tokens else []) + ([] if add_grads is None else shapes[2:])
    outs = [shaped(*pair) for pair in shapes]
    if settle:
        outs[2] = shaped((4, units // 4, 3 * rank), f32)
    return kernel_call(
        functools.partial(
            feed_kernel, far, add_tokens is not None, add_grads is not None, settle, tuple(sizes), which, turn
        ),
        "feed_far" if far else "feed_near",
        args + prior,
        ("s" if far else "") + "a" * (4 + len(weights) + len(prior)),
        outs,
        [v((length, width), bf), v((2, length, rank), bf), v((length, width), bf), v((length, rank), bf)]
        + [v((units, width + rank), bf)] * 3
        + [v((length, units), bf)] * 3
        + [v(*pair) for pair in shapes + prior_scratch],
        48,
        12 * length * units * (width + 2 * rank),
        30_000_000,
    )


def branch_kernel(plan, *refs):
    refs = list(refs)

    def take(n):
        return [refs.pop(0) for _ in range(n)]

    place_ref, came, mine, hidden, grad, two, gated, lows, select, gain_two, entry, exits, taps, prev, down_mine, down_next = take(16)
    kept, near, far_0, far_1, far_2, out_own = take(6)
    pieces = take(len(plan))
    grad_hidden_out, filtered_out, gates_out, edge_out, keep_out, give_out, sent_out, own_out = take(8)
    near_s, far_s, pack_s, part_s, out_s, kept_s, w_s, gb_s, lo_s, gf_s, gate_s, edge_s, wide_s, sems = refs
    length, width = hidden.shape
    share, rank = width // 4, select.shape[1]
    mover = Mover(sems)
    start_out(mover, [], out_own, pieces, plan, place_ref, out_s, share)
    mover.start(kept.at[1], kept_s.at[0])
    mover.start(kept.at[3], kept_s.at[1])
    loads = list(mover.pending)
    unit_loads = [mover.start(near, near_s)]
    quarter_rows, at = near.shape[0] // 4, 0
    for far in (far_0, far_1, far_2):
        n = far.shape[1]
        for q in range(4):
            unit_loads.append(mover.start(far.at[q], far_s.at[pl.ds(q * quarter_rows + at, n)]))
        at += n
    part_s[0] = low(hidden[...] + wide_value(down_mine[:, pl.ds(0, width)]))
    part_s[1] = down_next[:, pl.ds(0, width)]
    for t in range(2):
        for r in range(4):
            lanes = pl.ds(pl.multiple_of(jnp.bitwise_xor(place_ref[0], r) * share, 128), share)
            target = (own_out if r % 2 == 0 else sent_out).at[2 * t + r // 2]
            mover.start(part_s.at[t, :, lanes], target)
    side = pl.ds(width, 2 * rank)
    inner = wide_value(came[:, side]) + wide_value(mine[:, side])
    lo_s[0] = low(inner[:, :rank]) * select[...]
    lo_s[1] = low(inner[:, rank:]) * select[...]

    def combine(at, n):
        cols = pl.ds(at, n)
        total = wide_value(came[:, cols]) + wide_value(mine[:, cols])
        total += product_t(lo_s[0], entry[cols, pl.ds(2 * rank, rank)])
        total += product_t(lo_s[1], entry[cols, pl.ds(3 * rank, rank)])
        w_s[:, cols] = total * gain_two[:, cols]

    each_tile(width, width // 3, combine)

    def norm(at, n):
        rows = pl.ds(at, n)
        h, w = hidden[rows, :], w_s[rows, :]
        scale = lax.rsqrt(jnp.sum(h * h, 1, keepdims=True) / width + EPS)
        moment = jnp.sum(w * h, 1, keepdims=True) / width
        value = wide_value(grad[0, rows, :]) + scale * w - h * (scale * scale * scale * moment)
        w_s[rows, :] = value
        gb_s[rows, :] = low(value)

    each_tile(length, 32, norm)
    mover.start(w_s, grad_hidden_out)
    lo_s[2] = low(product_t(gb_s[...], exits[pl.ds(0, rank), :])) * select[...]
    mover.wait(loads)
    for r in range(4):
        cols = pl.ds(r * share, share)
        rows = pl.ds(pl.multiple_of(jnp.bitwise_xor(place_ref[0], r) * share, 128), share)
        gg = product_t(gb_s[...], out_s[cols, :]) + product_t(lo_s[2], entry[rows, pl.ds(rank, rank)])
        gf = gg * wide_value(kept_s[0, :, cols])
        gf_s[:, cols] = low(gf)
        first = gf[:8]
        beside = taps[pl.ds(1, 1), cols] * (prev[pl.ds(0, 8), pl.ds(0, 1)] * first)
        beyond = taps[pl.ds(0, 1), cols] * (prev[pl.ds(0, 8), pl.ds(1, 1)] * first)
        edge_s[pl.ds(0, 1), cols] = beyond[0:1]
        edge_s[pl.ds(1, 1), cols] = beside[0:1] + beyond[1:2]
        edge_s[pl.ds(2, 6), cols] = jnp.zeros((6, share), jnp.float32)
        gate_s[:, cols] = low(gg * wide_value(kept_s[1, :, cols]))
    mover.start(gf_s, filtered_out)
    mover.start(gate_s, gates_out)
    mover.start(edge_s, edge_out)
    for i, (left, right) in enumerate(((lo_s.at[0], two), (lo_s.at[1], two), (lows.at[1], gb_s))):
        turned = left[...].T

        def wide_tile(at, n):
            cols = pl.ds(at, n)
            wide_s[i, :, cols] = low(product(turned, right[:, cols]))

        each_tile(width, width // 3, wide_tile)
    turned = lo_s[2].T
    for r in range(4):
        lanes = pl.ds(pl.multiple_of(jnp.bitwise_xor(place_ref[0], r) * share, 128), share)
        wide_s[3, :, lanes] = low(product(turned, gated[:, pl.ds(r * share, share)]))
    mover.wait(unit_loads)
    half = near.shape[0] // 2
    for h, out in ((0, keep_out), (1, give_out)):
        mine = jnp.bitwise_xor(place_ref[1], h)
        rows = pl.ds(pl.multiple_of(mine * half, 16), half)
        at = 0
        for r, units in ((0, near_s), (2, far_s), (1, None), (3, None)):
            lanes = pl.ds(pl.multiple_of(jnp.bitwise_xor(place_ref[0], r) * share, 128), share)
            for j in range(2):
                pack_s[h, pl.ds(at + j * rank, rank), :] = wide_s[mine * 2 + j, :, lanes]
            at += 2 * rank
            if units is not None:
                pack_s[h, pl.ds(at, half), :] = low(units[rows, :])
                at += half
        mover.start(pack_s.at[h], out)
    mover.wait()


def branch_back(place_ids, small, kept, units, own, pieces):
    length, width = small[2].shape
    share, rank, unit_rows = width // 4, small[7].shape[1], units[0].shape[0]
    bf, f32, v = jnp.bfloat16, jnp.float32, pltpu.VMEM
    return kernel_call(
        functools.partial(branch_kernel, [p[1:] for p in pieces]),
        "branch_back",
        [place_ids, *small, kept, *units, own, *[p[0] for p in pieces]],
        "s" + "v" * len(small) + "a" * (2 + len(units) + len(pieces)),
        [
            shaped((length, width), f32),
            shaped((length, width)),
            shaped((length, width)),
            shaped((8, width), f32),
            shaped((unit_rows + 8 * rank, share)),
            shaped((unit_rows + 8 * rank, share)),
            shaped((4, length, share)),
            shaped((4, length, share)),
        ],
        [
            v((unit_rows, share), f32),
            v((unit_rows, share), f32),
            v((2, unit_rows + 8 * rank, share), bf),
            v((2, length, width), bf),
            v((width, width), bf),
            v((2, length, width), bf),
            v((length, width), f32),
            v((length, width), bf),
            v((3, length, rank), bf),
            v((length, width), bf),
            v((length, width), bf),
            v((8, width), f32),
            v((4, rank, width), bf),
        ],
        80,
        2 * length * width * width + 8 * length * rank * width,
        40_000_000,
    )


def input_kernel(plan, *refs):
    refs = list(refs)

    def take(n):
        return [refs.pop(0) for _ in range(n)]

    place_ref, filtered, gates, tail, taps, prev, grad_hidden, tokens, normed, lows, select, gain_one, entry, column, low_down, grad_down = take(16)
    kept, in_own = take(2)
    pieces = take(len(plan))
    grad_out, keep_out, give_out = take(3)
    in_s, kept_s, near_s, far_s, gp_s, w_s, gi_s, lo_s, wide_s, entry_s, down_s, block_s, pack_s, sems = refs
    length, width = filtered.shape
    share, rank = width // 4, select.shape[1]
    mover = Mover(sems)
    first = [mover.start(kept.at[0], kept_s.at[0]), mover.start(kept.at[2], kept_s.at[1])]
    loads = []
    start_in(mover, loads, in_own, pieces, plan, place_ref, in_s, width, share)
    mover.wait(first)
    for r in range(4):
        lanes = pl.ds(r * share, share)
        tap = [taps[pl.ds(i, 1), lanes] for i in range(3)]
        for at, n in spans(length, 128):
            rows = pl.ds(at, n)
            value = wide_value(filtered[rows, lanes])
            near_s[rows, :] = tap[1] * (prev[rows, pl.ds(0, 1)] * value)
            far_s[rows, :] = tap[0] * (prev[rows, pl.ds(1, 1)] * value)
        near_s[pl.ds(length, 8), :] = jnp.zeros((8, share), jnp.float32)
        far_s[pl.ds(length, 8), :] = tail[:, lanes]
        for at, n in spans(length, 128):
            rows = pl.ds(at, n)
            mixed = tap[2] * wide_value(filtered[rows, lanes]) + near_s[pl.ds(at + 1, n), :] + far_s[pl.ds(at + 2, n), :]
            gp_s[rows, pl.ds(r * share, share)] = low(mixed * wide_value(kept_s[1, rows, lanes]))
            gp_s[rows, pl.ds(2 * width + r * share, share)] = low(mixed * wide_value(kept_s[0, rows, lanes]))
    gp_s[:, pl.ds(width, width)] = gates[...]
    inner = 0.0
    for i in range(3):
        inner = inner + product_t(gp_s[:, pl.ds(i * width, width)], column[pl.ds(i * rank, rank), :])
    lo_s[...] = low(inner) * select[...]
    turned = lows[0].T
    turned_back = lo_s[...].T

    def exit_tile(at, n):
        cols = pl.ds(at, n)
        wide_s[:, cols] = low(product(turned, gp_s[:, cols]))

    each_tile(3 * width, width // 3, exit_tile)

    def entry_tile(at, n):
        cols = pl.ds(at, n)
        entry_s[:, cols] = low(product(turned_back, normed[:, cols]))

    each_tile(width, width // 3, entry_tile)
    turned_down = low_down[0].T

    def down_tile(at, n):
        cols = pl.ds(at, n)
        down_s[:, cols] = low(product(turned_down, grad_down[0, :, cols]))

    each_tile(width, width // 3, down_tile)
    half = 5 * rank // 2
    for r in range(4):
        lanes = pl.ds(pl.multiple_of(jnp.bitwise_xor(place_ref[0], r) * share, 128), share)
        block_s[pl.ds(0, rank), :] = entry_s[:, lanes]
        for i in range(3):
            block_s[pl.ds((1 + i) * rank, rank), :] = wide_s[:, pl.ds(i * width + r * share, share)]
        block_s[pl.ds(4 * rank, rank), :] = down_s[:, lanes]
        for h in range(2):
            rows = pl.ds(pl.multiple_of(jnp.bitwise_xor(place_ref[1], h) * half, 16), half)
            pack_s[h, pl.ds(r * half, half), :] = block_s[rows, :]
    mover.start(pack_s.at[0], keep_out)
    mover.start(pack_s.at[1], give_out)
    mover.wait(loads)

    def back(at, n):
        cols = pl.ds(at, n)
        total = product_t(gp_s[...], in_s[cols, :]) + product_t(lo_s[...], entry[cols, pl.ds(0, rank)])
        w_s[:, cols] = total * gain_one[:, cols]

    each_tile(width, width // 3, back)

    def norm(at, n):
        rows = pl.ds(at, n)
        x, w = wide_value(tokens[rows, :]), w_s[rows, :]
        scale = lax.rsqrt(jnp.sum(x * x, 1, keepdims=True) / width + EPS)
        moment = jnp.sum(w * x, 1, keepdims=True) / width
        gi_s[rows, :] = low(grad_hidden[rows, :] + scale * w - x * (scale * scale * scale * moment))

    each_tile(length, 32, norm)
    for r in range(4):
        at = pl.multiple_of(jnp.bitwise_xor(place_ref[0], r) * share, 128)
        mover.start(gi_s.at[:, pl.ds(at, share)], grad_out.at[r])
    mover.wait()


def input_back(place_ids, small, kept, own, pieces):
    length, width = small[0].shape
    share, rank = width // 4, small[9].shape[1]
    bf, f32, v = jnp.bfloat16, jnp.float32, pltpu.VMEM
    return kernel_call(
        functools.partial(input_kernel, [p[1:] for p in pieces]),
        "input_back",
        [place_ids, *small, kept, own, *[p[0] for p in pieces]],
        "s" + "v" * len(small) + "a" * (2 + len(pieces)),
        [shaped((4, length, share)), shaped((10 * rank, share)), shaped((10 * rank, share))],
        [
            v((width, 3 * width), bf),
            v((2, length, width), bf),
            v((length + 8, share), f32),
            v((length + 8, share), f32),
            v((length, 3 * width), bf),
            v((length, width), f32),
            v((length, width), bf),
            v((length, rank), bf),
            v((rank, 3 * width), bf),
            v((rank, width), bf),
            v((rank, width), bf),
            v((5 * rank, share), bf),
            v((2, 10 * rank, share), bf),
        ],
        64,
        6 * length * width * width,
        40_000_000,
    )


def results_kernel(place_ref, own, came, low_down, exits, kept_out, sent_out, out_s, sems):
    share, rank = own.shape[2], low_down.shape[2]
    mover = Mover(sems)
    for i, out in ((0, kept_out), (1, sent_out)):
        lanes = pl.ds(pl.multiple_of(jnp.bitwise_xor(place_ref[0], 2 * i) * share, 128), share)
        for t in range(2):
            total = wide_value(own[2 * t + i]) + wide_value(came[2 * (1 - t) + i])
            out_s[2 * i + t] = low(total + product(low_down[t], exits[pl.ds(rank, rank), lanes]))
            mover.start(out_s.at[2 * i + t], out.at[jnp.bitwise_xor(place_ref[3], t)])
    mover.wait()


def results_of(place_ids, own, came, low_down, exits):
    count, length, share = own.shape
    return kernel_call(
        results_kernel,
        "results",
        [place_ids, own, came, low_down, exits],
        "svvvv",
        [shaped((2, length, share))] * 2,
        [pltpu.VMEM((count, length, share), jnp.bfloat16)],
        8,
        8 * length * share * low_down.shape[2],
        8_000_000,
    )


def finish_kernel(place_ref, one_own, one_other, two_own, two_other, *refs):
    in_entry, in_exit, out_entry, out_exit, gate_entry, gate_exit, up_entry, up_exit, down_entry, down_exit = refs[:10]
    one_s, two_s, sems = refs[10:]
    rank = in_entry.shape[1]
    mover = Mover(sems)
    for h, one, two in ((0, one_own, two_own), (1, one_other, two_other)):
        at = jnp.bitwise_xor(place_ref[1], h)
        mover.start(one, one_s.at[at])
        mover.start(two, two_s.at[at])
    mover.wait()
    first, second = pl.ds(0, rank), pl.ds(rank, rank)
    gate_entry[...] = wide_value(one_s[0, first, :]).T
    up_entry[...] = wide_value(one_s[0, second, :]).T
    out_exit[...] = wide_value(one_s[1, first, :])
    out_entry[...] = wide_value(one_s[1, second, :]).T
    half = gate_exit.shape[0] // 2
    for h in range(2):
        rows = pl.ds(h * half, half)
        for i, out in enumerate((gate_exit, up_exit, down_entry)):
            out[rows, :] = wide_value(one_s[h, pl.ds(2 * rank, half), pl.ds(i * rank, rank)])
    cut = rank // 2
    in_entry[...] = wide_value(two_s[0, first, :]).T
    in_exit[0] = wide_value(two_s[0, second, :])
    in_exit[1, pl.ds(0, cut), :] = wide_value(two_s[0, pl.ds(2 * rank, cut), :])
    in_exit[1, pl.ds(cut, cut), :] = wide_value(two_s[1, pl.ds(0, cut), :])
    in_exit[2] = wide_value(two_s[1, pl.ds(cut, rank), :])
    down_exit[...] = wide_value(two_s[1, pl.ds(cut + rank, rank), :])


def finish(place_ids, one_own, one_other, two_own, two_other, units, rank):
    share, f32, bf = one_own.shape[1], jnp.float32, jnp.bfloat16
    entry, exits, unit = (share, rank), (rank, share), (units, rank)
    shapes = [entry, (3, rank, share), entry, exits, entry, unit, entry, unit, unit, exits]
    return kernel_call(
        finish_kernel,
        "finish",
        [place_ids, one_own, one_other, two_own, two_other],
        "saaaa",
        [shaped(v, f32) for v in shapes],
        [pltpu.VMEM((2, *one_own.shape), bf), pltpu.VMEM((2, *two_own.shape), bf)],
        4,
        0,
        8_000_000,
        pltpu.VMEM,
    )


def swap(value, axis, bit):
    return lax.ppermute(value, axis, [(i, i ^ bit) for i in range(lax.axis_size(axis))])


def after(value, *others):
    return lax.optimization_barrier((value, others))[0]


def together(*values):
    return lax.optimization_barrier(values)


def place(relative, me):
    stacked = jnp.stack(relative)
    return [lax.dynamic_index_in_dim(stacked, a ^ me, 0, keepdims=False) for a in range(len(relative))]


def part_of(block, dim, index, count):
    rows = block.shape[dim] // count
    return lax.dynamic_slice_in_dim(block, index * rows, rows, dim)


def seq_step(value, bit):
    return low(wide_value(value) + wide_value(swap(value, "seq", bit)))


def seq_bits():
    return [2**k for k in range(1, 16) if 2**k < lax.axis_size("seq")]


def seq_total(value):
    for bit in seq_bits():
        value = seq_step(value, bit)
    return value


def seq_total_parts(value, *firsts):
    s = lax.axis_index("seq")
    for bit, first in zip(seq_bits(), firsts + (None,) * len(seq_bits())):
        keep = s // bit % 2
        other = swap(part_of(value, 0, 1 - keep, 2), "seq", bit)
        if first is not None:
            other = after(other, first)
        value = low(wide_value(part_of(value, 0, keep, 2)) + wide_value(other))
    for bit in seq_bits()[::-1]:
        value = jnp.concatenate(place([value, swap(value, "seq", bit)], s // bit % 2), 0)
    return value


def chip_half(value, dim, core):
    other = swap(low(part_of(value, dim, 1 - core, 2)), "seq", 1)
    return low(wide_value(part_of(value, dim, core, 2)) + wide_value(other))


def own_block(chip):
    total = wide_value(chip[0])
    for r in (3, 1, 2):
        total = total + wide_value(swap(chip[r], "mp", r))
    return low(total)


def both_halves(own, core):
    return wide_value(jnp.concatenate(place([own, swap(own, "seq", 1)], core), 0))


def fast_local(
    inputs,
    cotangent,
    mixer_gain,
    in_weight,
    in_entry,
    in_exit,
    conv_weight,
    out_weight,
    out_entry,
    out_exit,
    ffn_gain,
    gate_weight,
    gate_entry,
    gate_exit,
    up_weight,
    up_entry,
    up_exit,
    down_weight,
    down_entry,
    down_exit,
    doc_starts,
    adapter_ids,
):
    seqs, length, share = inputs.shape
    width = 4 * share
    rank = in_entry.shape[1]
    units = gate_weight.shape[1]
    m = lax.axis_index("mp")
    s = lax.axis_index("seq")
    x, y, core, quarter = m % 2, m // 2, s % 2, s % 4
    place_ids = jnp.stack([m, core, quarter, x]).astype(jnp.int32)
    halo = 16

    def block_for(stack, r):
        return lax.dynamic_index_in_dim(stack, m ^ r, 0, keepdims=False)

    in_slabs = in_weight.swapaxes(0, 1)
    own_taps = jnp.pad(conv_weight, ((0, TAP_ROWS - 3), (0, 0)))
    entries = (in_entry, out_entry, gate_entry, up_entry)
    sides = (in_exit.swapaxes(0, 1), out_exit, down_exit)
    in_quarter = pack_in(place_ids, in_slabs)
    far_pack, beside, below, own_block_rows, ct_rows, ct_far = pack_first(
        after(place_ids, in_quarter), inputs, cotangent, in_slabs, out_weight, entries, sides, own_taps
    )
    near = [gate_weight.T, gate_exit.T, up_weight.T, up_exit.T, down_weight, down_entry]
    count = units // 4 // 16
    rows = (-(-count * 10 // 27) * 16, count * 9 // 27 * 16)
    cuts = ((0, rows[0]), (rows[0], rows[1]), (rows[0] + rows[1], units // 4 - rows[0] - rows[1]))

    def spread(got, over, r, base):
        return [
            (got, r, "quarter", 0, base),
            (swap(got, "seq", 1), r, "quarter", 1, base),
            (over, r, "quarter", 2, base),
            (swap(over, "seq", 1), r, "quarter", 3, base),
        ]

    in_x, in_y = swap(in_quarter, "mp", 1), swap(in_quarter, "mp", 2)
    far_pack = swap(after(far_pack, in_x, in_y), "mp", 3)
    over_x, over_y = swap(in_x, "seq", 2), swap(in_y, "seq", 2)
    packed = pack_second(after(place_ids, in_x, in_y), near, cuts)
    beside, below = after((beside, below), in_x, in_y)
    beside, below = swap(beside, "mp", 1), swap(below, "mp", 2)
    in_pieces = spread(in_x, over_x, 1, 0) + spread(in_y, over_y, 2, 0)
    far_count = far_pack.shape[0] - length
    far_weights = far_pack[:far_count]
    over_far = swap(after(far_weights, [p[0] for p in in_pieces], packed), "seq", 2)
    row_blocks = [own_block_rows, beside, below, far_pack]
    ends = [length, length, length, far_pack.shape[0]]
    head = from_behind(jnp.stack([b[e - halo : e] for b, e in zip(row_blocks, ends)]), "seq", 1)
    far_pieces = spread(far_weights, over_far, 3, 3 * width // 4)
    in_pieces += [p[:4] + (0,) for p in far_pieces]
    rest_pieces = list(far_pieces)
    for got, r in ((beside, 1), (below, 2)):
        rest_pieces += [(got, r, "half", 0, length), (swap(got, "seq", 1), r, "half", 1, length)]
    ct_rows, ct_far, *packed = after((ct_rows, ct_far, *packed), [p[0] for p in rest_pieces])
    ct_x, ct_y, ct_g = swap(ct_rows, "mp", 1), swap(ct_far, "mp", 2), swap(ct_far, "mp", 3)
    packed = [packed[0], *after(tuple(packed[1:]), ct_x)]
    far_first = [swap(p, "mp", 2) for p in packed]

    starts = jnp.stack([doc_starts[m], doc_starts[m ^ 1]])[:, None, :]
    ids = jnp.stack([adapter_ids[m], adapter_ids[m ^ 1]])
    steps = (ids - jnp.pad(ids, ((0, 0), (1, 0)))[:, :-1])[:, None, :]
    position = (s * length - halo + jnp.arange(halo + length, dtype=jnp.int32))[None, :, None]
    adapter = jnp.sum(jnp.where(starts <= position, steps, 0), 2)
    lane = jnp.arange(rank, dtype=jnp.int32) // RANK
    select_ext = (adapter[:, :, None] == lane).astype(jnp.bfloat16)
    select = select_ext[:, halo:]
    begins = jnp.any(starts[0] == position[0], 1).astype(jnp.float32)
    prev_one = 1.0 - begins[halo:]
    prev_two = prev_one * (1.0 - begins[halo - 1 : halo - 1 + length])
    prev = jnp.stack([prev_one, prev_two], 1)
    gain_one = wide_value(mixer_gain)[None]
    gain_two = wide_value(ffn_gain)[None]

    kept, gated, tokens, normed, hidden, normed_two, lows, entry_full, column_full, exit_full, taps = mixer(
        place_ids,
        (select_ext[0], prev, gain_one, gain_two),
        (head, in_slabs, out_weight, *entries, *sides, own_taps),
        row_blocks,
        in_pieces,
        rest_pieces,
    )
    normed_next = swap(normed_two, "mp", 1)
    grad_down, back_lows = ready(place_ids, select, exit_full, (ct_rows, ct_y, ct_x, ct_g))
    lows_next = lows_of(select[1], normed_next, entry_full)
    mine = (normed_two, lows, grad_down, back_lows), 2, 0
    other = (normed_next, lows_next, grad_down, back_lows), 0, 1
    at_quarter = jnp.full((1,), quarter, jnp.int32)

    def spread_far(first, then, last):
        over = swap(after(first, then), "seq", 2)
        return [first, over, swap(after(first, last), "seq", 1), swap(after(over, last), "seq", 1)]

    near_mine = feed(*mine, near)
    near_next = feed(*other, near, add_grads=near_mine[2])
    far_zero = spread_far(far_first[0], near_mine[2], near_next[2])
    next_zero = feed(*other, far_zero, at_quarter, add_tokens=near_next[:2])
    mine_zero = feed(*mine, far_zero, at_quarter, add_tokens=near_mine[:2], add_grads=next_zero[2], settle=True)
    far_one = spread_far(far_first[1], near_mine[2], next_zero[2])
    next_one = feed(*other, far_one, at_quarter, add_tokens=next_zero[:2])
    far_two = spread_far(far_first[2], next_zero[2], next_one[2])
    down_next, back_next, next_grads = feed(*other, far_two, at_quarter, add_tokens=next_one[:2])
    got_back = swap(back_next, "mp", 1)
    mine_one = feed(*mine, far_one, at_quarter, add_tokens=mine_zero[:2], add_grads=next_one[2], settle=True)
    down_mine, back_mine, mine_grads = feed(
        *mine, far_two, at_quarter, add_tokens=mine_one[:2], add_grads=next_grads, settle=True
    )

    grad_hidden, grad_filtered, grad_gates, edge, one_keep, one_give, sent, own_parts = branch_back(
        place_ids,
        (got_back, back_mine, hidden, grad_down, normed_two, gated, lows, select[0], gain_two, entry_full, exit_full, taps, prev, down_mine, down_next),
        kept,
        (near_next[2], mine_zero[2], mine_one[2], mine_grads),
        out_weight,
        rest_pieces,
    )
    came_edge = from_behind(edge, "seq", -1)
    came = swap(sent, "mp", 1)
    inner = after(jnp.stack([down_mine[:, width:], down_next[:, width:]]), got_back)
    inner_got = swap(inner, "mp", 1)
    low_down = low(wide_value(inner) + wide_value(inner_got[::-1])) * select

    def chip_sum(keep, give):
        return low(wide_value(keep) + wide_value(swap(give, "seq", 1)))

    one = chip_sum(one_keep, one_give)
    head_rows, unit_rows = 2 * rank, units // 2
    cut = head_rows + unit_rows
    one_x = swap(one[2 * cut : 2 * cut + head_rows], "mp", 1)
    one_y = swap(one[cut : 2 * cut], "mp", 2)
    one_g = swap(one[2 * cut + head_rows :], "mp", 3)
    grad_blocks, two_keep, two_give = input_back(
        place_ids,
        (grad_filtered, grad_gates, came_edge, taps, prev, grad_hidden, tokens, normed, lows, select[0], gain_one, entry_full, column_full, low_down, grad_down),
        kept,
        in_slabs,
        in_pieces,
    )
    one_x, one_y, one_g, came = after((one_x, one_y, one_g, came), grad_blocks)
    one_own = wide_value(one[:cut]) + wide_value(one_y)
    one_own = one_own.at[:head_rows].add(wide_value(one_x) + wide_value(one_g))
    one_own = low(one_own)
    kept_rows, sent_rows = results_of(place_ids, after(own_parts, one_own), came, low_down, exit_full)
    two_keep, two_give = after((two_keep, two_give), sent_rows)
    two = chip_sum(two_keep, two_give).reshape(4, 5 * rank // 2, share)
    two_own = own_block(two)
    grad_rows = [grad_blocks[0]] + [swap(after(grad_blocks[r], two_own), "mp", r) for r in (1, 2, 3)]
    grad_inputs = wide_value(jnp.stack(place(grad_rows, m)))
    one_own, two_own = seq_total_parts(one_own, two, two_own), seq_total(two_own)
    grads = finish(place_ids, one_own, swap(one_own, "seq", 1), two_own, swap(two_own, "seq", 1), units, rank)

    output = jnp.concatenate(place([kept_rows, swap(sent_rows, "mp", 2)], y), 0)
    in_entry_grad, in_exit_grad, out_entry_grad, out_exit_grad, gate_entry_grad, gate_exit_grad = grads[:6]
    up_entry_grad, up_exit_grad, down_entry_grad, down_exit_grad = grads[6:]
    return (
        output,
        grad_inputs,
        in_entry_grad,
        in_exit_grad.swapaxes(0, 1),
        out_entry_grad,
        out_exit_grad,
        gate_entry_grad,
        gate_exit_grad.T,
        up_entry_grad,
        up_exit_grad.T,
        down_entry_grad,
        down_exit_grad,
    )


def solution(mesh):
    fast = mesh.shape["mp"] == 4 and mesh.shape["seq"] % 4 == 0
    return jax.shard_map(
        fast_local if fast else general_local,
        mesh=mesh,
        in_specs=(
            P(None, "seq", "mp"),
            P(None, "seq", "mp"),
            P(),
            P(None, None, "mp"),
            P("mp", None),
            P(None, None, "mp"),
            P(None, "mp"),
            P("mp", None),
            P("mp", None),
            P(None, "mp"),
            P(),
            P(None, "mp"),
            P("mp", None),
            P(None, "mp"),
            P(None, "mp"),
            P("mp", None),
            P(None, "mp"),
            P("mp", None),
            P("mp", None),
            P(None, "mp"),
            P(),
            P(),
        ),
        out_specs=(
            P(None, "seq", "mp"),
            P(None, "seq", "mp"),
            P("mp", None),
            P(None, None, "mp"),
            P("mp", None),
            P(None, "mp"),
            P("mp", None),
            P(None, "mp"),
            P("mp", None),
            P(None, "mp"),
            P("mp", None),
            P(None, "mp"),
        ),
        check_vma=False,
    )
```

```python
import functools

import jax
import jax.numpy as jnp
from jax import lax
from jax.experimental import pallas as pl
from jax.experimental.pallas import tpu as pltpu
from jax.sharding import PartitionSpec as P

RANK = 16
ADAPT = 8
NDOC = 8


EPS = 1e-05


def from_behind(x, axis, by):
    count = lax.axis_size(axis)
    pairs = [(i, i + by) for i in range(count) if 0 <= i + by < count]
    return lax.ppermute(x, axis, pairs)


def contract(left, right, left_dim, right_extent):
    return lax.dot_general(
        left, right, (((left_dim,), (right_extent,)), ((), ())), preferred_element_type=jnp.float32
    )


def row_total(values):
    return lax.psum(jnp.sum(values, axis=-1), "mp")


def mid_total(parts):
    return lax.psum(parts, "mp")


def share_total(partial_value):
    return lax.psum_scatter(partial_value, "mp", scatter_dimension=1, tiled=True)


def column_products(share, weights):
    piece = lax.all_gather(share, "mp", axis=1, tiled=True)
    return tuple((jnp.dot(piece, weight, preferred_element_type=jnp.float32) for weight in weights))


def row_products(share, weight):
    return contract(lax.all_gather(share, "mp", axis=1, tiled=True), weight, 1, 1)


def doc_tables(starts, ids, length, offset):
    position = offset + jnp.arange(length, dtype=jnp.int32)
    begins = jnp.any(starts[:, :, None] == position[None, None, :], axis=1).astype(jnp.float32)
    earlier = jnp.any(starts[:, :, None] == position[None, None, :] - 1, axis=1).astype(jnp.float32)
    prev_one = 1.0 - begins
    prev_two = prev_one * (1.0 - earlier)
    segment = jnp.sum((starts[:, :, None] <= position[None, None, :]).astype(jnp.int32), axis=1) - 1
    document_onehot = (
        segment[:, :, None] == jnp.arange(NDOC, dtype=jnp.int32)[None, None, :]
    ).astype(jnp.float32)
    adapter_onehot = (ids[:, :, None] == jnp.arange(ADAPT, dtype=jnp.int32)[None, None, :]).astype(
        jnp.float32
    )
    token_onehot = jnp.einsum("cxn,cnt->cxt", document_onehot, adapter_onehot)
    select = jnp.repeat(token_onehot, RANK, axis=2).reshape(-1, ADAPT * RANK)
    return (prev_one, prev_two, select.astype(jnp.bfloat16))


def general_local(
    inputs,
    cotangent,
    mixer_gain,
    in_weight,
    in_entry,
    in_exit,
    conv_weight,
    out_weight,
    out_entry,
    out_exit,
    ffn_gain,
    gate_weight,
    gate_entry,
    gate_exit,
    up_weight,
    up_entry,
    up_exit,
    down_weight,
    down_entry,
    down_exit,
    doc_starts,
    adapter_ids,
):
    seq_count, length, width_share = inputs.shape
    tokens = seq_count * length
    width = width_share * lax.axis_size("mp")
    column = lax.axis_index("mp") * width_share
    prev_one, prev_two, select = doc_tables(
        doc_starts, adapter_ids, length, lax.axis_index("seq") * length
    )
    mixer_share = lax.dynamic_slice_in_dim(mixer_gain, column, width_share, 0).astype(jnp.float32)
    ffn_full = ffn_gain.astype(jnp.float32)
    ffn_share = lax.dynamic_slice_in_dim(ffn_full, column, width_share, 0)
    residual = inputs.reshape(tokens, width_share).astype(jnp.float32)
    scale_one = lax.rsqrt(row_total(residual * residual) / width + EPS)
    normed = (residual * scale_one[:, None] * mixer_share).astype(jnp.bfloat16)
    in_flat = in_weight.reshape(width, 3 * width_share)
    exit_flat = in_exit.reshape(in_exit.shape[0], 3 * width_share)
    inner_in = mid_total((jnp.dot(normed, in_entry, preferred_element_type=jnp.float32),))[0]
    low_in = inner_in.astype(jnp.bfloat16) * select
    project = column_products(normed, (in_flat,))[0] + jnp.dot(
        low_in, exit_flat, preferred_element_type=jnp.float32
    )
    parts = project.reshape(seq_count, length, 3, width_share)
    input_gate = parts[:, :, 0]
    output_gate = parts[:, :, 1]
    values = parts[:, :, 2]
    mixed = input_gate * values
    edge = from_behind(mixed[:, length - 2 :], "seq", 1)
    extended = jnp.concatenate([edge, mixed], 1)
    taps = conv_weight.astype(jnp.float32)
    filtered = (
        taps[2] * mixed
        + taps[1] * prev_one[..., None] * extended[:, 1 : length + 1]
        + taps[0] * prev_two[..., None] * extended[:, :length]
    )
    gated = (output_gate * filtered).astype(jnp.bfloat16).reshape(tokens, width_share)
    inner_out = mid_total((jnp.dot(gated, out_entry, preferred_element_type=jnp.float32),))[0]
    low_out = inner_out.astype(jnp.bfloat16) * select
    branch_tail = jnp.dot(low_out, out_exit, preferred_element_type=jnp.float32)
    partial_value = jnp.dot(gated, out_weight, preferred_element_type=jnp.float32)
    own = lax.dynamic_slice_in_dim(partial_value, column, width_share, 1) + residual + branch_tail
    rows_total = lax.psum(lax.dynamic_update_slice_in_dim(partial_value, own, column, 1), "mp")
    hidden = lax.dynamic_slice_in_dim(rows_total, column, width_share, 1)
    scale_two = lax.rsqrt(jnp.sum(rows_total * rows_total, axis=1) / width + EPS)
    normed_full = (rows_total * scale_two[:, None] * ffn_full).astype(jnp.bfloat16)
    normed_two = lax.dynamic_slice_in_dim(normed_full, column, width_share, 1)
    gate = jnp.dot(normed_full, gate_weight, preferred_element_type=jnp.float32)
    up = jnp.dot(normed_full, up_weight, preferred_element_type=jnp.float32)
    inner_gate, inner_up = mid_total(
        (
            jnp.dot(normed_two, gate_entry, preferred_element_type=jnp.float32),
            jnp.dot(normed_two, up_entry, preferred_element_type=jnp.float32),
        )
    )
    low_gate = inner_gate.astype(jnp.bfloat16) * select
    low_up = inner_up.astype(jnp.bfloat16) * select
    gate = gate + jnp.dot(low_gate, gate_exit, preferred_element_type=jnp.float32)
    up = up + jnp.dot(low_up, up_exit, preferred_element_type=jnp.float32)
    sigma = jax.nn.sigmoid(gate)
    swish = gate * sigma
    activated = (swish * up).astype(jnp.bfloat16)
    inner_down = mid_total((jnp.dot(activated, down_entry, preferred_element_type=jnp.float32),))[0]
    low_down = inner_down.astype(jnp.bfloat16) * select
    outcome = (
        hidden
        + share_total(jnp.dot(activated, down_weight, preferred_element_type=jnp.float32))
        + jnp.dot(low_down, down_exit, preferred_element_type=jnp.float32)
    )
    output = outcome.astype(jnp.bfloat16).reshape(seq_count, length, width_share)
    grad_hidden = cotangent.reshape(tokens, width_share).astype(jnp.float32)
    grad_down = grad_hidden.astype(jnp.bfloat16)
    grad_act = row_products(grad_down, down_weight)
    back_down = mid_total((contract(grad_down, down_exit, 1, 1),))[0]
    low_back_down = back_down.astype(jnp.bfloat16) * select
    grad_act = grad_act + contract(low_back_down, down_entry, 1, 1)
    down_entry_grad = contract(activated, low_back_down, 0, 0)
    down_exit_grad = contract(low_down, grad_down, 0, 0)
    up_projection_gradient = (grad_act * swish).astype(jnp.bfloat16)
    grad_gate = (grad_act * up * sigma * (1.0 + gate * (1.0 - sigma))).astype(jnp.bfloat16)
    back_gate, back_up = mid_total(
        (contract(grad_gate, gate_exit, 1, 1), contract(up_projection_gradient, up_exit, 1, 1))
    )
    low_back_gate = back_gate.astype(jnp.bfloat16) * select
    low_back_up = back_up.astype(jnp.bfloat16) * select
    grad_normed_two = share_total(
        contract(grad_gate, gate_weight, 1, 1) + contract(up_projection_gradient, up_weight, 1, 1)
    )
    grad_normed_two = (
        grad_normed_two
        + contract(low_back_gate, gate_entry, 1, 1)
        + contract(low_back_up, up_entry, 1, 1)
    )
    gate_entry_grad = contract(normed_two, low_back_gate, 0, 0)
    gate_exit_grad = contract(low_gate, grad_gate, 0, 0)
    up_entry_gradient = contract(normed_two, low_back_up, 0, 0)
    up_exit_grad = contract(low_up, up_projection_gradient, 0, 0)
    weighted_two = grad_normed_two * ffn_share
    cube_two = scale_two * scale_two * scale_two
    grad_hidden = (
        grad_hidden
        + scale_two[:, None] * weighted_two
        - hidden * (cube_two * row_total(weighted_two * hidden) / width)[:, None]
    )
    grad_branch = grad_hidden.astype(jnp.bfloat16)
    grad_gated = row_products(grad_branch, out_weight)
    back_out = mid_total((contract(grad_branch, out_exit, 1, 1),))[0]
    low_back_out = back_out.astype(jnp.bfloat16) * select
    grad_gated = grad_gated + contract(low_back_out, out_entry, 1, 1)
    out_entry_grad = contract(gated, low_back_out, 0, 0)
    out_exit_grad = contract(low_out, grad_branch, 0, 0)
    grad_gated = grad_gated.reshape(seq_count, length, width_share)
    grad_output_gate = grad_gated * filtered
    grad_filtered = grad_gated * output_gate
    near = taps[1] * prev_one[..., None] * grad_filtered
    far = taps[0] * prev_two[..., None] * grad_filtered
    sent = jnp.concatenate([far[:, :1], near[:, :1] + far[:, 1:2]], 1)
    came = from_behind(sent, "seq", -1)
    zero_one = jnp.zeros((seq_count, 1, width_share), jnp.float32)
    zero_two = jnp.zeros((seq_count, 2, width_share), jnp.float32)
    spacer = jnp.zeros((seq_count, length - 2, width_share), jnp.float32)
    grad_mixed = (
        taps[2] * grad_filtered
        + jnp.concatenate([near[:, 1:], zero_one], 1)
        + jnp.concatenate([far[:, 2:], zero_two], 1)
        + jnp.concatenate([spacer, came], 1)
    )
    grad_project = (
        jnp.stack([grad_mixed * values, grad_output_gate, grad_mixed * input_gate], 2)
        .reshape(tokens, 3 * width_share)
        .astype(jnp.bfloat16)
    )
    back_in = mid_total((contract(grad_project, exit_flat, 1, 1),))[0]
    low_back_in = back_in.astype(jnp.bfloat16) * select
    grad_normed = share_total(contract(grad_project, in_flat, 1, 1)) + contract(
        low_back_in, in_entry, 1, 1
    )
    in_entry_grad = contract(normed, low_back_in, 0, 0)
    in_exit_grad = contract(low_in, grad_project, 0, 0).reshape(in_exit.shape)
    weighted_one = grad_normed * mixer_share
    cube_one = scale_one * scale_one * scale_one
    grad_inputs = (
        grad_hidden
        + scale_one[:, None] * weighted_one
        - residual * (cube_one * row_total(weighted_one * residual) / width)[:, None]
    )
    summed = (
        lax.psum(in_entry_grad.astype(jnp.bfloat16), "seq").astype(jnp.float32),
        lax.psum(in_exit_grad.astype(jnp.bfloat16), "seq").astype(jnp.float32),
        lax.psum(out_entry_grad.astype(jnp.bfloat16), "seq").astype(jnp.float32),
        lax.psum(out_exit_grad.astype(jnp.bfloat16), "seq").astype(jnp.float32),
        lax.psum(gate_entry_grad.astype(jnp.bfloat16), "seq").astype(jnp.float32),
        lax.psum(gate_exit_grad.astype(jnp.bfloat16), "seq").astype(jnp.float32),
        lax.psum(up_entry_gradient.astype(jnp.bfloat16), "seq").astype(jnp.float32),
        lax.psum(up_exit_grad.astype(jnp.bfloat16), "seq").astype(jnp.float32),
        lax.psum(down_entry_grad.astype(jnp.bfloat16), "seq").astype(jnp.float32),
        lax.psum(down_exit_grad.astype(jnp.bfloat16), "seq").astype(jnp.float32),
    )
    return (
        output,
        grad_inputs.reshape(seq_count, length, width_share),
        summed[0],
        summed[1],
        summed[2],
        summed[3],
        summed[4],
        summed[5],
        summed[6],
        summed[7],
        summed[8],
        summed[9],
    )


VMEM_BYTES = 58 * 1024 * 1024


def product(left, right):
    return jnp.dot(left, right, preferred_element_type=jnp.float32)


def product_t(left, right):
    return lax.dot_general(left, right, (((1,), (1,)), ((), ())), preferred_element_type=jnp.float32)


def wide_value(value):
    return value.astype(jnp.float32)


def low(value):
    return value.astype(jnp.bfloat16)


def each_tile(total, size, body):
    whole = total // size
    if whole:

        @pl.loop(0, whole)
        def _(i):
            body(pl.multiple_of(i * size, size), size)

    if total % size:
        body(whole * size, total % size)


def spans(total, size):
    return [(at, min(size, total - at)) for at in range(0, total, size)]


class Mover:
    def __init__(self, sems):
        self.sems, self.count, self.pending = sems, 0, []

    def start(self, source, target):
        copy = pltpu.make_async_copy(source, target, self.sems.at[self.count])
        self.count += 1
        copy.start()
        self.pending.append(copy)
        return copy

    def wait(self, copies=None):
        for copy in list(self.pending if copies is None else copies):
            copy.wait()
            self.pending = [c for c in self.pending if c is not copy]


def piece_index(place_ref, kind, flip):
    return jnp.bitwise_xor(place_ref[1 if kind == "half" else 2], flip)


def start_in(mover, loads, own, pieces, plan, place_ref, target, width, share):
    for i in range(3):
        loads.append(mover.start(own.at[i], target.at[:, pl.ds(i * width, share)]))
    for ref, (r, kind, flip, _) in zip(pieces, plan):
        n = width // COUNT[kind]
        rows = pl.ds(pl.multiple_of(piece_index(place_ref, kind, flip) * n, 16), n)
        for i in range(3):
            loads.append(mover.start(ref.at[pl.ds(i * n, n)], target.at[rows, pl.ds(i * width + r * share, share)]))


def start_out(mover, loads, own, pieces, plan, place_ref, target, share):
    loads.append(mover.start(own, target.at[pl.ds(0, share)]))
    for ref, (r, kind, flip, base) in zip(pieces, plan):
        n = share // COUNT[kind]
        rows = pl.ds(pl.multiple_of(r * share + piece_index(place_ref, kind, flip) * n, 16), n)
        for i in range(4):
            loads.append(mover.start(ref.at[pl.ds(base + i * n, n)], target.at[rows, pl.ds(i * share, share)]))


def kernel_call(body, name, args, kinds, outs, scratch, sems, flops, size, out_space=pl.ANY):
    spaces = {"s": pltpu.SMEM, "v": pltpu.VMEM, "a": pl.ANY}
    return pl.pallas_call(
        body,
        out_shape=tuple(outs),
        in_specs=[pl.BlockSpec(memory_space=spaces[k]) for k in kinds],
        out_specs=tuple(pl.BlockSpec(memory_space=out_space) for _ in outs),
        scratch_shapes=list(scratch) + [pltpu.SemaphoreType.DMA((sems,))],
        compiler_params=pltpu.CompilerParams(vmem_limit_bytes=VMEM_BYTES),
        cost_estimate=pl.CostEstimate(flops=flops, bytes_accessed=size, transcendentals=0),
        name=name,
    )(*args)


def shaped(shape, kind=jnp.bfloat16):
    return jax.ShapeDtypeStruct(shape, kind)


TAP_ROWS = 16


class Rest:
    def __init__(self, share, rank, count):
        self.out_rows, self.side_rows = share // count, rank // count
        self.entry_at = 4 * self.out_rows
        self.side_at = self.entry_at + 2 * self.out_rows
        self.tap_at = self.side_at + 5 * self.side_rows
        self.rows = self.tap_at + TAP_ROWS


COUNT = {"half": 2, "quarter": 4}


def pack_in_kernel(place_ref, in_weight, out, sems):
    rows = in_weight.shape[1] // 4
    mover = Mover(sems)
    for i in range(3):
        part = pl.ds(pl.multiple_of(place_ref[2] * rows, 16), rows)
        mover.start(in_weight.at[i, part], out.at[pl.ds(i * rows, rows)])
    mover.wait()


def pack_in(place_ids, in_weight):
    _, width, share = in_weight.shape
    return kernel_call(
        pack_in_kernel, "pack_in", [place_ids, in_weight], "sa", [shaped((3 * width // 4, share))], [], 4, 0, 2_000_000, pltpu.VMEM
    )[0]


def pack_first_kernel(place_ref, inputs, cotangent, in_weight, out_weight, *refs):
    entries, (in_exit, out_exit, down_exit, taps), outs, sems = refs[:4], refs[4:8], refs[8:-1], refs[-1]
    far, beside, below, own_block, ct_rows, ct_far = outs
    share, width = out_weight.shape
    length, rank = inputs.shape[1], entries[0].shape[1]
    mover = Mover(sems)

    def part(index, rows):
        return pl.ds(pl.multiple_of(place_ref[index] * rows, 16), rows)

    in_rows = width // 4
    for i in range(3):
        mover.start(in_weight.at[i, part(2, in_rows)], far.at[pl.ds(i * in_rows, in_rows)])
    for index, target, base in ((2, far, 3 * in_rows), (1, beside, length), (1, below, length)):
        rest = Rest(share, rank, 4 if index == 2 else 2)
        rows = part(index, rest.out_rows)
        for i in range(4):
            spot = target.at[pl.ds(base + i * rest.out_rows, rest.out_rows)]
            mover.start(out_weight.at[rows, pl.ds(i * share, share)], spot)
            spot = target.at[pl.ds(base + rest.entry_at + i // 3 * rest.out_rows, rest.out_rows), pl.ds(i % 3 * rank, rank)]
            mover.start(entries[i].at[rows], spot)
        rows = part(index, rest.side_rows)
        for i, side in enumerate((in_exit.at[0], in_exit.at[1], in_exit.at[2], out_exit, down_exit)):
            mover.start(side.at[rows], target.at[pl.ds(base + rest.side_at + i * rest.side_rows, rest.side_rows)])
        mover.start(taps, target.at[pl.ds(base + rest.tap_at, TAP_ROWS)])
    far_block = far.at[pl.ds(far.shape[0] - length, length)]
    for r, target in enumerate((own_block, beside.at[pl.ds(0, length)], below.at[pl.ds(0, length)], far_block)):
        index = jnp.bitwise_xor(place_ref[0], r)
        mover.start(inputs.at[index], target)
        mover.start(cotangent.at[index], (ct_rows, ct_far)[r // 2].at[r % 2])
    mover.wait()


def pack_first(place_ids, inputs, cotangent, in_weight, out_weight, entries, sides, taps):
    length, share = inputs.shape[1:]
    width, rank = in_weight.shape[1], entries[0].shape[1]
    args = [place_ids, inputs, cotangent, in_weight, out_weight, *entries, *sides, taps]
    in_rows = 3 * width // 4
    heights = [in_rows + Rest(share, rank, 4).rows + length] + [length + Rest(share, rank, 2).rows] * 2 + [length]
    outs = [shaped((n, share)) for n in heights] + [shaped((2, length, share))] * 2
    return kernel_call(pack_first_kernel, "pack_first", args, "s" + "a" * 12, outs, [], 80, 0, 16_000_000, pltpu.VMEM)


def pack_second_kernel(cuts, place_ref, *refs):
    near, packs, sems = refs[:6], refs[6:-1], refs[-1]
    mover = Mover(sems)
    quarter_rows = near[0].shape[0] // 4
    width = near[0].shape[1]
    for (at, n), pack in zip(cuts, packs):
        rows = pl.ds(pl.multiple_of(place_ref[2] * quarter_rows + at, 16), n)
        for i in range(3):
            mover.start(near[2 * i].at[rows], pack.at[i, :, pl.ds(0, width)])
            mover.start(near[2 * i + 1].at[rows], pack.at[i, :, pl.ds(width, near[1].shape[1])])
    mover.wait()


def pack_second(place_ids, near, cuts):
    outs = [shaped((3, n, near[0].shape[1] + near[1].shape[1])) for _, n in cuts]
    return kernel_call(
        functools.partial(pack_second_kernel, cuts), "pack_second", [place_ids, *near], "s" + "a" * 6, outs, [], 32, 0, 20_000_000, pltpu.VMEM
    )


def mixer_kernel(in_plan, rest_plan, *refs):
    refs = list(refs)

    def take(n):
        return [refs.pop(0) for _ in range(n)]

    place_ref, select, prev, gain_one, gain_two = take(5)
    head, in_own, out_own, *own = take(11)
    entries_own, (in_exit, out_exit, down_exit, taps_own) = own[:4], own[4:]
    blocks = take(4)
    in_pieces, rest_pieces = take(len(in_plan)), take(len(rest_plan))
    kept_out, gated_out, tokens_out, normed_out, hidden_out, two_out, lows_out, entry_out, column_out, exit_out, taps_out = take(11)
    (x_s, n_s, in_s, out_s, entry_s, col_s, exit_s, tap_s, taps_s, proj_s, mix_s) = take(11)
    kept_s, gated_s, hid_s, two_s, low_in_s, lows_s, sems = refs
    length, width = gated_s.shape
    share, rank, edge = width // 4, low_in_s.shape[1], head.shape[1]
    mover = Mover(sems)

    def absolute(r):
        return pl.multiple_of(jnp.bitwise_xor(place_ref[0], r) * share, 128)

    for r in range(4):
        lanes = pl.ds(absolute(r), share)
        first = blocks[r].shape[0] - length if r == 3 else 0
        mover.start(blocks[r].at[pl.ds(first, length)], x_s.at[pl.ds(edge, length), lanes])
        mover.start(head.at[r], x_s.at[pl.ds(0, edge), lanes])
    token_loads = list(mover.pending)
    row_loads, column_loads, loads, out_loads = [], [], [], []
    for i, source in enumerate(entries_own):
        row_loads.append(mover.start(source, entry_s.at[pl.ds(absolute(0), share), pl.ds(i * rank, rank)]))
    for i, source in enumerate((in_exit.at[0], in_exit.at[1], in_exit.at[2], out_exit, down_exit)):
        column_loads.append(mover.start(source, col_s.at[pl.ds(i * rank, rank), pl.ds(0, share)]))
    column_loads.append(mover.start(taps_own, tap_s.at[:, pl.ds(0, share)]))
    for ref, (r, kind, flip, base) in zip(rest_pieces, rest_plan):
        rest, index, lanes = Rest(share, rank, COUNT[kind]), piece_index(place_ref, kind, flip), pl.ds(r * share, share)
        rows = pl.ds(pl.multiple_of(absolute(r) + index * rest.out_rows, 16), rest.out_rows)
        source = ref.at[pl.ds(base + rest.entry_at, rest.out_rows)]
        row_loads.append(mover.start(source, entry_s.at[rows, pl.ds(0, 3 * rank)]))
        source = ref.at[pl.ds(base + rest.entry_at + rest.out_rows, rest.out_rows), pl.ds(0, rank)]
        row_loads.append(mover.start(source, entry_s.at[rows, pl.ds(3 * rank, rank)]))
        for i in range(5):
            rows = pl.ds(pl.multiple_of(i * rank + index * rest.side_rows, 16), rest.side_rows)
            source = ref.at[pl.ds(base + rest.side_at + i * rest.side_rows, rest.side_rows)]
            column_loads.append(mover.start(source, col_s.at[rows, lanes]))
        if flip == 0:
            column_loads.append(mover.start(ref.at[pl.ds(base + rest.tap_at, TAP_ROWS)], tap_s.at[:, lanes]))
    start_in(mover, loads, in_own, in_pieces, in_plan, place_ref, in_s, width, share)
    start_out(mover, out_loads, out_own, rest_pieces, rest_plan, place_ref, out_s, share)
    mover.wait(token_loads)

    def norm(at, n):
        rows = pl.ds(at, n)
        x = wide_value(x_s[rows, :])
        scale = lax.rsqrt(jnp.sum(x * x, 1, keepdims=True) / width + EPS)
        n_s[rows, :] = low(x * scale * gain_one[...])

    each_tile(edge + length, 48, norm)
    main = pl.ds(edge, length)
    mover.start(x_s.at[main], tokens_out)
    mover.start(n_s.at[main], normed_out)
    mover.wait(row_loads)
    mover.start(entry_s, entry_out)
    low_in_s[...] = low(product(n_s[...], entry_s[:, pl.ds(0, rank)])) * select[...]
    lows_s[0] = low_in_s[main, :]
    mover.wait(column_loads)
    mover.start(col_s, column_out)
    taps_s[...] = wide_value(tap_s[...])[:8]
    mover.start(taps_s, taps_out)
    for r in range(4):
        exit_s[:, pl.ds(absolute(r), share)] = col_s[pl.ds(3 * rank, 2 * rank), pl.ds(r * share, share)]
    mover.start(exit_s, exit_out)
    mover.wait(loads)
    for i in range(3):

        def project(at, n):
            total = product(n_s[...], in_s[:, pl.ds(i * width + at, n)])
            total += product(low_in_s[...], col_s[pl.ds(i * rank, rank), pl.ds(at, n)])
            proj_s[:, pl.ds(i * width + at, n)] = total

        each_tile(width, width // 3, project)
    for r in range(4):
        lanes = pl.ds(r * share, share)
        mix_s[...] = proj_s[:, lanes] * proj_s[:, pl.ds(2 * width + r * share, share)]
        tap = [taps_s[pl.ds(i, 1), lanes] for i in range(3)]
        for at, n in spans(length, 128):
            rows, above = pl.ds(at, n), pl.ds(at + edge, n)
            filtered = (
                tap[2] * mix_s[above, :]
                + tap[1] * (prev[rows, pl.ds(0, 1)] * mix_s[pl.ds(at + edge - 1, n), :])
                + tap[0] * (prev[rows, pl.ds(1, 1)] * mix_s[pl.ds(at + edge - 2, n), :])
            )
            output_gate = proj_s[above, pl.ds(width + r * share, share)]
            gated_s[rows, lanes] = low(output_gate * filtered)
            kept_s[0, rows, lanes] = low(proj_s[above, lanes])
            kept_s[1, rows, lanes] = low(output_gate)
            kept_s[2, rows, lanes] = low(proj_s[above, pl.ds(2 * width + r * share, share)])
            kept_s[3, rows, lanes] = low(filtered)
    mover.start(kept_s, kept_out)
    mover.start(gated_s, gated_out)
    chosen = select[main, :]
    inner = 0.0
    for r in range(4):
        rows = pl.ds(absolute(r), share)
        inner = inner + product(gated_s[:, pl.ds(r * share, share)], entry_s[rows, pl.ds(rank, rank)])
    lows_s[1] = low(inner) * chosen
    mover.wait(out_loads)

    def branch(at, n):
        cols = pl.ds(at, n)
        total = product(gated_s[...], out_s[:, cols]) + product(lows_s[1], exit_s[pl.ds(0, rank), cols])
        hid_s[:, cols] = total + wide_value(x_s[main, cols])

    each_tile(width, width // 3, branch)
    mover.start(hid_s, hidden_out)

    def norm_two(at, n):
        rows = pl.ds(at, n)
        h = hid_s[rows, :]
        scale = lax.rsqrt(jnp.sum(h * h, 1, keepdims=True) / width + EPS)
        two_s[rows, :] = low(h * scale * gain_two[...])

    each_tile(length, 64, norm_two)
    mover.start(two_s, two_out)
    inner = product(two_s[...], entry_s[:, pl.ds(2 * rank, 2 * rank)])
    lows_s[2] = low(inner[:, :rank]) * chosen
    lows_s[3] = low(inner[:, rank:]) * chosen
    mover.start(lows_s, lows_out)
    mover.wait()


def mixer(place_ids, small, own, blocks, in_pieces, rest_pieces):
    length, share = blocks[0].shape
    width, rank, edge = 4 * share, own[3].shape[1], own[0].shape[1]
    bf, f32 = jnp.bfloat16, jnp.float32
    args = [place_ids, *small, *own, *blocks] + [p[0] for p in in_pieces + rest_pieces]
    kinds = "s" + "v" * len(small) + "a" * (len(args) - 1 - len(small))
    v = pltpu.VMEM
    columns, taps = 5 * rank, TAP_ROWS
    return kernel_call(
        functools.partial(mixer_kernel, [p[1:] for p in in_pieces], [p[1:] for p in rest_pieces]),
        "mixer",
        args,
        kinds,
        [
            shaped((4, length, width)),
            shaped((length, width)),
            shaped((length, width)),
            shaped((length, width)),
            shaped((length, width), f32),
            shaped((length, width)),
            shaped((4, length, rank)),
            shaped((width, 4 * rank)),
            shaped((columns, width)),
            shaped((2 * rank, width)),
            shaped((8, width), f32),
        ],
        [
            v((edge + length, width), bf),
            v((edge + length, width), bf),
            v((width, 3 * width), bf),
            v((width, width), bf),
            v((width, 4 * rank), bf),
            v((columns, width), bf),
            v((2 * rank, width), bf),
            v((taps, width), bf),
            v((8, width), f32),
            v((edge + length, 3 * width), f32),
            v((edge + length, share), f32),
            v((4, length, width), bf),
            v((length, width), bf),
            v((length, width), f32),
            v((length, width), bf),
            v((edge + length, rank), bf),
            v((4, length, rank), bf),
        ],
        200,
        2 * length * width * 4 * width,
        50_000_000,
    )


def ready_kernel(place_ref, select, exits, rows_mine, rows_far, rows_x, rows_far_x, grad_out, back_out, grad_s, back_s, sems):
    share, rank = rows_mine.shape[2], select.shape[2]
    mover = Mover(sems)
    for t in range(2):
        for r, source in enumerate((rows_mine.at[t], rows_x.at[1 - t], rows_far.at[t], rows_far_x.at[1 - t])):
            at = pl.multiple_of(jnp.bitwise_xor(place_ref[0], r) * share, 128)
            mover.start(source, grad_s.at[t, :, pl.ds(at, share)])
    mover.wait()
    mover.start(grad_s, grad_out)
    for t in range(2):
        back_s[t] = low(product_t(grad_s[t], exits[pl.ds(rank, rank), :])) * select[t]
    mover.start(back_s, back_out)
    mover.wait()


def ready(place_ids, select, exits, cotangents):
    length, share = cotangents[0].shape[1:]
    rank, width = select.shape[2], 4 * share
    shapes = [(2, length, width), (2, length, rank)]
    return kernel_call(
        ready_kernel,
        "ready",
        [place_ids, select, exits, *cotangents],
        "svvaaaa",
        [shaped(v) for v in shapes],
        [pltpu.VMEM(v, jnp.bfloat16) for v in shapes],
        16,
        4 * length * width * rank,
        10_000_000,
    )


def lows_kernel(select, seen, entry, lows):
    rank = select.shape[1]
    inner = product(seen[...], entry[:, pl.ds(2 * rank, 2 * rank)])
    lows[0] = low(inner[:, :rank]) * select[...]
    lows[1] = low(inner[:, rank:]) * select[...]


def lows_of(select, seen, entry):
    length, rank = select.shape
    return pl.pallas_call(
        lows_kernel,
        out_shape=shaped((2, length, rank)),
        in_specs=[pl.BlockSpec(memory_space=pltpu.VMEM)] * 3,
        out_specs=pl.BlockSpec(memory_space=pltpu.VMEM),
        cost_estimate=pl.CostEstimate(flops=4 * length * rank * seen.shape[1], bytes_accessed=3_000_000, transcendentals=0),
        compiler_params=pltpu.CompilerParams(vmem_limit_bytes=16 * 1024 * 1024),
        name="lows",
    )(select, seen, entry)


FAR_FLIPS = (0, 2, 1, 3)


def feed_kernel(far, add_tokens, add_grads, settle, sizes, which, turn, *refs):
    refs = list(refs)

    def take(n):
        return [refs.pop(0) for _ in range(n)]

    (quarter_ref,) = take(1) if far else (None,)
    token_refs = take(4)
    weights = take(4 if far else 6)
    prior_refs = take(2 * add_tokens + add_grads)
    down_out, back_out, grads_out = take(3)
    seen, lows, grad, low_back, gate_w, up_w, down_w, act_s, gg_s, gu_s, down_s, back_s, grads_s, *prior, sems = refs
    low_gate, low_up = lows.at[0], lows.at[1]
    width, rank, units = seen.shape[1], low_back.shape[1], gate_w.shape[0]
    whole, side = pl.ds(0, width), pl.ds(width, rank)
    steps = []
    for size in sizes:
        steps.append((sum(n for _, n in steps), size))
    quarter_rows = units // 4
    mover = Mover(sems)
    token_refs[1] = token_refs[1].at[pl.ds(which, 2)]
    token_refs[2], token_refs[3] = token_refs[2].at[turn], token_refs[3].at[turn]
    token_loads = [mover.start(a, b) for a, b in zip(token_refs, (seen, lows, grad, low_back))]
    loads = []
    if far:
        for n, ref in enumerate(weights):
            rows = pl.ds(n * quarter_rows, quarter_rows)
            for i, dst in enumerate((gate_w, up_w, down_w)):
                loads.append((n * quarter_rows, mover.start(ref.at[i], dst.at[rows])))
    else:
        for at, n in steps:
            rows = pl.ds(at, n)
            for i, dst in enumerate((gate_w, up_w, down_w)):
                loads.append((at, mover.start(weights[2 * i].at[rows], dst.at[rows, whole])))
                loads.append((at, mover.start(weights[2 * i + 1].at[rows], dst.at[rows, side])))
    prior_loads = [mover.start(a, b) for a, b in zip(prior_refs, prior)]
    if add_tokens:
        down_prior, back_prior = prior[:2]
    if add_grads:
        grads_prior = prior[-1]
    mover.wait(token_loads)

    for at, n in steps:
        while loads and loads[0][0] < at + n:
            mover.wait([loads.pop(0)[1]])
        cols = pl.ds(at, n)
        gate = product_t(seen[...], gate_w[cols, whole]) + product_t(low_gate[...], gate_w[cols, side])
        up = product_t(seen[...], up_w[cols, whole]) + product_t(low_up[...], up_w[cols, side])
        ga = product_t(grad[...], down_w[cols, whole]) + product_t(low_back[...], down_w[cols, side])
        sigma = jax.nn.sigmoid(gate)
        swish = gate * sigma
        act_s[:, cols] = low(swish * up)
        gu_s[:, cols] = low(ga * swish)
        gg_s[:, cols] = low(ga * up * (sigma + swish * (1.0 - sigma)))

    mover.wait(prior_loads)
    for i, (left, right) in enumerate(((low_gate, gg_s), (low_up, gu_s), (low_back, act_s))):
        turned, lanes = left[...].T, pl.ds(i * rank, rank)

        def grad_tile(at, n):
            cols = pl.ds(at, n)
            total = product(turned, right[:, cols]).T
            if add_grads:
                total += grads_prior[cols, lanes]
            grads_s[cols, lanes] = total

        each_tile(units, units if units < 640 else 512, grad_tile)
    if settle:
        for n, flip in enumerate(FAR_FLIPS):
            at = jnp.bitwise_xor(quarter_ref[0], flip)
            mover.start(grads_s.at[pl.ds(n * quarter_rows, quarter_rows)], grads_out.at[at])
    else:
        mover.start(grads_s, grads_out)

    def back_tile(at, n):
        cols = pl.ds(at, n)
        total = product(gg_s[...], gate_w[:, cols]) + product(gu_s[...], up_w[:, cols])
        if add_tokens:
            total += wide_value(back_prior[:, cols])
        back_s[:, cols] = low(total)

    each_tile(width, 512, back_tile)
    for i, (left, right) in enumerate(((gg_s, gate_w), (gu_s, up_w))):
        total = product(left[...], right[:, side])
        cols = pl.ds(width + i * rank, rank)
        if add_tokens:
            total += wide_value(back_prior[:, cols])
        back_s[:, cols] = low(total)
    mover.start(back_s, back_out)

    def down_tile(at, n):
        cols = pl.ds(at, n)
        total = product(act_s[...], down_w[:, cols])
        if add_tokens:
            total += wide_value(down_prior[:, cols])
        down_s[:, cols] = low(total)

    each_tile(width + rank, 512, down_tile)
    mover.start(down_s, down_out)
    mover.wait()


def feed(tokens, which, turn, weights, quarter=None, add_tokens=None, add_grads=None, settle=False):
    far = quarter is not None
    length, width = tokens[0].shape
    rank = tokens[1].shape[2]
    units = 4 * weights[0].shape[1] if far else weights[0].shape[0]
    sizes = [n for _, n in spans(units, 512)]
    if len(sizes) > 1 and sizes[-1] < 256:
        sizes[-2:] = [256, sizes[-2] + sizes[-1] - 256]
    bf, f32, v = jnp.bfloat16, jnp.float32, pltpu.VMEM
    args = ([quarter] if far else []) + list(tokens) + list(weights)
    shapes = [((length, width + rank), bf), ((length, width + 2 * rank), bf), ((units, 3 * rank), f32)]
    prior = list(add_tokens or ()) + ([] if add_grads is None else [add_grads])
    prior_scratch = (shapes[:2] if add_tokens else []) + ([] if add_grads is None else shapes[2:])
    outs = [shaped(*pair) for pair in shapes]
    if settle:
        outs[2] = shaped((4, units // 4, 3 * rank), f32)
    return kernel_call(
        functools.partial(
            feed_kernel, far, add_tokens is not None, add_grads is not None, settle, tuple(sizes), which, turn
        ),
        "feed_far" if far else "feed_near",
        args + prior,
        ("s" if far else "") + "a" * (4 + len(weights) + len(prior)),
        outs,
        [v((length, width), bf), v((2, length, rank), bf), v((length, width), bf), v((length, rank), bf)]
        + [v((units, width + rank), bf)] * 3
        + [v((length, units), bf)] * 3
        + [v(*pair) for pair in shapes + prior_scratch],
        48,
        12 * length * units * (width + 2 * rank),
        30_000_000,
    )


def branch_kernel(plan, *refs):
    refs = list(refs)

    def take(n):
        return [refs.pop(0) for _ in range(n)]

    place_ref, came, mine, hidden, grad, two, gated, lows, select, gain_two, entry, exits, taps, prev, down_mine, down_next = take(16)
    kept, near, far_0, far_1, far_2, out_own = take(6)
    pieces = take(len(plan))
    grad_hidden_out, filtered_out, gates_out, edge_out, keep_out, give_out, sent_out, own_out = take(8)
    near_s, far_s, pack_s, part_s, out_s, kept_s, w_s, gb_s, lo_s, gf_s, gate_s, edge_s, wide_s, sems = refs
    length, width = hidden.shape
    share, rank = width // 4, select.shape[1]
    mover = Mover(sems)
    start_out(mover, [], out_own, pieces, plan, place_ref, out_s, share)
    mover.start(kept.at[1], kept_s.at[0])
    mover.start(kept.at[3], kept_s.at[1])
    loads = list(mover.pending)
    unit_loads = [mover.start(near, near_s)]
    quarter_rows, at = near.shape[0] // 4, 0
    for far in (far_0, far_1, far_2):
        n = far.shape[1]
        for q in range(4):
            unit_loads.append(mover.start(far.at[q], far_s.at[pl.ds(q * quarter_rows + at, n)]))
        at += n
    part_s[0] = low(hidden[...] + wide_value(down_mine[:, pl.ds(0, width)]))
    part_s[1] = down_next[:, pl.ds(0, width)]
    for t in range(2):
        for r in range(4):
            lanes = pl.ds(pl.multiple_of(jnp.bitwise_xor(place_ref[0], r) * share, 128), share)
            target = (own_out if r % 2 == 0 else sent_out).at[2 * t + r // 2]
            mover.start(part_s.at[t, :, lanes], target)
    side = pl.ds(width, 2 * rank)
    inner = wide_value(came[:, side]) + wide_value(mine[:, side])
    lo_s[0] = low(inner[:, :rank]) * select[...]
    lo_s[1] = low(inner[:, rank:]) * select[...]

    def combine(at, n):
        cols = pl.ds(at, n)
        total = wide_value(came[:, cols]) + wide_value(mine[:, cols])
        total += product_t(lo_s[0], entry[cols, pl.ds(2 * rank, rank)])
        total += product_t(lo_s[1], entry[cols, pl.ds(3 * rank, rank)])
        w_s[:, cols] = total * gain_two[:, cols]

    each_tile(width, width // 3, combine)

    def norm(at, n):
        rows = pl.ds(at, n)
        h, w = hidden[rows, :], w_s[rows, :]
        scale = lax.rsqrt(jnp.sum(h * h, 1, keepdims=True) / width + EPS)
        moment = jnp.sum(w * h, 1, keepdims=True) / width
        value = wide_value(grad[0, rows, :]) + scale * w - h * (scale * scale * scale * moment)
        w_s[rows, :] = value
        gb_s[rows, :] = low(value)

    each_tile(length, 32, norm)
    mover.start(w_s, grad_hidden_out)
    lo_s[2] = low(product_t(gb_s[...], exits[pl.ds(0, rank), :])) * select[...]
    mover.wait(loads)
    for r in range(4):
        cols = pl.ds(r * share, share)
        rows = pl.ds(pl.multiple_of(jnp.bitwise_xor(place_ref[0], r) * share, 128), share)
        gg = product_t(gb_s[...], out_s[cols, :]) + product_t(lo_s[2], entry[rows, pl.ds(rank, rank)])
        gf = gg * wide_value(kept_s[0, :, cols])
        gf_s[:, cols] = low(gf)
        first = gf[:8]
        beside = taps[pl.ds(1, 1), cols] * (prev[pl.ds(0, 8), pl.ds(0, 1)] * first)
        beyond = taps[pl.ds(0, 1), cols] * (prev[pl.ds(0, 8), pl.ds(1, 1)] * first)
        edge_s[pl.ds(0, 1), cols] = beyond[0:1]
        edge_s[pl.ds(1, 1), cols] = beside[0:1] + beyond[1:2]
        edge_s[pl.ds(2, 6), cols] = jnp.zeros((6, share), jnp.float32)
        gate_s[:, cols] = low(gg * wide_value(kept_s[1, :, cols]))
    mover.start(gf_s, filtered_out)
    mover.start(gate_s, gates_out)
    mover.start(edge_s, edge_out)
    for i, (left, right) in enumerate(((lo_s.at[0], two), (lo_s.at[1], two), (lows.at[1], gb_s))):
        turned = left[...].T

        def wide_tile(at, n):
            cols = pl.ds(at, n)
            wide_s[i, :, cols] = low(product(turned, right[:, cols]))

        each_tile(width, width // 3, wide_tile)
    turned = lo_s[2].T
    for r in range(4):
        lanes = pl.ds(pl.multiple_of(jnp.bitwise_xor(place_ref[0], r) * share, 128), share)
        wide_s[3, :, lanes] = low(product(turned, gated[:, pl.ds(r * share, share)]))
    mover.wait(unit_loads)
    half = near.shape[0] // 2
    for h, out in ((0, keep_out), (1, give_out)):
        mine = jnp.bitwise_xor(place_ref[1], h)
        rows = pl.ds(pl.multiple_of(mine * half, 16), half)
        at = 0
        for r, units in ((0, near_s), (2, far_s), (1, None), (3, None)):
            lanes = pl.ds(pl.multiple_of(jnp.bitwise_xor(place_ref[0], r) * share, 128), share)
            for j in range(2):
                pack_s[h, pl.ds(at + j * rank, rank), :] = wide_s[mine * 2 + j, :, lanes]
            at += 2 * rank
            if units is not None:
                pack_s[h, pl.ds(at, half), :] = low(units[rows, :])
                at += half
        mover.start(pack_s.at[h], out)
    mover.wait()


def branch_back(place_ids, small, kept, units, own, pieces):
    length, width = small[2].shape
    share, rank, unit_rows = width // 4, small[7].shape[1], units[0].shape[0]
    bf, f32, v = jnp.bfloat16, jnp.float32, pltpu.VMEM
    return kernel_call(
        functools.partial(branch_kernel, [p[1:] for p in pieces]),
        "branch_back",
        [place_ids, *small, kept, *units, own, *[p[0] for p in pieces]],
        "s" + "v" * len(small) + "a" * (2 + len(units) + len(pieces)),
        [
            shaped((length, width), f32),
            shaped((length, width)),
            shaped((length, width)),
            shaped((8, width), f32),
            shaped((unit_rows + 8 * rank, share)),
            shaped((unit_rows + 8 * rank, share)),
            shaped((4, length, share)),
            shaped((4, length, share)),
        ],
        [
            v((unit_rows, share), f32),
            v((unit_rows, share), f32),
            v((2, unit_rows + 8 * rank, share), bf),
            v((2, length, width), bf),
            v((width, width), bf),
            v((2, length, width), bf),
            v((length, width), f32),
            v((length, width), bf),
            v((3, length, rank), bf),
            v((length, width), bf),
            v((length, width), bf),
            v((8, width), f32),
            v((4, rank, width), bf),
        ],
        80,
        2 * length * width * width + 8 * length * rank * width,
        40_000_000,
    )


def input_kernel(plan, *refs):
    refs = list(refs)

    def take(n):
        return [refs.pop(0) for _ in range(n)]

    place_ref, filtered, gates, tail, taps, prev, grad_hidden, tokens, normed, lows, select, gain_one, entry, column, low_down, grad_down = take(16)
    kept, in_own = take(2)
    pieces = take(len(plan))
    grad_out, keep_out, give_out = take(3)
    in_s, kept_s, near_s, far_s, gp_s, w_s, gi_s, lo_s, wide_s, entry_s, down_s, block_s, pack_s, sems = refs
    length, width = filtered.shape
    share, rank = width // 4, select.shape[1]
    mover = Mover(sems)
    first = [mover.start(kept.at[0], kept_s.at[0]), mover.start(kept.at[2], kept_s.at[1])]
    loads = []
    start_in(mover, loads, in_own, pieces, plan, place_ref, in_s, width, share)
    mover.wait(first)
    for r in range(4):
        lanes = pl.ds(r * share, share)
        tap = [taps[pl.ds(i, 1), lanes] for i in range(3)]
        for at, n in spans(length, 128):
            rows = pl.ds(at, n)
            value = wide_value(filtered[rows, lanes])
            near_s[rows, :] = tap[1] * (prev[rows, pl.ds(0, 1)] * value)
            far_s[rows, :] = tap[0] * (prev[rows, pl.ds(1, 1)] * value)
        near_s[pl.ds(length, 8), :] = jnp.zeros((8, share), jnp.float32)
        far_s[pl.ds(length, 8), :] = tail[:, lanes]
        for at, n in spans(length, 128):
            rows = pl.ds(at, n)
            mixed = tap[2] * wide_value(filtered[rows, lanes]) + near_s[pl.ds(at + 1, n), :] + far_s[pl.ds(at + 2, n), :]
            gp_s[rows, pl.ds(r * share, share)] = low(mixed * wide_value(kept_s[1, rows, lanes]))
            gp_s[rows, pl.ds(2 * width + r * share, share)] = low(mixed * wide_value(kept_s[0, rows, lanes]))
    gp_s[:, pl.ds(width, width)] = gates[...]
    inner = 0.0
    for i in range(3):
        inner = inner + product_t(gp_s[:, pl.ds(i * width, width)], column[pl.ds(i * rank, rank), :])
    lo_s[...] = low(inner) * select[...]
    turned = lows[0].T
    turned_back = lo_s[...].T

    def exit_tile(at, n):
        cols = pl.ds(at, n)
        wide_s[:, cols] = low(product(turned, gp_s[:, cols]))

    each_tile(3 * width, width // 3, exit_tile)

    def entry_tile(at, n):
        cols = pl.ds(at, n)
        entry_s[:, cols] = low(product(turned_back, normed[:, cols]))

    each_tile(width, width // 3, entry_tile)
    turned_down = low_down[0].T

    def down_tile(at, n):
        cols = pl.ds(at, n)
        down_s[:, cols] = low(product(turned_down, grad_down[0, :, cols]))

    each_tile(width, width // 3, down_tile)
    half = 5 * rank // 2
    for r in range(4):
        lanes = pl.ds(pl.multiple_of(jnp.bitwise_xor(place_ref[0], r) * share, 128), share)
        block_s[pl.ds(0, rank), :] = entry_s[:, lanes]
        for i in range(3):
            block_s[pl.ds((1 + i) * rank, rank), :] = wide_s[:, pl.ds(i * width + r * share, share)]
        block_s[pl.ds(4 * rank, rank), :] = down_s[:, lanes]
        for h in range(2):
            rows = pl.ds(pl.multiple_of(jnp.bitwise_xor(place_ref[1], h) * half, 16), half)
            pack_s[h, pl.ds(r * half, half), :] = block_s[rows, :]
    mover.start(pack_s.at[0], keep_out)
    mover.start(pack_s.at[1], give_out)
    mover.wait(loads)

    def back(at, n):
        cols = pl.ds(at, n)
        total = product_t(gp_s[...], in_s[cols, :]) + product_t(lo_s[...], entry[cols, pl.ds(0, rank)])
        w_s[:, cols] = total * gain_one[:, cols]

    each_tile(width, width // 3, back)

    def norm(at, n):
        rows = pl.ds(at, n)
        x, w = wide_value(tokens[rows, :]), w_s[rows, :]
        scale = lax.rsqrt(jnp.sum(x * x, 1, keepdims=True) / width + EPS)
        moment = jnp.sum(w * x, 1, keepdims=True) / width
        gi_s[rows, :] = low(grad_hidden[rows, :] + scale * w - x * (scale * scale * scale * moment))

    each_tile(length, 32, norm)
    for r in range(4):
        at = pl.multiple_of(jnp.bitwise_xor(place_ref[0], r) * share, 128)
        mover.start(gi_s.at[:, pl.ds(at, share)], grad_out.at[r])
    mover.wait()


def input_back(place_ids, small, kept, own, pieces):
    length, width = small[0].shape
    share, rank = width // 4, small[9].shape[1]
    bf, f32, v = jnp.bfloat16, jnp.float32, pltpu.VMEM
    return kernel_call(
        functools.partial(input_kernel, [p[1:] for p in pieces]),
        "input_back",
        [place_ids, *small, kept, own, *[p[0] for p in pieces]],
        "s" + "v" * len(small) + "a" * (2 + len(pieces)),
        [shaped((4, length, share)), shaped((10 * rank, share)), shaped((10 * rank, share))],
        [
            v((width, 3 * width), bf),
            v((2, length, width), bf),
            v((length + 8, share), f32),
            v((length + 8, share), f32),
            v((length, 3 * width), bf),
            v((length, width), f32),
            v((length, width), bf),
            v((length, rank), bf),
            v((rank, 3 * width), bf),
            v((rank, width), bf),
            v((rank, width), bf),
            v((5 * rank, share), bf),
            v((2, 10 * rank, share), bf),
        ],
        64,
        6 * length * width * width,
        40_000_000,
    )


def results_kernel(place_ref, own, came, low_down, exits, kept_out, sent_out, out_s, sems):
    share, rank = own.shape[2], low_down.shape[2]
    mover = Mover(sems)
    for i, out in ((0, kept_out), (1, sent_out)):
        lanes = pl.ds(pl.multiple_of(jnp.bitwise_xor(place_ref[0], 2 * i) * share, 128), share)
        for t in range(2):
            total = wide_value(own[2 * t + i]) + wide_value(came[2 * (1 - t) + i])
            out_s[2 * i + t] = low(total + product(low_down[t], exits[pl.ds(rank, rank), lanes]))
            mover.start(out_s.at[2 * i + t], out.at[jnp.bitwise_xor(place_ref[3], t)])
    mover.wait()


def results_of(place_ids, own, came, low_down, exits):
    count, length, share = own.shape
    return kernel_call(
        results_kernel,
        "results",
        [place_ids, own, came, low_down, exits],
        "svvvv",
        [shaped((2, length, share))] * 2,
        [pltpu.VMEM((count, length, share), jnp.bfloat16)],
        8,
        8 * length * share * low_down.shape[2],
        8_000_000,
    )


def finish_kernel(place_ref, one_own, one_other, two_own, two_other, *refs):
    in_entry, in_exit, out_entry, out_exit, gate_entry, gate_exit, up_entry, up_exit, down_entry, down_exit = refs[:10]
    one_s, two_s, sems = refs[10:]
    rank = in_entry.shape[1]
    mover = Mover(sems)
    for h, one, two in ((0, one_own, two_own), (1, one_other, two_other)):
        at = jnp.bitwise_xor(place_ref[1], h)
        mover.start(one, one_s.at[at])
        mover.start(two, two_s.at[at])
    mover.wait()
    first, second = pl.ds(0, rank), pl.ds(rank, rank)
    gate_entry[...] = wide_value(one_s[0, first, :]).T
    up_entry[...] = wide_value(one_s[0, second, :]).T
    out_exit[...] = wide_value(one_s[1, first, :])
    out_entry[...] = wide_value(one_s[1, second, :]).T
    half = gate_exit.shape[0] // 2
    for h in range(2):
        rows = pl.ds(h * half, half)
        for i, out in enumerate((gate_exit, up_exit, down_entry)):
            out[rows, :] = wide_value(one_s[h, pl.ds(2 * rank, half), pl.ds(i * rank, rank)])
    cut = rank // 2
    in_entry[...] = wide_value(two_s[0, first, :]).T
    in_exit[0] = wide_value(two_s[0, second, :])
    in_exit[1, pl.ds(0, cut), :] = wide_value(two_s[0, pl.ds(2 * rank, cut), :])
    in_exit[1, pl.ds(cut, cut), :] = wide_value(two_s[1, pl.ds(0, cut), :])
    in_exit[2] = wide_value(two_s[1, pl.ds(cut, rank), :])
    down_exit[...] = wide_value(two_s[1, pl.ds(cut + rank, rank), :])


def finish(place_ids, one_own, one_other, two_own, two_other, units, rank):
    share, f32, bf = one_own.shape[1], jnp.float32, jnp.bfloat16
    entry, exits, unit = (share, rank), (rank, share), (units, rank)
    shapes = [entry, (3, rank, share), entry, exits, entry, unit, entry, unit, unit, exits]
    return kernel_call(
        finish_kernel,
        "finish",
        [place_ids, one_own, one_other, two_own, two_other],
        "saaaa",
        [shaped(v, f32) for v in shapes],
        [pltpu.VMEM((2, *one_own.shape), bf), pltpu.VMEM((2, *two_own.shape), bf)],
        4,
        0,
        8_000_000,
        pltpu.VMEM,
    )


def swap(value, axis, bit):
    return lax.ppermute(value, axis, [(i, i ^ bit) for i in range(lax.axis_size(axis))])


def after(value, *others):
    return lax.optimization_barrier((value, others))[0]


def together(*values):
    return lax.optimization_barrier(values)


def place(relative, me):
    stacked = jnp.stack(relative)
    return [lax.dynamic_index_in_dim(stacked, a ^ me, 0, keepdims=False) for a in range(len(relative))]


def part_of(block, dim, index, count):
    rows = block.shape[dim] // count
    return lax.dynamic_slice_in_dim(block, index * rows, rows, dim)


def seq_step(value, bit):
    return low(wide_value(value) + wide_value(swap(value, "seq", bit)))


def seq_bits():
    return [2**k for k in range(1, 16) if 2**k < lax.axis_size("seq")]


def seq_total(value):
    for bit in seq_bits():
        value = seq_step(value, bit)
    return value


def seq_total_parts(value, *firsts):
    s = lax.axis_index("seq")
    for bit, first in zip(seq_bits(), firsts + (None,) * len(seq_bits())):
        keep = s // bit % 2
        other = swap(part_of(value, 0, 1 - keep, 2), "seq", bit)
        if first is not None:
            other = after(other, first)
        value = low(wide_value(part_of(value, 0, keep, 2)) + wide_value(other))
    for bit in seq_bits()[::-1]:
        value = jnp.concatenate(place([value, swap(value, "seq", bit)], s // bit % 2), 0)
    return value


def chip_half(value, dim, core):
    other = swap(low(part_of(value, dim, 1 - core, 2)), "seq", 1)
    return low(wide_value(part_of(value, dim, core, 2)) + wide_value(other))


def own_block(chip):
    total = wide_value(chip[0])
    for r in (3, 1, 2):
        total = total + wide_value(swap(chip[r], "mp", r))
    return low(total)


def both_halves(own, core):
    return wide_value(jnp.concatenate(place([own, swap(own, "seq", 1)], core), 0))


def fast_local(
    inputs,
    cotangent,
    mixer_gain,
    in_weight,
    in_entry,
    in_exit,
    conv_weight,
    out_weight,
    out_entry,
    out_exit,
    ffn_gain,
    gate_weight,
    gate_entry,
    gate_exit,
    up_weight,
    up_entry,
    up_exit,
    down_weight,
    down_entry,
    down_exit,
    doc_starts,
    adapter_ids,
):
    seqs, length, share = inputs.shape
    width = 4 * share
    rank = in_entry.shape[1]
    units = gate_weight.shape[1]
    m = lax.axis_index("mp")
    s = lax.axis_index("seq")
    x, y, core, quarter = m % 2, m // 2, s % 2, s % 4
    place_ids = jnp.stack([m, core, quarter, x]).astype(jnp.int32)
    halo = 16

    def block_for(stack, r):
        return lax.dynamic_index_in_dim(stack, m ^ r, 0, keepdims=False)

    in_slabs = in_weight.swapaxes(0, 1)
    own_taps = jnp.pad(conv_weight, ((0, TAP_ROWS - 3), (0, 0)))
    entries = (in_entry, out_entry, gate_entry, up_entry)
    sides = (in_exit.swapaxes(0, 1), out_exit, down_exit)
    in_quarter = pack_in(place_ids, in_slabs)
    far_pack, beside, below, own_block_rows, ct_rows, ct_far = pack_first(
        after(place_ids, in_quarter), inputs, cotangent, in_slabs, out_weight, entries, sides, own_taps
    )
    near = [gate_weight.T, gate_exit.T, up_weight.T, up_exit.T, down_weight, down_entry]
    count = units // 4 // 16
    rows = (-(-count * 10 // 27) * 16, count * 9 // 27 * 16)
    cuts = ((0, rows[0]), (rows[0], rows[1]), (rows[0] + rows[1], units // 4 - rows[0] - rows[1]))

    def spread(got, over, r, base):
        return [
            (got, r, "quarter", 0, base),
            (swap(got, "seq", 1), r, "quarter", 1, base),
            (over, r, "quarter", 2, base),
            (swap(over, "seq", 1), r, "quarter", 3, base),
        ]

    in_x, in_y = swap(in_quarter, "mp", 1), swap(in_quarter, "mp", 2)
    far_pack = swap(after(far_pack, in_x, in_y), "mp", 3)
    over_x, over_y = swap(in_x, "seq", 2), swap(in_y, "seq", 2)
    packed = pack_second(after(place_ids, in_x, in_y), near, cuts)
    beside, below = after((beside, below), in_x, in_y)
    beside, below = swap(beside, "mp", 1), swap(below, "mp", 2)
    in_pieces = spread(in_x, over_x, 1, 0) + spread(in_y, over_y, 2, 0)
    far_count = far_pack.shape[0] - length
    far_weights = far_pack[:far_count]
    over_far = swap(after(far_weights, [p[0] for p in in_pieces], packed), "seq", 2)
    row_blocks = [own_block_rows, beside, below, far_pack]
    ends = [length, length, length, far_pack.shape[0]]
    head = from_behind(jnp.stack([b[e - halo : e] for b, e in zip(row_blocks, ends)]), "seq", 1)
    far_pieces = spread(far_weights, over_far, 3, 3 * width // 4)
    in_pieces += [p[:4] + (0,) for p in far_pieces]
    rest_pieces = list(far_pieces)
    for got, r in ((beside, 1), (below, 2)):
        rest_pieces += [(got, r, "half", 0, length), (swap(got, "seq", 1), r, "half", 1, length)]
    ct_rows, ct_far, *packed = after((ct_rows, ct_far, *packed), [p[0] for p in rest_pieces])
    ct_x, ct_y, ct_g = swap(ct_rows, "mp", 1), swap(ct_far, "mp", 2), swap(ct_far, "mp", 3)
    packed = [packed[0], *after(tuple(packed[1:]), ct_x)]
    far_first = [swap(p, "mp", 2) for p in packed]

    starts = jnp.stack([doc_starts[m], doc_starts[m ^ 1]])[:, None, :]
    ids = jnp.stack([adapter_ids[m], adapter_ids[m ^ 1]])
    steps = (ids - jnp.pad(ids, ((0, 0), (1, 0)))[:, :-1])[:, None, :]
    position = (s * length - halo + jnp.arange(halo + length, dtype=jnp.int32))[None, :, None]
    adapter = jnp.sum(jnp.where(starts <= position, steps, 0), 2)
    lane = jnp.arange(rank, dtype=jnp.int32) // RANK
    select_ext = (adapter[:, :, None] == lane).astype(jnp.bfloat16)
    select = select_ext[:, halo:]
    begins = jnp.any(starts[0] == position[0], 1).astype(jnp.float32)
    prev_one = 1.0 - begins[halo:]
    prev_two = prev_one * (1.0 - begins[halo - 1 : halo - 1 + length])
    prev = jnp.stack([prev_one, prev_two], 1)
    gain_one = wide_value(mixer_gain)[None]
    gain_two = wide_value(ffn_gain)[None]

    kept, gated, tokens, normed, hidden, normed_two, lows, entry_full, column_full, exit_full, taps = mixer(
        place_ids,
        (select_ext[0], prev, gain_one, gain_two),
        (head, in_slabs, out_weight, *entries, *sides, own_taps),
        row_blocks,
        in_pieces,
        rest_pieces,
    )
    normed_next = swap(normed_two, "mp", 1)
    grad_down, back_lows = ready(place_ids, select, exit_full, (ct_rows, ct_y, ct_x, ct_g))
    lows_next = lows_of(select[1], normed_next, entry_full)
    mine = (normed_two, lows, grad_down, back_lows), 2, 0
    other = (normed_next, lows_next, grad_down, back_lows), 0, 1
    at_quarter = jnp.full((1,), quarter, jnp.int32)

    def spread_far(first, then, last):
        over = swap(after(first, then), "seq", 2)
        return [first, over, swap(after(first, last), "seq", 1), swap(after(over, last), "seq", 1)]

    near_mine = feed(*mine, near)
    near_next = feed(*other, near, add_grads=near_mine[2])
    far_zero = spread_far(far_first[0], near_mine[2], near_next[2])
    next_zero = feed(*other, far_zero, at_quarter, add_tokens=near_next[:2])
    mine_zero = feed(*mine, far_zero, at_quarter, add_tokens=near_mine[:2], add_grads=next_zero[2], settle=True)
    far_one = spread_far(far_first[1], near_mine[2], next_zero[2])
    next_one = feed(*other, far_one, at_quarter, add_tokens=next_zero[:2])
    far_two = spread_far(far_first[2], near_next[2], next_one[2])
    down_next, back_next, next_grads = feed(*other, far_two, at_quarter, add_tokens=next_one[:2])
    got_back = swap(back_next, "mp", 1)
    mine_one = feed(*mine, far_one, at_quarter, add_tokens=mine_zero[:2], add_grads=next_one[2], settle=True)
    down_mine, back_mine, mine_grads = feed(
        *mine, far_two, at_quarter, add_tokens=mine_one[:2], add_grads=next_grads, settle=True
    )

    grad_hidden, grad_filtered, grad_gates, edge, one_keep, one_give, sent, own_parts = branch_back(
        place_ids,
        (got_back, back_mine, hidden, grad_down, normed_two, gated, lows, select[0], gain_two, entry_full, exit_full, taps, prev, down_mine, down_next),
        kept,
        (near_next[2], mine_zero[2], mine_one[2], mine_grads),
        out_weight,
        rest_pieces,
    )
    came_edge = from_behind(edge, "seq", -1)
    came = swap(sent, "mp", 1)
    inner = after(jnp.stack([down_mine[:, width:], down_next[:, width:]]), got_back)
    inner_got = swap(inner, "mp", 1)
    low_down = low(wide_value(inner) + wide_value(inner_got[::-1])) * select

    def chip_sum(keep, give):
        return low(wide_value(keep) + wide_value(swap(give, "seq", 1)))

    one = chip_sum(one_keep, one_give)
    head_rows, unit_rows = 2 * rank, units // 2
    cut = head_rows + unit_rows
    one_x = swap(one[2 * cut : 2 * cut + head_rows], "mp", 1)
    one_y = swap(one[cut : 2 * cut], "mp", 2)
    one_g = swap(one[2 * cut + head_rows :], "mp", 3)
    grad_blocks, two_keep, two_give = input_back(
        place_ids,
        (grad_filtered, grad_gates, came_edge, taps, prev, grad_hidden, tokens, normed, lows, select[0], gain_one, entry_full, column_full, low_down, grad_down),
        kept,
        in_slabs,
        in_pieces,
    )
    one_x, one_y, one_g, came = after((one_x, one_y, one_g, came), grad_blocks)
    one_own = wide_value(one[:cut]) + wide_value(one_y)
    one_own = one_own.at[:head_rows].add(wide_value(one_x) + wide_value(one_g))
    one_own = low(one_own)
    kept_rows, sent_rows = results_of(place_ids, after(own_parts, one_own), came, low_down, exit_full)
    two_keep, two_give = after((two_keep, two_give), sent_rows)
    two = chip_sum(two_keep, two_give).reshape(4, 5 * rank // 2, share)
    two_own = own_block(two)
    grad_rows = [grad_blocks[0]] + [swap(after(grad_blocks[r], two_own), "mp", r) for r in (1, 2, 3)]
    grad_inputs = wide_value(jnp.stack(place(grad_rows, m)))
    one_own, two_own = seq_total_parts(one_own, two, two_own), seq_total(two_own)
    grads = finish(place_ids, one_own, swap(one_own, "seq", 1), two_own, swap(two_own, "seq", 1), units, rank)

    output = jnp.concatenate(place([kept_rows, swap(sent_rows, "mp", 2)], y), 0)
    in_entry_grad, in_exit_grad, out_entry_grad, out_exit_grad, gate_entry_grad, gate_exit_grad = grads[:6]
    up_entry_grad, up_exit_grad, down_entry_grad, down_exit_grad = grads[6:]
    return (
        output,
        grad_inputs,
        in_entry_grad,
        in_exit_grad.swapaxes(0, 1),
        out_entry_grad,
        out_exit_grad,
        gate_entry_grad,
        gate_exit_grad.T,
        up_entry_grad,
        up_exit_grad.T,
        down_entry_grad,
        down_exit_grad,
    )


def solution(mesh):
    fast = mesh.shape["mp"] == 4 and mesh.shape["seq"] % 4 == 0
    return jax.shard_map(
        fast_local if fast else general_local,
        mesh=mesh,
        in_specs=(
            P(None, "seq", "mp"),
            P(None, "seq", "mp"),
            P(),
            P(None, None, "mp"),
            P("mp", None),
            P(None, None, "mp"),
            P(None, "mp"),
            P("mp", None),
            P("mp", None),
            P(None, "mp"),
            P(),
            P(None, "mp"),
            P("mp", None),
            P(None, "mp"),
            P(None, "mp"),
            P("mp", None),
            P(None, "mp"),
            P("mp", None),
            P("mp", None),
            P(None, "mp"),
            P(),
            P(),
        ),
        out_specs=(
            P(None, "seq", "mp"),
            P(None, "seq", "mp"),
            P("mp", None),
            P(None, None, "mp"),
            P("mp", None),
            P(None, "mp"),
            P("mp", None),
            P(None, "mp"),
            P("mp", None),
            P(None, "mp"),
            P("mp", None),
            P(None, "mp"),
        ),
        check_vma=False,
    )
```
